32 devices in a mesh: gx: 4 (over y, x), gy: 4 (over z), gz: 2 (over core).
Axes of the slice: x: 2, y: 2, z: 4, core: 2. Of those that a mesh axis runs over, the one named last changes fastest.
Arguments:
- displacement: float32 [3, 4096], P(None, ('gx', 'gy', 'gz')), may hold values from -6 to 6
- reference_image: bfloat16 [4096, 512], P(('gx', 'gy', 'gz')), may hold values from -6 to 6
- image_gradient: bfloat16 [3, 4096, 512], P(None, ('gx', 'gy', 'gz')), may hold values from -6 to 6
- deformed_blocks: bfloat16 [4096, 4096], P(('gx', 'gy', 'gz')), may hold values from -6 to 6
- fractions: bfloat16 [24, 4096], P(None, ('gx', 'gy', 'gz')), may hold values from 0 to 1
- offsets: int32 [3, 4096], P(None, ('gx', 'gy', 'gz')), may hold values from 0 to 7
- send_list: int32 [16384], P(('gx', 'gy', 'gz')), may hold values from 0 to 127, as said below
- recv_slot: int32 [4096], P(('gx', 'gy', 'gz')), may hold values from 0 to 511, as said below
Outputs:
- gradient: float32 [3, 4096], P(None, ('gx', 'gy', 'gz'))
The draws below stay inside these ranges and needn't reach their ends.
Inputs may be any that keep to these rules, and one draw needn't show every extreme that they name: `recv_slot`: within one device the 128 entries are distinct slots; slot s is served by the device with the same gx index whose gy+gz index is s // 64. `send_list`: entry p * 64 + k of a device is the block, among that device's 128 rows of deformed_blocks, read by the device of the same gx index with gy+gz index p through its slot (this device's gy+gz index) * 64 + k; entries that no slot reads name arbitrary blocks.
All inputs are finite; a program needn't handle non-finite values.
Results may differ from the reference program's by a relative error of at most 0.00039.
Values may be sent and summed in bfloat16 or wider, within the bound.
No kernel may reach another device: no remote copies, remote signals or barrier semaphores. Data moves between devices by JAX's collectives and lax.ppermute only.
A program may use at most 64 MiB of HBM per device.

```python
import jax
import jax.numpy as jnp
from jax import lax

CX = 2
CY = 8
CZ = 8
CAP = 64
ELEMS = 4096
NX = 8
NY = 32
NZ = 16
N_GX = 4
N_GY = 4
N_GZ = 2


def reading_plan(key):
    peer_count = N_GY * N_GZ
    slot_count = peer_count * CAP
    device_count = N_GX * peer_count
    per_device = CX * CY * CZ
    popular_count = max(1, peer_count // 16)
    key_popular, key_score, key_order, key_block, key_spare = jax.random.split(key, 5)
    favoured = jax.random.permutation(key_popular, peer_count)[:popular_count]
    popular = jnp.zeros((peer_count,), jnp.int32).at[favoured].set(1)
    slot_peer = jnp.arange(slot_count, dtype=jnp.int32) // CAP
    scores = jax.random.randint(key_score, (device_count, slot_count), 0, 1024)
    scores = (scores + 2048 * popular[slot_peer][None, :]) * slot_count + jnp.arange(slot_count, dtype=jnp.int32)[None, :]
    best = lax.top_k(scores, per_device)[1].astype(jnp.int32)
    mixing = jax.random.randint(key_order, (device_count, per_device), 0, 1024) * per_device + jnp.arange(per_device, dtype=jnp.int32)[None, :]
    ordering = jnp.argsort(mixing, axis=1)
    chosen = jnp.take_along_axis(best, ordering, axis=1)
    wanted = jax.random.randint(key_block, (device_count, per_device), 0, per_device)
    devices = jnp.arange(device_count, dtype=jnp.int32)[:, None]
    sources = devices // peer_count * peer_count + chosen // CAP
    entries = devices % peer_count * CAP + chosen % CAP
    listing = jax.random.randint(key_spare, (device_count, slot_count), 0, per_device)
    listing = listing.at[sources, entries].set(wanted)
    return (chosen.reshape(-1).astype(jnp.int32), listing.reshape(-1).astype(jnp.int32))


def draw_send_list(key, part):
    return reading_plan(key)[1]


def draw_recv_slot(key, part):
    return reading_plan(key)[0]


def set_ends(drawn, own_key, least, top_value):
    longest = drawn.shape.index(max(drawn.shape))
    spots = []
    for shift in (0, 1):
        where = [jax.random.randint(jax.random.fold_in(own_key, axis), (), 0, length) for axis, length in enumerate(drawn.shape)]
        where[longest] = (where[longest] + shift) % drawn.shape[longest]
        spots.append(tuple(where))
    return drawn.at[spots[0]].set(least).at[spots[1]].set(top_value)


def steps_of(stream_key, shape, cuts, smallest, largest):
    level = 1.0
    for dim, blocks in cuts:
        steps = jax.random.uniform(jax.random.fold_in(jax.random.fold_in(stream_key, 6), dim), (blocks,), jnp.float32, smallest / len(cuts), largest / len(cuts))
        level = level * jnp.repeat(jnp.exp(steps), shape[dim] // blocks).reshape((-1,) + (1,) * (len(shape) - 1 - dim))
    return level


def bell_draw(key, extent, scale, limit, pieces=(), kind=jnp.bfloat16):
    array = scale * jax.random.normal(key, extent, jnp.float32)
    if pieces:
        array = array * steps_of(key, extent, pieces, -0.22, 0.18)
    return jnp.clip(array, -limit, limit).astype(kind)


def setup_inputs(seed: int = 0) -> dict:
    key_of = jax.random.split(jax.random.key(seed), 9)
    return {
        "displacement": bell_draw(key_of[0], (3, ELEMS), 1.0, 6.0, ((1, 32),), jnp.float32),
        "reference_image": bell_draw(key_of[1], (ELEMS, 512), 1.0, 6.0, ((0, 32),)),
        "image_gradient": bell_draw(key_of[2], (3, ELEMS, 512), 1.0, 6.0, ((1, 32),)),
        "deformed_blocks": bell_draw(key_of[3], (ELEMS, 4096), 1.0, 6.0, ((0, 32),)),
        "fractions": jnp.clip(1.0 * jax.random.uniform(key_of[4], (24, ELEMS), jnp.float32) ** steps_of(key_of[4], (24, ELEMS), ((1, 32),), -0.2, 0.2), 0.0, 1.0).astype(jnp.bfloat16),
        "offsets": set_ends(jax.random.randint(key_of[5], (3, ELEMS), 0, 8), jax.random.fold_in(key_of[5], 1), 0, 7).astype(jnp.int32),
        "send_list": draw_send_list(jax.random.fold_in(key_of[8], 71), 0),
        "recv_slot": draw_recv_slot(jax.random.fold_in(key_of[8], 71), 0),
    }


shear_modulus = 0.05
lame_first = 1.0
data_weight = 0.0625
highest = lax.Precision.HIGHEST


def shape_table():
    centres = (jnp.arange(8, dtype=jnp.float32) + 0.5) / 8.0
    weights = jnp.stack([1.0 - centres, centres], axis=1)
    values = (weights[:, None, None, :, None, None] * weights[None, :, None, None, :, None]
              * weights[None, None, :, None, None, :])
    return values.reshape(512, 8)


def interpolate(voxels, fraction, offset):
    number = voxels.shape[0]
    volume = voxels.astype(jnp.float32).reshape(number, 16, 16, 16)
    starts = offset.astype(jnp.int32)[:, :, None] + jnp.arange(8, dtype=jnp.int32)[None, None, :]
    columns = jnp.arange(16, dtype=jnp.int32)
    upper_weight = jnp.swapaxes(fraction.astype(jnp.float32), 1, 2)[..., None]
    lower_hit = (columns == starts[..., None]).astype(jnp.float32)
    upper_hit = (columns == starts[..., None] + 1).astype(jnp.float32)
    matrices = (1.0 - upper_weight) * lower_hit + upper_weight * upper_hit
    partial_z = jnp.einsum("nkc,nabc->nabk", matrices[2], volume, precision=highest)
    partial_y = jnp.einsum("njb,nabk->najk", matrices[1], partial_z, precision=highest)
    result = jnp.einsum("nia,najk->nijk", matrices[0], partial_y, precision=highest)
    return result.reshape(number, 512).astype(jnp.bfloat16)


def element_forces(samples, image, slopes, shape_values):
    difference = image.astype(jnp.float32) - samples.astype(jnp.float32)
    weighted = slopes.astype(jnp.float32) * difference[None]
    number = image.shape[0]
    return jnp.dot(weighted.reshape(3 * number, 512), shape_values, precision=highest).reshape(3, number, 8)


def displaced(padded, vector):
    return padded[:, 1 + vector[0]:padded.shape[1] - 1 + vector[0],
                  1 + vector[1]:padded.shape[2] - 1 + vector[1],
                  1 + vector[2]:padded.shape[3] - 1 + vector[2]]


def combined(outer_step, inner_step, sign_outer, sign_inner):
    return tuple(sign_outer * outer_step[position] + sign_inner * inner_step[position] for position in range(3))


def navier(padded):
    unit_steps = ((1, 0, 0), (0, 1, 0), (0, 0, 1))
    centre = displaced(padded, (0, 0, 0))
    laplace = -6.0 * centre
    for unit_step in unit_steps:
        laplace = laplace + displaced(padded, unit_step) + displaced(padded, combined(unit_step, unit_step, -1, 0))
    gathered_rows = []
    for outer_axis in range(3):
        accumulated = jnp.zeros_like(centre[0])
        for inner_axis in range(3):
            outer_step = unit_steps[outer_axis]
            inner_step = unit_steps[inner_axis]
            if outer_axis == inner_axis:
                element_term = (displaced(padded, outer_step)[inner_axis]
                                + displaced(padded, combined(outer_step, outer_step, -1, 0))[inner_axis]
                                - 2.0 * centre[inner_axis])
            else:
                element_term = 0.25 * (displaced(padded, combined(outer_step, inner_step, 1, 1))[inner_axis]
                                       - displaced(padded, combined(outer_step, inner_step, 1, -1))[inner_axis]
                                       - displaced(padded, combined(outer_step, inner_step, -1, 1))[inner_axis]
                                       + displaced(padded, combined(outer_step, inner_step, -1, -1))[inner_axis])
            accumulated = accumulated + element_term
        gathered_rows.append(accumulated)
    divergence_grad = jnp.stack(gathered_rows)
    return -(shear_modulus * laplace + (lame_first + shear_modulus) * divergence_grad)


def to_grid(flat):
    leading = flat.shape[0]
    shaped = flat.reshape(leading, N_GX, N_GY, N_GZ, CX, CY, CZ)
    return shaped.transpose(0, 1, 4, 2, 5, 3, 6).reshape(leading, NX, NY, NZ)


def from_grid(grid):
    leading = grid.shape[0]
    shaped = grid.reshape(leading, N_GX, CX, N_GY, CY, N_GZ, CZ)
    return shaped.transpose(0, 1, 3, 5, 2, 4, 6).reshape(leading, NX * NY * NZ)


def push_up(carried, axis):
    length = carried.shape[axis]
    head = jnp.zeros_like(lax.slice_in_dim(carried, 0, 1, axis=axis))
    return jnp.concatenate([head, lax.slice_in_dim(carried, 0, length - 1, axis=axis)], axis=axis)


def reference(displacement, reference_image, image_gradient, deformed_blocks, fractions, offsets, send_list, recv_slot):
    peer_count = N_GY * N_GZ
    slot_count = peer_count * CAP
    device_count = N_GX * peer_count
    per_device = CX * CY * CZ
    devices = jnp.arange(device_count, dtype=jnp.int32)
    slot_grid = recv_slot.reshape(device_count, per_device)
    sources = (devices[:, None] // peer_count) * peer_count + slot_grid // CAP
    entries = (devices[:, None] % peer_count) * CAP + slot_grid % CAP
    chosen = send_list.reshape(device_count, slot_count)[sources, entries]
    source_rows = (sources * per_device + chosen).astype(jnp.int32)
    shape_values = shape_table()

    def per_brick(device):
        start = (device * per_device).astype(jnp.int32)
        rows_here = lax.dynamic_index_in_dim(source_rows, device, 0, keepdims=False)
        voxels = jnp.take(deformed_blocks, rows_here, axis=0)
        fraction = lax.dynamic_slice_in_dim(fractions, start, per_device, 1).reshape(3, 8, per_device)
        offset = lax.dynamic_slice_in_dim(offsets, start, per_device, 1)
        samples = interpolate(voxels, fraction, offset)
        image = lax.dynamic_slice_in_dim(reference_image, start, per_device, 0)
        slopes = lax.dynamic_slice_in_dim(image_gradient, start, per_device, 1)
        return element_forces(samples, image, slopes, shape_values)

    forces = lax.map(per_brick, devices)
    flat_forces = forces.transpose(1, 3, 0, 2).reshape(24, device_count * per_device)
    corners = to_grid(flat_forces).reshape(3, 2, 2, 2, NX, NY, NZ)
    after_x = corners[:, 0] + push_up(corners[:, 1], 3)
    after_y = after_x[:, 0] + push_up(after_x[:, 1], 3)
    data_force = after_y[:, 0] + push_up(after_y[:, 1], 3)
    padded = jnp.pad(to_grid(displacement), ((0, 0), (1, 1), (1, 1), (1, 1)))
    stiffness = navier(padded)
    return from_grid(data_force * data_weight + stiffness)
```

```python
import functools

import jax
import jax.numpy as jnp
from jax import lax
from jax.experimental import pallas as pl
from jax.experimental.pallas import tpu as pltpu
from jax.sharding import PartitionSpec as P

CX = 2
CY = 8
CZ = 8
LANES = CX * CY * CZ
SLAB = ("gy", "gz")

shear_modulus = 0.05
lame_first = 1.0
data_weight = 0.0625

DISP = 24
OFFS = 27
SLOT = 30
META = 32


def iota(shape, dim):
    return lax.broadcasted_iota(jnp.int32, shape, dim)


def shifted(planes, bits):
    for bit, count in ((2, 12), (1, 10), (0, 9)):
        step = 1 << bit
        planes = [jnp.where(bits[bit], planes[p + step], planes[p]) for p in range(count)]
    return planes


def offset_bits(offset, rows):
    wide = jnp.broadcast_to(offset, (rows, LANES))
    return [(wide & (1 << bit)) != 0 for bit in range(3)]


def sample_kernel(cap, readers, swap, block_row, send_ref, meta_ref, table_ref, *rest):
    outs, (along_a, along_b, along_c) = rest[:-3], rest[-3:]
    holder = lax.axis_index("gy") * lax.axis_size("gz") + lax.axis_index("gz")
    row = send_ref[pl.ds(block_row(), 1), :]
    if swap:
        row = jnp.where(lax.axis_index("gz") == 1, pltpu.roll(row, LANES // 2, 1), row)
    pick = (iota((LANES, LANES), 0) == row).astype(jnp.bfloat16)
    slot = iota((LANES, LANES), 0)
    meta = jnp.zeros((META, LANES), jnp.float32)
    for r in range(readers):
        wanted = meta_ref[r, SLOT : SLOT + 1, :].astype(jnp.int32)
        hit = (wanted == holder * cap + slot - r * cap) & (slot // cap == r)
        meta = meta + lax.dot_general(
            meta_ref[r].astype(jnp.bfloat16),
            hit.astype(jnp.bfloat16),
            (((1,), (1,)), ((), ())),
            preferred_element_type=jnp.float32,
        )
    upper = meta[:24]
    lower = 1.0 - upper
    offsets = meta[OFFS : OFFS + 3].astype(jnp.int32)
    bits = offset_bits(offsets[0:1], 16)
    for b in range(16):
        rows = jnp.concatenate(
            [table_ref[256 * a + 16 * b : 256 * a + 16 * b + 16, :] for a in range(16)], axis=0
        )
        voxels = jnp.dot(rows, pick, preferred_element_type=jnp.float32)
        window = shifted([voxels[16 * a : 16 * a + 16] for a in range(16)], bits)
        for i in range(8):
            along_a[256 * i + 16 * b : 256 * i + 16 * b + 16, :] = (
                lower[i : i + 1] * window[i] + upper[i : i + 1] * window[i + 1]
            )
    bits = offset_bits(offsets[1:2], 16)
    for i in range(8):
        window = shifted(
            [along_a[256 * i + 16 * b : 256 * i + 16 * b + 16, :] for b in range(16)], bits
        )
        for j in range(8):
            along_b[128 * i + 16 * j : 128 * i + 16 * j + 16, :] = (
                lower[8 + j : 9 + j] * window[j] + upper[8 + j : 9 + j] * window[j + 1]
            )
    bits = offset_bits(offsets[2:3], 8)
    for i in range(8):
        window = shifted(
            [along_b[pl.ds(128 * i + c, 8, stride=16), :] for c in range(16)], bits
        )
        for k in range(8):
            along_c[pl.ds(64 * i + k, 8, stride=8), :] = (
                lower[16 + k : 17 + k] * window[k] + upper[16 + k : 17 + k] * window[k + 1]
            )
    samples = along_c[...].T.astype(jnp.bfloat16)
    height = LANES // len(outs)
    for n, out in enumerate(outs):
        out[...] = samples[height * n : height * n + height]


def sample_call(cap, readers, swap, block_row, pieces, send_rows, meta, table):
    vmem = pl.BlockSpec(memory_space=pltpu.VMEM)
    return pl.pallas_call(
        functools.partial(sample_kernel, cap, readers, swap, block_row),
        out_shape=[jax.ShapeDtypeStruct((LANES // pieces, 512), jnp.bfloat16)] * pieces,
        in_specs=[vmem] * 3,
        out_specs=[vmem] * pieces,
        scratch_shapes=[
            pltpu.VMEM((2048, LANES), jnp.float32),
            pltpu.VMEM((1024, LANES), jnp.float32),
            pltpu.VMEM((512, LANES), jnp.float32),
        ],
        compiler_params=pltpu.CompilerParams(vmem_limit_bytes=24 << 20),
        cost_estimate=pl.CostEstimate(
            flops=2 * 4096 * 128 * 128, bytes_accessed=2 << 20, transcendentals=0
        ),
        name="interpolate",
    )(send_rows, meta, table)


def shape_table():
    centres = (jnp.arange(8, dtype=jnp.float32) + 0.5) / 8.0
    weights = jnp.stack([1.0 - centres, centres], axis=1)
    values = (
        weights[:, None, None, None, :, None]
        * weights[None, :, None, None, None, :]
        * weights[None, None, :, :, None, None]
    ).reshape(512, 8)
    return jnp.pad(values, ((0, 0), (0, LANES - 8)))


def axis_of_lane(rows):
    lane = iota((rows, LANES), 1)
    return lane // (CY * CZ), lane // CZ % CY, lane % CZ


def force_kernel(cap, relative, slot_ref, image_ref, slope_ref, shape_ref, *rest):
    arrived, (kept_ref, sent_ref) = rest[:-2], rest[-2:]
    total = sum(piece.shape[0] for piece in arrived)
    number = iota((LANES, total), 1)
    if relative:
        own = lax.axis_index("gy") * lax.axis_size("gz") + lax.axis_index("gz")
        number = ((number // cap) ^ own) * cap + number % cap
    hit = (slot_ref[...] == number).astype(jnp.bfloat16)
    rows = jnp.concatenate([piece[...] for piece in arrived], axis=0)
    samples = jnp.dot(hit, rows, preferred_element_type=jnp.float32)
    difference = image_ref[...].astype(jnp.float32) - samples
    _, _, at_k = axis_of_lane(8)
    for d in range(3):
        weighted = slope_ref[d].astype(jnp.float32) * difference
        corners = jnp.dot(
            weighted,
            shape_ref[...],
            preferred_element_type=jnp.float32,
            precision=lax.Precision.HIGHEST,
        ).T[:8]
        carried = pltpu.roll(corners, 4, 0)
        kept_ref[8 * d : 8 * d + 8, :] = corners + jnp.where(at_k > 0, pltpu.roll(carried, 1, 1), 0.0)
        sent_ref[8 * d : 8 * d + 8, :] = jnp.where(at_k == 0, pltpu.roll(carried, LANES - 7, 1), 0.0)


def layer_kernel(kept_ref, arrived_ref, own_ref, x_ref, y_ref, xy_ref):
    at_i, at_j, _ = axis_of_lane(8)
    behind = lax.axis_index("gz") > 0

    def along_x(lower_half, upper_half):
        moved = pltpu.roll(upper_half, CY * CZ, 1)
        return lower_half + jnp.where(at_i > 0, moved, 0.0), jnp.where(at_i == 0, moved, 0.0)

    for d in range(3):
        part = slice(8 * d, 8 * d + 8)
        z = kept_ref[part, :] + jnp.where(behind, arrived_ref[part, :], 0.0)
        carried = pltpu.roll(z, 7, 0)
        stay = z + jnp.where(at_j > 0, pltpu.roll(carried, CZ, 1), 0.0)
        leave = jnp.where(at_j == 0, pltpu.roll(carried, LANES - CZ * (CY - 1), 1), 0.0)
        own, x = along_x(stay, pltpu.roll(stay, 6, 0))
        y, xy = along_x(leave, pltpu.roll(leave, 6, 0))
        for ref, value in ((own_ref, own), (x_ref, x), (y_ref, y), (xy_ref, xy)):
            ref[d : d + 1, :] = value[0:1]


def final_kernel(own_ref, x_ref, y_ref, xy_ref, stiff_ref, out_ref):
    has_x = lax.axis_index("gx") > 0
    has_y = lax.axis_index("gy") > 0
    force = own_ref[0:3, :]
    force = force + jnp.where(has_x, x_ref[0:3, :], 0.0)
    force = force + jnp.where(has_y, y_ref[0:3, :], 0.0)
    force = force + jnp.where(has_x & has_y, xy_ref[0:3, :], 0.0)
    out_ref[...] = force * data_weight + stiff_ref[0:3, :]


def stiffness_kernel(relative, below_ref, own_ref, above_ref, out_ref):
    here = [lax.axis_index(name) for name in ("gx", "gy", "gz")]
    sizes = [lax.axis_size(name) for name in ("gx", "gy", "gz")]
    own = here[1] * sizes[2] + here[2]
    slabs = {-1: below_ref, 0: own_ref, 1: above_ref}
    at = axis_of_lane(8)
    steps = (CY * CZ, CZ, 1)
    extents = (CX, CY, CZ)
    fields = {}
    for ox in (-1, 0, 1):
        for oy in (-1, 0, 1):
            for oz in (-1, 0, 1):
                if ox and oy and oz:
                    continue
                place = (here[0] + ox, here[1] + oy, here[2] + oz)
                inside = True
                for where, size in zip(place, sizes):
                    inside = inside & (where >= 0) & (where < size)
                peer = jnp.clip(place[1], 0, sizes[1] - 1) * sizes[2] + jnp.clip(
                    place[2], 0, sizes[2] - 1
                )
                if relative:
                    peer = peer ^ own
                fields[ox, oy, oz] = jnp.where(inside, slabs[ox][peer], 0.0)

    def along(axis, sign, centre, beyond):
        step, extent = steps[axis], extents[axis]
        back = step * (extent - 1)
        if sign > 0:
            return jnp.where(
                at[axis] < extent - 1,
                pltpu.roll(centre, LANES - step, 1),
                pltpu.roll(beyond, back, 1),
            )
        return jnp.where(
            at[axis] > 0, pltpu.roll(centre, step, 1), pltpu.roll(beyond, LANES - back, 1)
        )

    def moved(vector, frame=(0, 0, 0), axis=2):
        if axis < 0:
            return fields[frame]
        sign = vector[axis]
        centre = moved(vector, frame, axis - 1)
        if sign == 0:
            return centre
        other = tuple(sign if n == axis else frame[n] for n in range(3))
        return along(axis, sign, centre, moved(vector, other, axis - 1))

    units = ((1, 0, 0), (0, 1, 0), (0, 0, 1))
    centre = fields[0, 0, 0]
    laplace = -6.0 * centre
    second = []
    for unit in units:
        both = moved(unit) + moved(tuple(-n for n in unit))
        laplace = laplace + both
        second.append(both - 2.0 * centre)
    mixed = {}
    for outer in range(3):
        for inner in range(outer + 1, 3):
            plus = tuple(p + q for p, q in zip(units[outer], units[inner]))
            cross = tuple(p - q for p, q in zip(units[outer], units[inner]))
            mixed[outer, inner] = 0.25 * (
                moved(plus)
                - moved(cross)
                - moved(tuple(-n for n in cross))
                + moved(tuple(-n for n in plus))
            )
    for d in range(3):
        total = second[d][d : d + 1]
        for b in range(3):
            if b != d:
                total = total + mixed[min(b, d), max(b, d)][b : b + 1]
        out_ref[d : d + 1, :] = -(
            shear_modulus * laplace[d : d + 1] + (lame_first + shear_modulus) * total
        )


def small_call(kernel, shapes, name, *operands):
    vmem = pl.BlockSpec(memory_space=pltpu.VMEM)
    return pl.pallas_call(
        kernel,
        out_shape=[jax.ShapeDtypeStruct(shape, jnp.float32) for shape in shapes],
        in_specs=[vmem] * len(operands),
        out_specs=[vmem] * len(shapes),
        compiler_params=pltpu.CompilerParams(vmem_limit_bytes=24 << 20),
        cost_estimate=pl.CostEstimate(flops=1 << 20, bytes_accessed=1 << 20, transcendentals=0),
        name=name,
    )(*operands)


def ring(value, axes, distance=1):
    count = lax.axis_size(axes)
    return lax.ppermute(value, axes, [(i, (i + distance) % count) for i in range(count)])


def ring_2(value):
    nx, ny = lax.axis_size("gx"), lax.axis_size("gy")
    route = [
        (x * ny + y, (x + 1) % nx * ny + (y + 1) % ny) for x in range(nx) for y in range(ny)
    ]
    return lax.ppermute(value, ("gx", "gy"), route)


def swapped(value, axes, mask):
    return lax.ppermute(value, axes, [(i, i ^ mask) for i in range(lax.axis_size(axes))])


def local(
    displacement,
    reference_image,
    image_gradient,
    deformed_blocks,
    fractions,
    offsets,
    send_list,
    recv_slot,
):
    n_y, n_z = lax.axis_size("gy"), lax.axis_size("gz")
    peers = n_y * n_z
    cap = send_list.shape[0] // peers
    f32 = jnp.float32
    packed = jnp.concatenate(
        [
            fractions.astype(f32),
            displacement,
            offsets.astype(f32),
            recv_slot.astype(f32)[None],
            jnp.zeros((1, LANES), f32),
        ],
        axis=0,
    )
    table = deformed_blocks.T
    send_rows = send_list.reshape(-1, LANES)
    relative = n_z == 2 and n_y in (2, 4) and 2 * cap == LANES
    if relative:
        chip = jnp.stack([packed, swapped(packed, "gz", 1)])
        metas = [chip] + [swapped(chip, "gy", d) for d in range(1, n_y)]
        arrived = [None] * peers
        order = list(range(n_y - 1, 0, -1)) + [0]
        for d in order:
            pair = sample_call(
                cap, 2, True, lambda d=d: lax.axis_index("gy") ^ d, 2, send_rows, metas[d], table
            )
            for other in range(2):
                mask = 2 * d + other
                arrived[mask] = swapped(pair[other], SLAB, mask) if mask else pair[other]
        slab = jnp.concatenate([meta[:, DISP:META] for meta in metas], axis=0)
    else:
        gathered = lax.all_gather(packed, SLAB, axis=0)
        readers = LANES // cap
        groups = peers // readers
        samples = [
            sample_call(
                cap,
                readers,
                False,
                lambda g=g: g,
                1,
                send_rows,
                gathered[g * readers : (g + 1) * readers],
                table,
            )[0]
            for g in range(groups)
        ]
        outgoing = jnp.concatenate(samples, axis=0)
        arrived = [lax.all_to_all(outgoing, SLAB, split_axis=0, concat_axis=0, tiled=True)]
        slab = gathered[:, DISP:META]
    below, above = ring(slab, "gx", 1), ring(slab, "gx", -1)
    (stiff,) = small_call(
        functools.partial(stiffness_kernel, relative), [(8, LANES)], "stiffness", below, slab, above
    )
    kept, sent = small_call(
        functools.partial(force_kernel, cap, relative),
        [(24, LANES)] * 2,
        "forces",
        recv_slot[:, None],
        reference_image,
        image_gradient,
        shape_table(),
        *arrived,
    )
    own, x, y, xy = small_call(
        layer_kernel, [(8, LANES)] * 4, "layers", kept, ring(sent, "gz")
    )
    return small_call(
        final_kernel,
        [(3, LANES)],
        "total",
        own,
        ring(x, "gx"),
        ring(y, "gy"),
        ring_2(xy),
        stiff,
    )[0]


def solution(mesh):
    in_specs = (
        P(None, ("gx", "gy", "gz")),
        P(("gx", "gy", "gz"), None),
        P(None, ("gx", "gy", "gz"), None),
        P(("gx", "gy", "gz"), None),
        P(None, ("gx", "gy", "gz")),
        P(None, ("gx", "gy", "gz")),
        P(("gx", "gy", "gz")),
        P(("gx", "gy", "gz")),
    )
    out_specs = P(None, ("gx", "gy", "gz"))
    return jax.shard_map(local, mesh=mesh, in_specs=in_specs, out_specs=out_specs, check_vma=False)
```

```python
import functools

import jax
import jax.numpy as jnp
from jax import lax
from jax.experimental import pallas as pl
from jax.experimental.pallas import tpu as pltpu
from jax.sharding import PartitionSpec as P

CX = 2
CY = 8
CZ = 8
LANES = CX * CY * CZ
SLAB = ("gy", "gz")

shear_modulus = 0.05
lame_first = 1.0
data_weight = 0.0625

DISP = 24
OFFS = 27
SLOT = 30
META = 32

VOXELS = 4096
TABLE = VOXELS + 16


def iota(shape, dim):
    return lax.broadcasted_iota(jnp.int32, shape, dim)


def shifted(planes, bits):
    for bit, count in ((2, 12), (1, 10), (0, 9)):
        step = 1 << bit
        planes = [jnp.where(bits[bit], planes[p + step], planes[p]) for p in range(count)]
    return planes


def offset_bits(offset, rows):
    wide = jnp.broadcast_to(offset, (rows, LANES))
    return [(wide & (1 << bit)) != 0 for bit in range(3)]


def pack_kernel(fraction_ref, displacement_ref, offset_ref, slot_ref, out_ref):
    out_ref[:DISP, :] = fraction_ref[...].astype(jnp.float32)
    out_ref[DISP:OFFS, :] = displacement_ref[...]
    out_ref[OFFS:SLOT, :] = offset_ref[...].astype(jnp.float32)
    out_ref[SLOT : SLOT + 1, :] = slot_ref[...].astype(jnp.float32)
    out_ref[SLOT + 1 :, :] = jnp.zeros((META - SLOT - 1, LANES), jnp.float32)


def table_kernel(block_ref, send_ref, out_ref):
    for start in range(0, VOXELS, 512):
        out_ref[start : start + 512, :] = block_ref[:, start : start + 512].T
    rows = send_ref.shape[0]
    listed = jnp.concatenate(
        [send_ref[...].astype(jnp.float32), jnp.zeros((TABLE - VOXELS - rows, LANES), jnp.float32)],
        axis=0,
    )
    out_ref[VOXELS:, :] = listed.astype(jnp.bfloat16)


def interpolated(table_refs, pick, meta, along_a, along_b, along_c):
    upper = meta[:24]
    lower = 1.0 - upper
    offsets = meta[OFFS : OFFS + 3].astype(jnp.int32)
    bits = offset_bits(offsets[0:1], 16)
    for b in range(16):
        starts = [256 * a + 16 * b for a in range(16)]
        rows = jnp.concatenate(
            [
                jnp.concatenate([ref[start : start + 16, :] for start in starts], axis=0)
                for ref in table_refs
            ],
            axis=1,
        )
        voxels = jnp.dot(rows, pick, preferred_element_type=jnp.float32)
        window = shifted([voxels[16 * a : 16 * a + 16] for a in range(16)], bits)
        for i in range(8):
            along_a[256 * i + 16 * b : 256 * i + 16 * b + 16, :] = (
                lower[i : i + 1] * window[i] + upper[i : i + 1] * window[i + 1]
            )
    bits = offset_bits(offsets[1:2], 16)
    for i in range(8):
        window = shifted(
            [along_a[256 * i + 16 * b : 256 * i + 16 * b + 16, :] for b in range(16)], bits
        )
        for j in range(8):
            along_b[128 * i + 16 * j : 128 * i + 16 * j + 16, :] = (
                lower[8 + j : 9 + j] * window[j] + upper[8 + j : 9 + j] * window[j + 1]
            )
    bits = offset_bits(offsets[2:3], 8)
    for i in range(8):
        window = shifted(
            [along_b[pl.ds(128 * i + c, 8, stride=16), :] for c in range(16)], bits
        )
        for k in range(8):
            along_c[pl.ds(64 * i + k, 8, stride=8), :] = (
                lower[16 + k : 17 + k] * window[k] + upper[16 + k : 17 + k] * window[k + 1]
            )
    return along_c[...].T.astype(jnp.bfloat16)


def slot_meta(meta, slots):
    wanted = meta[SLOT : SLOT + 1].astype(jnp.int32)
    return lax.dot_general(
        meta.astype(jnp.bfloat16),
        (wanted == slots).astype(jnp.bfloat16),
        (((1,), (1,)), ((), ())),
        preferred_element_type=jnp.float32,
    )


def pair_kernel(distance, meta_ref, own_ref, mate_ref, *rest):
    out_ref, scratch = rest[-4], rest[-3:]
    gy, gz = lax.axis_index("gy"), lax.axis_index("gz")
    half = LANES // 2
    slot = iota((LANES, LANES), 0)
    slots = (((2 * gy + gz) ^ (slot // half)) * half) + slot % half
    meta = slot_meta(meta_ref[...], slots)
    chip = gy ^ distance
    lists = [ref[VOXELS:, :].astype(jnp.float32) for ref in (own_ref, mate_ref)]
    here = iota(lists[0].shape, 0) == chip
    own, mate = [
        jnp.sum(jnp.where(here, listed, 0.0), axis=0, keepdims=True).astype(jnp.int32)
        for listed in lists
    ]
    first = gz == 0
    own = jnp.where(first, own, pltpu.roll(own, half, 1))
    mate = jnp.where(first, pltpu.roll(mate, half, 1), mate)
    row = jnp.where(iota((1, LANES), 1) < half, own, mate + LANES)
    pick = (iota((2 * LANES, LANES), 0) == row).astype(jnp.bfloat16)
    out_ref[...] = interpolated((own_ref, mate_ref), pick, meta, *scratch)


def group_kernel(group, cap, meta_ref, table_ref, out_ref, *scratch):
    holder = lax.axis_index("gy") * lax.axis_size("gz") + lax.axis_index("gz")
    slot = iota((LANES, LANES), 0)
    meta = jnp.zeros((META, LANES), jnp.float32)
    for r in range(LANES // cap):
        slots = jnp.where(slot // cap == r, holder * cap + slot - r * cap, -1)
        meta = meta + slot_meta(meta_ref[r], slots)
    row = table_ref[VOXELS:, :].astype(jnp.float32)[group : group + 1].astype(jnp.int32)
    pick = (iota((LANES, LANES), 0) == row).astype(jnp.bfloat16)
    out_ref[...] = interpolated((table_ref,), pick, meta, *scratch)


def sample_call(kernel, *operands):
    vmem = pl.BlockSpec(memory_space=pltpu.VMEM)
    return pl.pallas_call(
        kernel,
        out_shape=jax.ShapeDtypeStruct((LANES, 512), jnp.bfloat16),
        in_specs=[vmem] * len(operands),
        out_specs=vmem,
        scratch_shapes=[
            pltpu.VMEM((2048, LANES), jnp.float32),
            pltpu.VMEM((1024, LANES), jnp.float32),
            pltpu.VMEM((512, LANES), jnp.float32),
        ],
        compiler_params=pltpu.CompilerParams(vmem_limit_bytes=24 << 20),
        cost_estimate=pl.CostEstimate(
            flops=2 * 4096 * 128 * 256, bytes_accessed=2 << 20, transcendentals=0
        ),
        name="interpolate",
    )(*operands)


def shape_table():
    centres = (jnp.arange(8, dtype=jnp.float32) + 0.5) / 8.0
    weights = jnp.stack([1.0 - centres, centres], axis=1)
    values = (
        weights[:, None, None, None, :, None]
        * weights[None, :, None, None, None, :]
        * weights[None, None, :, :, None, None]
    ).reshape(512, 8)
    return jnp.pad(values, ((0, 0), (0, LANES - 8)))


def axis_of_lane(rows):
    lane = iota((rows, LANES), 1)
    return lane // (CY * CZ), lane // CZ % CY, lane % CZ


def force_kernel(cap, relative, slot_ref, image_ref, slope_ref, shape_ref, *rest):
    arrived, (kept_ref, sent_ref) = rest[:-2], rest[-2:]
    total = sum(piece.shape[0] for piece in arrived)
    number = iota((LANES, total), 1)
    if relative:
        own = lax.axis_index("gy") * lax.axis_size("gz") + lax.axis_index("gz")
        number = ((number // cap) ^ own) * cap + number % cap
    hit = (slot_ref[...] == number).astype(jnp.bfloat16)
    rows = jnp.concatenate([piece[...] for piece in arrived], axis=0)
    samples = jnp.dot(hit, rows, preferred_element_type=jnp.float32)
    difference = image_ref[...].astype(jnp.float32) - samples
    _, _, at_k = axis_of_lane(8)
    for d in range(3):
        weighted = slope_ref[d].astype(jnp.float32) * difference
        corners = jnp.dot(
            weighted,
            shape_ref[...],
            preferred_element_type=jnp.float32,
            precision=lax.Precision.HIGHEST,
        ).T[:8]
        carried = pltpu.roll(corners, 4, 0)
        kept_ref[8 * d : 8 * d + 8, :] = corners + jnp.where(at_k > 0, pltpu.roll(carried, 1, 1), 0.0)
        sent_ref[8 * d : 8 * d + 8, :] = jnp.where(at_k == 0, pltpu.roll(carried, LANES - 7, 1), 0.0)


def layer_kernel(kept_ref, arrived_ref, own_ref, x_ref, y_ref, xy_ref):
    at_i, at_j, _ = axis_of_lane(8)
    behind = lax.axis_index("gz") > 0

    def along_x(lower_half, upper_half):
        moved = pltpu.roll(upper_half, CY * CZ, 1)
        return lower_half + jnp.where(at_i > 0, moved, 0.0), jnp.where(at_i == 0, moved, 0.0)

    for d in range(3):
        part = slice(8 * d, 8 * d + 8)
        z = kept_ref[part, :] + jnp.where(behind, arrived_ref[part, :], 0.0)
        carried = pltpu.roll(z, 7, 0)
        stay = z + jnp.where(at_j > 0, pltpu.roll(carried, CZ, 1), 0.0)
        leave = jnp.where(at_j == 0, pltpu.roll(carried, LANES - CZ * (CY - 1), 1), 0.0)
        own, x = along_x(stay, pltpu.roll(stay, 6, 0))
        y, xy = along_x(leave, pltpu.roll(leave, 6, 0))
        for ref, value in ((own_ref, own), (x_ref, x), (y_ref, y), (xy_ref, xy)):
            ref[d : d + 1, :] = value[0:1]


def final_kernel(own_ref, x_ref, y_ref, xy_ref, stiff_ref, out_ref):
    has_x = lax.axis_index("gx") > 0
    has_y = lax.axis_index("gy") > 0
    force = own_ref[0:3, :]
    force = force + jnp.where(has_x, x_ref[0:3, :], 0.0)
    force = force + jnp.where(has_y, y_ref[0:3, :], 0.0)
    force = force + jnp.where(has_x & has_y, xy_ref[0:3, :], 0.0)
    out_ref[...] = force * data_weight + stiff_ref[0:3, :]


def stiffness_kernel(relative, below_ref, own_ref, above_ref, out_ref):
    here = [lax.axis_index(name) for name in ("gx", "gy", "gz")]
    sizes = [lax.axis_size(name) for name in ("gx", "gy", "gz")]
    own = here[1] * sizes[2] + here[2]
    slabs = {-1: below_ref, 0: own_ref, 1: above_ref}
    at = axis_of_lane(8)
    steps = (CY * CZ, CZ, 1)
    extents = (CX, CY, CZ)
    fields = {}
    for ox in (-1, 0, 1):
        for oy in (-1, 0, 1):
            for oz in (-1, 0, 1):
                if ox and oy and oz:
                    continue
                place = (here[0] + ox, here[1] + oy, here[2] + oz)
                inside = True
                for where, size in zip(place, sizes):
                    inside = inside & (where >= 0) & (where < size)
                peer = jnp.clip(place[1], 0, sizes[1] - 1) * sizes[2] + jnp.clip(
                    place[2], 0, sizes[2] - 1
                )
                if relative:
                    peer = peer ^ own
                    peer = peer % 2 * sizes[1] + peer // 2
                fields[ox, oy, oz] = jnp.where(inside, slabs[ox][peer], 0.0)

    def along(axis, sign, centre, beyond):
        step, extent = steps[axis], extents[axis]
        back = step * (extent - 1)
        if sign > 0:
            return jnp.where(
                at[axis] < extent - 1,
                pltpu.roll(centre, LANES - step, 1),
                pltpu.roll(beyond, back, 1),
            )
        return jnp.where(
            at[axis] > 0, pltpu.roll(centre, step, 1), pltpu.roll(beyond, LANES - back, 1)
        )

    def moved(vector, frame=(0, 0, 0), axis=2):
        if axis < 0:
            return fields[frame]
        sign = vector[axis]
        centre = moved(vector, frame, axis - 1)
        if sign == 0:
            return centre
        other = tuple(sign if n == axis else frame[n] for n in range(3))
        return along(axis, sign, centre, moved(vector, other, axis - 1))

    units = ((1, 0, 0), (0, 1, 0), (0, 0, 1))
    centre = fields[0, 0, 0]
    laplace = -6.0 * centre
    second = []
    for unit in units:
        both = moved(unit) + moved(tuple(-n for n in unit))
        laplace = laplace + both
        second.append(both - 2.0 * centre)
    mixed = {}
    for outer in range(3):
        for inner in range(outer + 1, 3):
            plus = tuple(p + q for p, q in zip(units[outer], units[inner]))
            cross = tuple(p - q for p, q in zip(units[outer], units[inner]))
            mixed[outer, inner] = 0.25 * (
                moved(plus)
                - moved(cross)
                - moved(tuple(-n for n in cross))
                + moved(tuple(-n for n in plus))
            )
    for d in range(3):
        total = second[d][d : d + 1]
        for b in range(3):
            if b != d:
                total = total + mixed[min(b, d), max(b, d)][b : b + 1]
        out_ref[d : d + 1, :] = -(
            shear_modulus * laplace[d : d + 1] + (lame_first + shear_modulus) * total
        )


def collect_kernel(*refs):
    for n, ref in enumerate(refs[:-1]):
        refs[-1][n] = ref[DISP:META, :]


def join_kernel(first_ref, second_ref, out_ref):
    count = first_ref.shape[0]
    out_ref[:count] = first_ref[...]
    out_ref[count:] = second_ref[...]


def small_call(kernel, shapes, name, *operands, dtype=jnp.float32):
    vmem = pl.BlockSpec(memory_space=pltpu.VMEM)
    return pl.pallas_call(
        kernel,
        out_shape=[jax.ShapeDtypeStruct(shape, dtype) for shape in shapes],
        in_specs=[vmem] * len(operands),
        out_specs=[vmem] * len(shapes),
        compiler_params=pltpu.CompilerParams(vmem_limit_bytes=24 << 20),
        cost_estimate=pl.CostEstimate(flops=1 << 20, bytes_accessed=1 << 20, transcendentals=0),
        name=name,
    )(*operands)


def ring(value, axes, distance=1):
    count = lax.axis_size(axes)
    return lax.ppermute(value, axes, [(i, (i + distance) % count) for i in range(count)])


def ring_2(value):
    nx, ny = lax.axis_size("gx"), lax.axis_size("gy")
    route = [
        (x * ny + y, (x + 1) % nx * ny + (y + 1) % ny) for x in range(nx) for y in range(ny)
    ]
    return lax.ppermute(value, ("gx", "gy"), route)


def swapped(value, axes, mask):
    return lax.ppermute(value, axes, [(i, i ^ mask) for i in range(lax.axis_size(axes))])


def local(
    displacement,
    reference_image,
    image_gradient,
    deformed_blocks,
    fractions,
    offsets,
    send_list,
    recv_slot,
):
    n_y, n_z = lax.axis_size("gy"), lax.axis_size("gz")
    peers = n_y * n_z
    cap = send_list.shape[0] // peers
    (packed,) = small_call(
        pack_kernel,
        [(META, LANES)],
        "pack",
        fractions,
        displacement,
        offsets,
        recv_slot[None],
    )
    (table,) = small_call(
        table_kernel,
        [(TABLE, LANES)],
        "table",
        deformed_blocks,
        send_list.reshape(-1, LANES),
        dtype=jnp.bfloat16,
    )
    relative = n_z == 2 and n_y in (2, 4) and 2 * cap == LANES
    if relative:
        metas = [packed] + [swapped(packed, "gy", d) for d in range(1, n_y)]
        mate = swapped(table, "gz", 1)
        arrived = [None] * n_y
        previous = []
        for d in range(n_y - 1, -1, -1):
            samples = sample_call(
                functools.partial(pair_kernel, d), metas[d], table, mate, *previous
            )
            previous = [samples]
            arrived[d] = swapped(samples, "gy", d) if d else samples
        (column,) = small_call(collect_kernel, [(n_y, 8, LANES)], "collect", *metas)
        (slab,) = small_call(
            join_kernel, [(peers, 8, LANES)], "join", column, swapped(column, "gz", 1)
        )
    else:
        gathered = lax.all_gather(packed, SLAB, axis=0)
        readers = LANES // cap
        samples = [
            sample_call(
                functools.partial(group_kernel, g, cap),
                gathered[g * readers : (g + 1) * readers],
                table,
            )
            for g in range(peers // readers)
        ]
        outgoing = jnp.concatenate(samples, axis=0)
        arrived = [lax.all_to_all(outgoing, SLAB, split_axis=0, concat_axis=0, tiled=True)]
        slab = gathered[:, DISP:META]
    below, above = ring(slab, "gx", 1), ring(slab, "gx", -1)
    (stiff,) = small_call(
        functools.partial(stiffness_kernel, relative), [(8, LANES)], "stiffness", below, slab, above
    )
    kept, sent = small_call(
        functools.partial(force_kernel, cap, relative),
        [(24, LANES)] * 2,
        "forces",
        recv_slot[:, None],
        reference_image,
        image_gradient,
        shape_table(),
        *arrived,
    )
    own, x, y, xy = small_call(
        layer_kernel, [(8, LANES)] * 4, "layers", kept, ring(sent, "gz")
    )
    return small_call(
        final_kernel,
        [(3, LANES)],
        "total",
        own,
        ring(x, "gx"),
        ring(y, "gy"),
        ring_2(xy),
        stiff,
    )[0]


def solution(mesh):
    in_specs = (
        P(None, ("gx", "gy", "gz")),
        P(("gx", "gy", "gz"), None),
        P(None, ("gx", "gy", "gz"), None),
        P(("gx", "gy", "gz"), None),
        P(None, ("gx", "gy", "gz")),
        P(None, ("gx", "gy", "gz")),
        P(("gx", "gy", "gz")),
        P(("gx", "gy", "gz")),
    )
    out_specs = P(None, ("gx", "gy", "gz"))
    return jax.shard_map(local, mesh=mesh, in_specs=in_specs, out_specs=out_specs, check_vma=False)
```

```python
import functools

import jax
import jax.numpy as jnp
from jax import lax
from jax.experimental import pallas as pl
from jax.experimental.pallas import tpu as pltpu
from jax.sharding import PartitionSpec as P

CX = 2
CY = 8
CZ = 8
LANES = CX * CY * CZ
SLAB = ("gy", "gz")

shear_modulus = 0.05
lame_first = 1.0
data_weight = 0.0625

DISP = 24
OFFS = 27
SLOT = 30
META = 32

VOXELS = 4096
TABLE = VOXELS + 16


def iota(shape, dim):
    return lax.broadcasted_iota(jnp.int32, shape, dim)


def shifted(planes, bits):
    for bit, count in ((2, 12), (1, 10), (0, 9)):
        step = 1 << bit
        planes = [jnp.where(bits[bit], planes[p + step], planes[p]) for p in range(count)]
    return planes


def offset_bits(offset, rows):
    wide = jnp.broadcast_to(offset, (rows, LANES))
    return [(wide & (1 << bit)) != 0 for bit in range(3)]


def shape_kernel(out_ref):
    voxel, column = iota((512, LANES), 0), iota((512, LANES), 1)

    def weight(index, upper):
        centre = (index.astype(jnp.float32) + 0.5) * 0.125
        return jnp.where(upper == 1, centre, 1.0 - centre)

    values = weight(voxel // 64, column // 2 % 2) * weight(voxel // 8 % 8, column % 2)
    values = values * weight(voxel % 8, column // 4)
    out_ref[...] = jnp.where(column < 8, values, 0.0)


def prepare_kernel(
    after_ref, fraction_ref, displacement_ref, offset_ref, slot_ref, send_ref, block_ref, packed_ref, table_ref
):
    packed_ref[:DISP, :] = fraction_ref[...].astype(jnp.float32)
    packed_ref[DISP:OFFS, :] = displacement_ref[...]
    packed_ref[OFFS:SLOT, :] = offset_ref[...].astype(jnp.float32)
    packed_ref[SLOT : SLOT + 1, :] = slot_ref[...].astype(jnp.float32)
    packed_ref[SLOT + 1 :, :] = jnp.zeros((META - SLOT - 1, LANES), jnp.float32)
    for start in range(0, VOXELS, 512):
        table_ref[start : start + 512, :] = block_ref[:, start : start + 512].T
    rows = send_ref.shape[0]
    listed = jnp.concatenate(
        [send_ref[...].astype(jnp.float32), jnp.zeros((TABLE - VOXELS - rows, LANES), jnp.float32)],
        axis=0,
    )
    table_ref[VOXELS:, :] = listed.astype(jnp.bfloat16)


def vmem_call(kernel, shapes, name, *operands, cost=1 << 20, flops=1 << 20):
    vmem = pl.BlockSpec(memory_space=pltpu.VMEM)
    return pl.pallas_call(
        kernel,
        out_shape=[jax.ShapeDtypeStruct(shape, dtype) for shape, dtype in shapes],
        in_specs=[vmem] * len(operands),
        out_specs=[vmem] * len(shapes),
        compiler_params=pltpu.CompilerParams(vmem_limit_bytes=24 << 20),
        cost_estimate=pl.CostEstimate(flops=flops, bytes_accessed=cost, transcendentals=0),
        name=name,
    )(*operands)


def interpolated(table_refs, pick, meta, along_a, along_b, along_c):
    upper = meta[:24]
    lower = 1.0 - upper
    offsets = meta[OFFS : OFFS + 3].astype(jnp.int32)
    bits = offset_bits(offsets[0:1], 16)
    for b in range(16):
        starts = [256 * a + 16 * b for a in range(16)]
        rows = jnp.concatenate(
            [
                jnp.concatenate([ref[start : start + 16, :] for start in starts], axis=0)
                for ref in table_refs
            ],
            axis=1,
        )
        voxels = jnp.dot(rows, pick, preferred_element_type=jnp.float32)
        window = shifted([voxels[16 * a : 16 * a + 16] for a in range(16)], bits)
        for i in range(8):
            along_a[256 * i + 16 * b : 256 * i + 16 * b + 16, :] = (
                lower[i : i + 1] * window[i] + upper[i : i + 1] * window[i + 1]
            )
    bits = offset_bits(offsets[1:2], 16)
    for i in range(8):
        window = shifted(
            [along_a[256 * i + 16 * b : 256 * i + 16 * b + 16, :] for b in range(16)], bits
        )
        for j in range(8):
            along_b[128 * i + 16 * j : 128 * i + 16 * j + 16, :] = (
                lower[8 + j : 9 + j] * window[j] + upper[8 + j : 9 + j] * window[j + 1]
            )
    bits = offset_bits(offsets[2:3], 8)
    for i in range(8):
        window = shifted(
            [along_b[pl.ds(128 * i + c, 8, stride=16), :] for c in range(16)], bits
        )
        for k in range(8):
            along_c[pl.ds(64 * i + k, 8, stride=8), :] = (
                lower[16 + k : 17 + k] * window[k] + upper[16 + k : 17 + k] * window[k + 1]
            )
    return along_c[...].T.astype(jnp.bfloat16)


def slot_meta(meta, slots):
    wanted = meta[SLOT : SLOT + 1].astype(jnp.int32)
    return lax.dot_general(
        meta.astype(jnp.bfloat16),
        (wanted == slots).astype(jnp.bfloat16),
        (((1,), (1,)), ((), ())),
        preferred_element_type=jnp.float32,
    )


def pair_kernel(distance, meta_ref, own_ref, mate_ref, *rest):
    out_ref, scratch = rest[-4], rest[-3:]
    gy, gz = lax.axis_index("gy"), lax.axis_index("gz")
    half = LANES // 2
    slot = iota((LANES, LANES), 0)
    slots = (((2 * gy + gz) ^ (slot // half)) * half) + slot % half
    meta = slot_meta(meta_ref[...], slots)
    chip = lax.rem(gy + distance, lax.axis_size("gy"))
    lists = [ref[VOXELS:, :].astype(jnp.float32) for ref in (own_ref, mate_ref)]
    here = iota(lists[0].shape, 0) == chip
    own, mate = [
        jnp.sum(jnp.where(here, listed, 0.0), axis=0, keepdims=True).astype(jnp.int32)
        for listed in lists
    ]
    first = gz == 0
    own = jnp.where(first, own, pltpu.roll(own, half, 1))
    mate = jnp.where(first, pltpu.roll(mate, half, 1), mate)
    row = jnp.where(iota((1, LANES), 1) < half, own, mate + LANES)
    pick = (iota((2 * LANES, LANES), 0) == row).astype(jnp.bfloat16)
    out_ref[...] = interpolated((own_ref, mate_ref), pick, meta, *scratch)


def group_kernel(group, cap, meta_ref, table_ref, out_ref, *scratch):
    holder = lax.axis_index("gy") * lax.axis_size("gz") + lax.axis_index("gz")
    slot = iota((LANES, LANES), 0)
    meta = jnp.zeros((META, LANES), jnp.float32)
    for r in range(LANES // cap):
        slots = jnp.where(slot // cap == r, holder * cap + slot - r * cap, -1)
        meta = meta + slot_meta(meta_ref[r], slots)
    row = table_ref[VOXELS:, :].astype(jnp.float32)[group : group + 1].astype(jnp.int32)
    pick = (iota((LANES, LANES), 0) == row).astype(jnp.bfloat16)
    out_ref[...] = interpolated((table_ref,), pick, meta, *scratch)


def sample_call(kernel, *operands):
    vmem = pl.BlockSpec(memory_space=pltpu.VMEM)
    return pl.pallas_call(
        kernel,
        out_shape=jax.ShapeDtypeStruct((LANES, 512), jnp.bfloat16),
        in_specs=[vmem] * len(operands),
        out_specs=vmem,
        scratch_shapes=[
            pltpu.VMEM((2048, LANES), jnp.float32),
            pltpu.VMEM((1024, LANES), jnp.float32),
            pltpu.VMEM((512, LANES), jnp.float32),
        ],
        compiler_params=pltpu.CompilerParams(vmem_limit_bytes=24 << 20),
        cost_estimate=pl.CostEstimate(
            flops=1, bytes_accessed=1, transcendentals=0
        ),
        name="interpolate",
    )(*operands)


def axis_of_lane(rows):
    lane = iota((rows, LANES), 1)
    return lane // (CY * CZ), lane // CZ % CY, lane % CZ


def force_kernel(cap, relative, across_ref, slot_ref, image_ref, slope_ref, shape_ref, *rest):
    arrived, (kept_ref, sent_ref) = rest[:-2], rest[-2:]
    total = sum(piece.shape[0] for piece in arrived)
    number = iota((LANES, total), 1)
    if relative:
        n_y = lax.axis_size("gy")
        chip = lax.rem(lax.axis_index("gy") + n_y - number // (2 * cap), n_y)
        core = (number // cap % 2) ^ lax.axis_index("gz")
        number = (2 * chip + core) * cap + number % cap
    hit = (slot_ref[...] == number).astype(jnp.bfloat16)
    rows = jnp.concatenate([piece[...] for piece in arrived], axis=0)
    samples = jnp.dot(hit, rows, preferred_element_type=jnp.float32)
    difference = image_ref[...].astype(jnp.float32) - samples
    _, _, at_k = axis_of_lane(8)
    for d in range(3):
        weighted = slope_ref[d].astype(jnp.float32) * difference
        corners = jnp.dot(
            weighted,
            shape_ref[...],
            preferred_element_type=jnp.float32,
            precision=lax.Precision.HIGHEST,
        ).T[:8]
        carried = pltpu.roll(corners, 4, 0)
        kept_ref[8 * d : 8 * d + 8, :] = corners + jnp.where(at_k > 0, pltpu.roll(carried, 1, 1), 0.0)
        sent_ref[8 * d : 8 * d + 8, :] = jnp.where(at_k == 0, pltpu.roll(carried, LANES - 7, 1), 0.0)
        sent_ref[8 * d + 4 : 8 * d + 6, :] = across_ref[2 * d : 2 * d + 2, :]


def layer_kernel(kept_ref, arrived_ref, stiff_ref, xy_ref, y_ref, x_ref, own_ref):
    at_i, at_j, _ = axis_of_lane(8)
    behind = lax.axis_index("gz") > 0

    def along_x(lower_half, upper_half):
        moved = pltpu.roll(upper_half, CY * CZ, 1)
        return lower_half + jnp.where(at_i > 0, moved, 0.0), jnp.where(at_i == 0, moved, 0.0)

    for d in range(3):
        part = slice(8 * d, 8 * d + 8)
        z = kept_ref[part, :] + jnp.where(behind, arrived_ref[part, :], 0.0)
        carried = pltpu.roll(z, 7, 0)
        stay = z + jnp.where(at_j > 0, pltpu.roll(carried, CZ, 1), 0.0)
        leave = jnp.where(at_j == 0, pltpu.roll(carried, LANES - CZ * (CY - 1), 1), 0.0)
        own, x = along_x(stay, pltpu.roll(stay, 6, 0))
        y, xy = along_x(leave, pltpu.roll(leave, 6, 0))
        stiff = stiff_ref[2 * d : 2 * d + 2, :] + arrived_ref[8 * d + 4 : 8 * d + 6, :]
        row = slice(d, d + 1)
        xy_ref[row, :] = xy[0:1] * data_weight
        y_ref[row, :] = y[0:1] * data_weight
        x_ref[row, :] = x[0:1] * data_weight + stiff[1:2]
        own_ref[row, :] = own[0:1] * data_weight + stiff[0:1]


def final_kernel(own_ref, xy_ref, y_ref, x_ref, out_ref):
    has_x = lax.axis_index("gx") > 0
    has_y = lax.axis_index("gy") > 0
    total = own_ref[0:3, :] + jnp.where(has_x, x_ref[0:3, :], 0.0)
    total = total + jnp.where(has_y, y_ref[0:3, :], 0.0)
    out_ref[...] = total + jnp.where(has_x & has_y, xy_ref[0:3, :], 0.0)


def navier(fields):
    at = axis_of_lane(8)
    steps = (CY * CZ, CZ, 1)
    extents = (CX, CY, CZ)

    def plus(p, q):
        return q if p is None else p if q is None else p + q

    def times(factor, p):
        return None if p is None else factor * p

    def along(axis, sign, centre, beyond):
        step, extent = steps[axis], extents[axis]
        back = step * (extent - 1)
        if sign > 0:
            inside, near, far = at[axis] < extent - 1, LANES - step, back
        else:
            inside, near, far = at[axis] > 0, step, LANES - back
        if centre is None and beyond is None:
            return None
        return jnp.where(
            inside,
            0.0 if centre is None else pltpu.roll(centre, near, 1),
            0.0 if beyond is None else pltpu.roll(beyond, far, 1),
        )

    def moved(vector, frame=(0, 0, 0), axis=2):
        if axis < 0:
            return fields.get(frame)
        sign = vector[axis]
        centre = moved(vector, frame, axis - 1)
        if sign == 0:
            return centre
        other = tuple(sign if n == axis else frame[n] for n in range(3))
        return along(axis, sign, centre, moved(vector, other, axis - 1))

    units = ((1, 0, 0), (0, 1, 0), (0, 0, 1))
    centre = fields.get((0, 0, 0))
    laplace = times(-6.0, centre)
    second = []
    for unit in units:
        both = plus(moved(unit), moved(tuple(-n for n in unit)))
        laplace = plus(laplace, both)
        second.append(plus(both, times(-2.0, centre)))
    mixed = {}
    for outer in range(3):
        for inner in range(outer + 1, 3):
            ahead = tuple(p + q for p, q in zip(units[outer], units[inner]))
            cross = tuple(p - q for p, q in zip(units[outer], units[inner]))
            aligned = plus(moved(ahead), moved(tuple(-n for n in ahead)))
            crossed = plus(moved(cross), moved(tuple(-n for n in cross)))
            mixed[outer, inner] = times(0.25, plus(aligned, times(-1.0, crossed)))
    rows = []
    for d in range(3):
        parts = [second[d]]
        for b in range(3):
            if b != d:
                part = mixed[min(b, d), max(b, d)]
                parts.append(None if part is None else pltpu.roll(part, (d - b) % 8, 0))
        total = functools.reduce(plus, parts)
        value = plus(times(shear_modulus, laplace), times(lame_first + shear_modulus, total))
        rows.append(jnp.zeros((1, LANES), jnp.float32) if value is None else -value[d : d + 1])
    return rows


def stiffness_kernel(below_ref, own_ref, above_ref, out_ref):
    here = [lax.axis_index(name) for name in ("gx", "gy", "gz")]
    sizes = [lax.axis_size(name) for name in ("gx", "gy", "gz")]
    slabs = {-1: below_ref, 0: own_ref, 1: above_ref}
    fields = {}
    for ox in (-1, 0, 1):
        for oy in (-1, 0, 1):
            for oz in (-1, 0, 1):
                if ox and oy and oz:
                    continue
                place = (here[0] + ox, here[1] + oy, here[2] + oz)
                inside = True
                for where, size in zip(place, sizes):
                    inside = inside & (where >= 0) & (where < size)
                peer = jnp.clip(place[1], 0, sizes[1] - 1) * sizes[2] + jnp.clip(
                    place[2], 0, sizes[2] - 1
                )
                fields[ox, oy, oz] = jnp.where(inside, slabs[ox][peer], 0.0)
    out_ref[...] = jnp.zeros((8, LANES), jnp.float32)
    for d, row in enumerate(navier(fields)):
        out_ref[2 * d : 2 * d + 1, :] = row


def column_kernel(own_ref, above_ref, kept_ref, across_ref):
    gx, gy, gz = [lax.axis_index(name) for name in ("gx", "gy", "gz")]
    n_x, n_y = lax.axis_size("gx"), lax.axis_size("gy")
    here, ahead = {}, {}
    for oy in (-1, 0, 1):
        place = gy + oy
        inside = (place >= 0) & (place < n_y)
        distance = lax.rem(oy + n_y, n_y)
        here[0, oy] = jnp.where(inside, own_ref[distance], 0.0)
        here[1, oy] = jnp.where(inside & (gx + 1 < n_x), above_ref[distance], 0.0)
        ahead[-1, oy] = here[0, oy]
    for n, columns in enumerate((here, ahead)):
        kept = {(ox, oy, 0): value for (ox, oy), value in columns.items()}
        across = {}
        for (ox, oy), value in columns.items():
            if not (ox and oy):
                across[ox, oy, -1] = jnp.where(gz == 0, value, 0.0)
                across[ox, oy, 1] = jnp.where(gz == 1, value, 0.0)
        for ref, fields in ((kept_ref, kept), (across_ref, across)):
            for d, row in enumerate(navier(fields)):
                ref[2 * d + n : 2 * d + n + 1, :] = row


def collect_kernel(after_ref, *refs):
    for n, ref in enumerate(refs[:-1]):
        refs[-1][n] = ref[DISP:META, :]


def small_call(kernel, shapes, name, *operands):
    return vmem_call(kernel, [(shape, jnp.float32) for shape in shapes], name, *operands)


def ring(value, axes, distance=1):
    count = lax.axis_size(axes)
    return lax.ppermute(value, axes, [(i, (i + distance) % count) for i in range(count)])


def ring_2(value):
    nx, ny = lax.axis_size("gx"), lax.axis_size("gy")
    route = [
        (x * ny + y, (x + 1) % nx * ny + (y + 1) % ny) for x in range(nx) for y in range(ny)
    ]
    return lax.ppermute(value, ("gx", "gy"), route)


def swapped(value, axes, mask):
    return lax.ppermute(value, axes, [(i, i ^ mask) for i in range(lax.axis_size(axes))])


def local(
    displacement,
    reference_image,
    image_gradient,
    deformed_blocks,
    fractions,
    offsets,
    send_list,
    recv_slot,
):
    n_y, n_z = lax.axis_size("gy"), lax.axis_size("gz")
    peers = n_y * n_z
    cap = send_list.shape[0] // peers
    (shape_values,) = vmem_call(
        shape_kernel, [((512, LANES), jnp.float32)], "shapes", cost=16 << 20, flops=1 << 33
    )
    packed, table = vmem_call(
        prepare_kernel,
        [((META, LANES), jnp.float32), ((TABLE, LANES), jnp.bfloat16)],
        "prepare",
        shape_values,
        fractions,
        displacement,
        offsets,
        recv_slot[None],
        send_list.reshape(-1, LANES),
        deformed_blocks,
    )
    relative = n_z == 2 and n_y in (2, 4) and 2 * cap == LANES
    if relative:
        metas = [packed] + [ring(packed, "gy", -d) for d in range(1, n_y)]
        mate = swapped(table, "gz", 1)
        arrived = [None] * n_y
        previous = metas[1:]
        for d in ([3, 1, 2] if n_y == 4 else [1]) + [0]:
            samples = sample_call(
                functools.partial(pair_kernel, d),
                metas[d],
                table,
                mate,
                *previous,
            )
            arrived[d] = ring(samples, "gy", d) if d else samples
            previous = [samples]
        (column,) = small_call(collect_kernel, [(n_y, 8, LANES)], "collect", arrived[n_y - 1], *metas)
        stiff, across = small_call(
            column_kernel, [(8, LANES)] * 2, "stiffness", column, ring(column, "gx", -1)
        )
    else:
        gathered = lax.all_gather(packed, SLAB, axis=0)
        readers = LANES // cap
        samples = [
            sample_call(
                functools.partial(group_kernel, g, cap),
                gathered[g * readers : (g + 1) * readers],
                table,
            )
            for g in range(peers // readers)
        ]
        outgoing = jnp.concatenate(samples, axis=0)
        arrived = [lax.all_to_all(outgoing, SLAB, split_axis=0, concat_axis=0, tiled=True)]
        slab = gathered[:, DISP:META]
        (stiff,) = small_call(
            stiffness_kernel, [(8, LANES)], "stiffness", ring(slab, "gx", 1), slab, ring(slab, "gx", -1)
        )
        across = jnp.zeros((8, LANES), jnp.float32)
    kept, sent = small_call(
        functools.partial(force_kernel, cap, relative),
        [(24, LANES)] * 2,
        "forces",
        across,
        recv_slot[:, None],
        reference_image,
        image_gradient,
        shape_values,
        *arrived,
    )
    xy, y, x, own = small_call(
        layer_kernel, [(8, LANES)] * 4, "layers", kept, ring(sent, "gz"), stiff
    )
    return small_call(
        final_kernel, [(3, LANES)], "total", own, ring_2(xy), ring(y, "gy"), ring(x, "gx")
    )[0]


def solution(mesh):
    in_specs = (
        P(None, ("gx", "gy", "gz")),
        P(("gx", "gy", "gz"), None),
        P(None, ("gx", "gy", "gz"), None),
        P(("gx", "gy", "gz"), None),
        P(None, ("gx", "gy", "gz")),
        P(None, ("gx", "gy", "gz")),
        P(("gx", "gy", "gz")),
        P(("gx", "gy", "gz")),
    )
    out_specs = P(None, ("gx", "gy", "gz"))
    return jax.shard_map(local, mesh=mesh, in_specs=in_specs, out_specs=out_specs, check_vma=False)
```

```python
import functools

import jax
import jax.numpy as jnp
from jax import lax
from jax.experimental import pallas as pl
from jax.experimental.pallas import tpu as pltpu
from jax.sharding import PartitionSpec as P

CX = 2
CY = 8
CZ = 8
LANES = CX * CY * CZ
SLAB = ("gy", "gz")

shear_modulus = 0.05
lame_first = 1.0
data_weight = 0.0625

DISP = 24
OFFS = 27
SLOT = 30
META = 32

VOXELS = 4096
TABLE = VOXELS + 16


def iota(shape, dim):
    return lax.broadcasted_iota(jnp.int32, shape, dim)


def shifted(planes, bits):
    for bit, count in ((2, 12), (1, 10), (0, 9)):
        step = 1 << bit
        planes = [jnp.where(bits[bit], planes[p + step], planes[p]) for p in range(count)]
    return planes


def offset_bits(offset, rows):
    wide = jnp.broadcast_to(offset, (rows, LANES))
    return [(wide & (1 << bit)) != 0 for bit in range(3)]


def shape_kernel(out_ref):
    voxel, column = iota((512, LANES), 0), iota((512, LANES), 1)

    def weight(index, upper):
        centre = (index.astype(jnp.float32) + 0.5) * 0.125
        return jnp.where(upper == 1, centre, 1.0 - centre)

    values = weight(voxel // 64, column // 2 % 2) * weight(voxel // 8 % 8, column % 2)
    values = values * weight(voxel % 8, column // 4)
    out_ref[...] = jnp.where(column < 8, values, 0.0)


def prepare_kernel(
    after_ref, fraction_ref, displacement_ref, offset_ref, slot_ref, send_ref, block_ref, packed_ref, table_ref
):
    packed_ref[:DISP, :] = fraction_ref[...].astype(jnp.float32)
    packed_ref[DISP:OFFS, :] = displacement_ref[...]
    packed_ref[OFFS:SLOT, :] = offset_ref[...].astype(jnp.float32)
    packed_ref[SLOT : SLOT + 1, :] = slot_ref[...].astype(jnp.float32)
    packed_ref[SLOT + 1 :, :] = jnp.zeros((META - SLOT - 1, LANES), jnp.float32)
    for start in range(0, VOXELS, 512):
        table_ref[start : start + 512, :] = block_ref[:, start : start + 512].T
    rows = send_ref.shape[0]
    listed = jnp.concatenate(
        [send_ref[...].astype(jnp.float32), jnp.zeros((TABLE - VOXELS - rows, LANES), jnp.float32)],
        axis=0,
    )
    table_ref[VOXELS:, :] = listed.astype(jnp.bfloat16)


def vmem_call(kernel, shapes, name, *operands, cost=1 << 20, flops=1 << 20):
    vmem = pl.BlockSpec(memory_space=pltpu.VMEM)
    return pl.pallas_call(
        kernel,
        out_shape=[jax.ShapeDtypeStruct(shape, dtype) for shape, dtype in shapes],
        in_specs=[vmem] * len(operands),
        out_specs=[vmem] * len(shapes),
        compiler_params=pltpu.CompilerParams(vmem_limit_bytes=24 << 20),
        cost_estimate=pl.CostEstimate(flops=flops, bytes_accessed=cost, transcendentals=0),
        name=name,
    )(*operands)


def interpolated(table_refs, pick, meta, along_a, along_b, along_c):
    upper = meta[:24]
    lower = 1.0 - upper
    offsets = meta[OFFS : OFFS + 3].astype(jnp.int32)
    bits = offset_bits(offsets[0:1], 16)
    for b in range(16):
        starts = [256 * a + 16 * b for a in range(16)]
        rows = jnp.concatenate(
            [
                jnp.concatenate([ref[start : start + 16, :] for start in starts], axis=0)
                for ref in table_refs
            ],
            axis=1,
        )
        voxels = jnp.dot(rows, pick, preferred_element_type=jnp.float32)
        window = shifted([voxels[16 * a : 16 * a + 16] for a in range(16)], bits)
        for i in range(8):
            along_a[256 * i + 16 * b : 256 * i + 16 * b + 16, :] = (
                lower[i : i + 1] * window[i] + upper[i : i + 1] * window[i + 1]
            )
    bits = offset_bits(offsets[1:2], 16)
    for i in range(8):
        window = shifted(
            [along_a[256 * i + 16 * b : 256 * i + 16 * b + 16, :] for b in range(16)], bits
        )
        for j in range(8):
            along_b[128 * i + 16 * j : 128 * i + 16 * j + 16, :] = (
                lower[8 + j : 9 + j] * window[j] + upper[8 + j : 9 + j] * window[j + 1]
            )
    bits = offset_bits(offsets[2:3], 8)
    for i in range(8):
        window = shifted(
            [along_b[pl.ds(128 * i + c, 8, stride=16), :] for c in range(16)], bits
        )
        for k in range(8):
            along_c[pl.ds(64 * i + k, 8, stride=8), :] = (
                lower[16 + k : 17 + k] * window[k] + upper[16 + k : 17 + k] * window[k + 1]
            )
    return along_c[...].T.astype(jnp.bfloat16)


def slot_meta(meta, slots):
    wanted = meta[SLOT : SLOT + 1].astype(jnp.int32)
    return lax.dot_general(
        meta.astype(jnp.bfloat16),
        (wanted == slots).astype(jnp.bfloat16),
        (((1,), (1,)), ((), ())),
        preferred_element_type=jnp.float32,
    )


def pair_kernel(distance, meta_ref, own_ref, mate_ref, *rest):
    out_ref, scratch = rest[-4], rest[-3:]
    gy, gz = lax.axis_index("gy"), lax.axis_index("gz")
    half = LANES // 2
    slot = iota((LANES, LANES), 0)
    slots = (((2 * gy + gz) ^ (slot // half)) * half) + slot % half
    meta = slot_meta(meta_ref[...], slots)
    chip = lax.rem(gy + distance, lax.axis_size("gy"))
    lists = [ref[VOXELS:, :].astype(jnp.float32) for ref in (own_ref, mate_ref)]
    here = iota(lists[0].shape, 0) == chip
    own, mate = [
        jnp.sum(jnp.where(here, listed, 0.0), axis=0, keepdims=True).astype(jnp.int32)
        for listed in lists
    ]
    first = gz == 0
    own = jnp.where(first, own, pltpu.roll(own, half, 1))
    mate = jnp.where(first, pltpu.roll(mate, half, 1), mate)
    row = jnp.where(iota((1, LANES), 1) < half, own, mate + LANES)
    pick = (iota((2 * LANES, LANES), 0) == row).astype(jnp.bfloat16)
    out_ref[...] = interpolated((own_ref, mate_ref), pick, meta, *scratch)


def group_kernel(group, cap, meta_ref, table_ref, out_ref, *scratch):
    holder = lax.axis_index("gy") * lax.axis_size("gz") + lax.axis_index("gz")
    slot = iota((LANES, LANES), 0)
    meta = jnp.zeros((META, LANES), jnp.float32)
    for r in range(LANES // cap):
        slots = jnp.where(slot // cap == r, holder * cap + slot - r * cap, -1)
        meta = meta + slot_meta(meta_ref[r], slots)
    row = table_ref[VOXELS:, :].astype(jnp.float32)[group : group + 1].astype(jnp.int32)
    pick = (iota((LANES, LANES), 0) == row).astype(jnp.bfloat16)
    out_ref[...] = interpolated((table_ref,), pick, meta, *scratch)


def sample_call(kernel, *operands):
    vmem = pl.BlockSpec(memory_space=pltpu.VMEM)
    return pl.pallas_call(
        kernel,
        out_shape=jax.ShapeDtypeStruct((LANES, 512), jnp.bfloat16),
        in_specs=[vmem] * len(operands),
        out_specs=vmem,
        scratch_shapes=[
            pltpu.VMEM((2048, LANES), jnp.float32),
            pltpu.VMEM((1024, LANES), jnp.float32),
            pltpu.VMEM((512, LANES), jnp.float32),
        ],
        compiler_params=pltpu.CompilerParams(vmem_limit_bytes=24 << 20),
        cost_estimate=pl.CostEstimate(
            flops=1300000000, bytes_accessed=1, transcendentals=0
        ),
        name="interpolate",
    )(*operands)


def axis_of_lane(rows):
    lane = iota((rows, LANES), 1)
    return lane // (CY * CZ), lane // CZ % CY, lane % CZ


def force_kernel(cap, relative, across_ref, slot_ref, image_ref, slope_ref, shape_ref, *rest):
    arrived, (kept_ref, sent_ref) = rest[:-2], rest[-2:]
    total = sum(piece.shape[0] for piece in arrived)
    number = iota((LANES, total), 1)
    if relative:
        n_y = lax.axis_size("gy")
        chip = lax.rem(lax.axis_index("gy") + n_y - number // (2 * cap), n_y)
        core = (number // cap % 2) ^ lax.axis_index("gz")
        number = (2 * chip + core) * cap + number % cap
    hit = (slot_ref[...] == number).astype(jnp.bfloat16)
    rows = jnp.concatenate([piece[...] for piece in arrived], axis=0)
    samples = jnp.dot(hit, rows, preferred_element_type=jnp.float32)
    difference = image_ref[...].astype(jnp.float32) - samples
    _, _, at_k = axis_of_lane(8)
    for d in range(3):
        weighted = slope_ref[d].astype(jnp.float32) * difference
        corners = jnp.dot(
            weighted,
            shape_ref[...],
            preferred_element_type=jnp.float32,
            precision=lax.Precision.HIGHEST,
        ).T[:8]
        carried = pltpu.roll(corners, 4, 0)
        kept_ref[8 * d : 8 * d + 8, :] = corners + jnp.where(at_k > 0, pltpu.roll(carried, 1, 1), 0.0)
        sent_ref[8 * d : 8 * d + 8, :] = jnp.where(at_k == 0, pltpu.roll(carried, LANES - 7, 1), 0.0)
        sent_ref[8 * d + 4 : 8 * d + 6, :] = across_ref[2 * d : 2 * d + 2, :]


def layer_kernel(kept_ref, arrived_ref, stiff_ref, xy_ref, y_ref, x_ref, own_ref):
    at_i, at_j, _ = axis_of_lane(8)
    behind = lax.axis_index("gz") > 0

    def along_x(lower_half, upper_half):
        moved = pltpu.roll(upper_half, CY * CZ, 1)
        return lower_half + jnp.where(at_i > 0, moved, 0.0), jnp.where(at_i == 0, moved, 0.0)

    for d in range(3):
        part = slice(8 * d, 8 * d + 8)
        z = kept_ref[part, :] + jnp.where(behind, arrived_ref[part, :], 0.0)
        carried = pltpu.roll(z, 7, 0)
        stay = z + jnp.where(at_j > 0, pltpu.roll(carried, CZ, 1), 0.0)
        leave = jnp.where(at_j == 0, pltpu.roll(carried, LANES - CZ * (CY - 1), 1), 0.0)
        own, x = along_x(stay, pltpu.roll(stay, 6, 0))
        y, xy = along_x(leave, pltpu.roll(leave, 6, 0))
        stiff = stiff_ref[2 * d : 2 * d + 2, :] + arrived_ref[8 * d + 4 : 8 * d + 6, :]
        row = slice(d, d + 1)
        xy_ref[row, :] = xy[0:1] * data_weight
        y_ref[row, :] = y[0:1] * data_weight
        x_ref[row, :] = x[0:1] * data_weight + stiff[1:2]
        own_ref[row, :] = own[0:1] * data_weight + stiff[0:1]


def final_kernel(own_ref, xy_ref, y_ref, x_ref, out_ref):
    has_x = lax.axis_index("gx") > 0
    has_y = lax.axis_index("gy") > 0
    total = own_ref[0:3, :] + jnp.where(has_x, x_ref[0:3, :], 0.0)
    total = total + jnp.where(has_y, y_ref[0:3, :], 0.0)
    out_ref[...] = total + jnp.where(has_x & has_y, xy_ref[0:3, :], 0.0)


def navier(fields):
    at = axis_of_lane(8)
    steps = (CY * CZ, CZ, 1)
    extents = (CX, CY, CZ)

    def plus(p, q):
        return q if p is None else p if q is None else p + q

    def times(factor, p):
        return None if p is None else factor * p

    def along(axis, sign, centre, beyond):
        step, extent = steps[axis], extents[axis]
        back = step * (extent - 1)
        if sign > 0:
            inside, near, far = at[axis] < extent - 1, LANES - step, back
        else:
            inside, near, far = at[axis] > 0, step, LANES - back
        if centre is None and beyond is None:
            return None
        return jnp.where(
            inside,
            0.0 if centre is None else pltpu.roll(centre, near, 1),
            0.0 if beyond is None else pltpu.roll(beyond, far, 1),
        )

    def moved(vector, frame=(0, 0, 0), axis=2):
        if axis < 0:
            return fields.get(frame)
        sign = vector[axis]
        centre = moved(vector, frame, axis - 1)
        if sign == 0:
            return centre
        other = tuple(sign if n == axis else frame[n] for n in range(3))
        return along(axis, sign, centre, moved(vector, other, axis - 1))

    units = ((1, 0, 0), (0, 1, 0), (0, 0, 1))
    centre = fields.get((0, 0, 0))
    laplace = times(-6.0, centre)
    second = []
    for unit in units:
        both = plus(moved(unit), moved(tuple(-n for n in unit)))
        laplace = plus(laplace, both)
        second.append(plus(both, times(-2.0, centre)))
    mixed = {}
    for outer in range(3):
        for inner in range(outer + 1, 3):
            ahead = tuple(p + q for p, q in zip(units[outer], units[inner]))
            cross = tuple(p - q for p, q in zip(units[outer], units[inner]))
            aligned = plus(moved(ahead), moved(tuple(-n for n in ahead)))
            crossed = plus(moved(cross), moved(tuple(-n for n in cross)))
            mixed[outer, inner] = times(0.25, plus(aligned, times(-1.0, crossed)))
    rows = []
    for d in range(3):
        parts = [second[d]]
        for b in range(3):
            if b != d:
                part = mixed[min(b, d), max(b, d)]
                parts.append(None if part is None else pltpu.roll(part, (d - b) % 8, 0))
        total = functools.reduce(plus, parts)
        value = plus(times(shear_modulus, laplace), times(lame_first + shear_modulus, total))
        rows.append(jnp.zeros((1, LANES), jnp.float32) if value is None else -value[d : d + 1])
    return rows


def stiffness_kernel(below_ref, own_ref, above_ref, out_ref):
    here = [lax.axis_index(name) for name in ("gx", "gy", "gz")]
    sizes = [lax.axis_size(name) for name in ("gx", "gy", "gz")]
    slabs = {-1: below_ref, 0: own_ref, 1: above_ref}
    fields = {}
    for ox in (-1, 0, 1):
        for oy in (-1, 0, 1):
            for oz in (-1, 0, 1):
                if ox and oy and oz:
                    continue
                place = (here[0] + ox, here[1] + oy, here[2] + oz)
                inside = True
                for where, size in zip(place, sizes):
                    inside = inside & (where >= 0) & (where < size)
                peer = jnp.clip(place[1], 0, sizes[1] - 1) * sizes[2] + jnp.clip(
                    place[2], 0, sizes[2] - 1
                )
                fields[ox, oy, oz] = jnp.where(inside, slabs[ox][peer], 0.0)
    out_ref[...] = jnp.zeros((8, LANES), jnp.float32)
    for d, row in enumerate(navier(fields)):
        out_ref[2 * d : 2 * d + 1, :] = row


def column_kernel(own_ref, above_ref, kept_ref, across_ref):
    gx, gy, gz = [lax.axis_index(name) for name in ("gx", "gy", "gz")]
    n_x, n_y = lax.axis_size("gx"), lax.axis_size("gy")
    here, ahead = {}, {}
    for oy in (-1, 0, 1):
        place = gy + oy
        inside = (place >= 0) & (place < n_y)
        distance = lax.rem(oy + n_y, n_y)
        here[0, oy] = jnp.where(inside, own_ref[distance], 0.0)
        here[1, oy] = jnp.where(inside & (gx + 1 < n_x), above_ref[distance], 0.0)
        ahead[-1, oy] = here[0, oy]
    for n, columns in enumerate((here, ahead)):
        kept = {(ox, oy, 0): value for (ox, oy), value in columns.items()}
        across = {}
        for (ox, oy), value in columns.items():
            if not (ox and oy):
                across[ox, oy, -1] = jnp.where(gz == 0, value, 0.0)
                across[ox, oy, 1] = jnp.where(gz == 1, value, 0.0)
        for ref, fields in ((kept_ref, kept), (across_ref, across)):
            for d, row in enumerate(navier(fields)):
                ref[2 * d + n : 2 * d + n + 1, :] = row


def collect_kernel(after_ref, *refs):
    for n, ref in enumerate(refs[:-1]):
        refs[-1][n] = ref[DISP:META, :]


def small_call(kernel, shapes, name, *operands):
    return vmem_call(kernel, [(shape, jnp.float32) for shape in shapes], name, *operands)


def ring(value, axes, distance=1):
    count = lax.axis_size(axes)
    return lax.ppermute(value, axes, [(i, (i + distance) % count) for i in range(count)])


def ring_2(value):
    nx, ny = lax.axis_size("gx"), lax.axis_size("gy")
    route = [
        (x * ny + y, (x + 1) % nx * ny + (y + 1) % ny) for x in range(nx) for y in range(ny)
    ]
    return lax.ppermute(value, ("gx", "gy"), route)


def swapped(value, axes, mask):
    return lax.ppermute(value, axes, [(i, i ^ mask) for i in range(lax.axis_size(axes))])


def local(
    displacement,
    reference_image,
    image_gradient,
    deformed_blocks,
    fractions,
    offsets,
    send_list,
    recv_slot,
):
    n_y, n_z = lax.axis_size("gy"), lax.axis_size("gz")
    peers = n_y * n_z
    cap = send_list.shape[0] // peers
    (shape_values,) = vmem_call(
        shape_kernel, [((512, LANES), jnp.float32)], "shapes", cost=16 << 20, flops=1 << 33
    )
    packed, table = vmem_call(
        prepare_kernel,
        [((META, LANES), jnp.float32), ((TABLE, LANES), jnp.bfloat16)],
        "prepare",
        shape_values,
        fractions,
        displacement,
        offsets,
        recv_slot[None],
        send_list.reshape(-1, LANES),
        deformed_blocks,
    )
    relative = n_z == 2 and n_y in (2, 4) and 2 * cap == LANES
    if relative:
        metas = [packed] + [ring(packed, "gy", -d) for d in range(1, n_y)]
        mate = swapped(table, "gz", 1)
        arrived = [None] * n_y
        previous = []
        for d in ([3, 1, 2] if n_y == 4 else [1]) + [0]:
            samples = sample_call(
                functools.partial(pair_kernel, d),
                metas[d],
                table,
                mate,
                *previous,
            )
            arrived[d] = ring(samples, "gy", d) if d else samples
            previous = [samples]
        (column,) = small_call(collect_kernel, [(n_y, 8, LANES)], "collect", arrived[n_y - 1], *metas)
        stiff, across = small_call(
            column_kernel, [(8, LANES)] * 2, "stiffness", column, ring(column, "gx", -1)
        )
    else:
        gathered = lax.all_gather(packed, SLAB, axis=0)
        readers = LANES // cap
        samples = [
            sample_call(
                functools.partial(group_kernel, g, cap),
                gathered[g * readers : (g + 1) * readers],
                table,
            )
            for g in range(peers // readers)
        ]
        outgoing = jnp.concatenate(samples, axis=0)
        arrived = [lax.all_to_all(outgoing, SLAB, split_axis=0, concat_axis=0, tiled=True)]
        slab = gathered[:, DISP:META]
        (stiff,) = small_call(
            stiffness_kernel, [(8, LANES)], "stiffness", ring(slab, "gx", 1), slab, ring(slab, "gx", -1)
        )
        across = jnp.zeros((8, LANES), jnp.float32)
    kept, sent = small_call(
        functools.partial(force_kernel, cap, relative),
        [(24, LANES)] * 2,
        "forces",
        across,
        recv_slot[:, None],
        reference_image,
        image_gradient,
        shape_values,
        *arrived,
    )
    xy, y, x, own = small_call(
        layer_kernel, [(8, LANES)] * 4, "layers", kept, ring(sent, "gz"), stiff
    )
    return small_call(
        final_kernel, [(3, LANES)], "total", own, ring_2(xy), ring(y, "gy"), ring(x, "gx")
    )[0]


def solution(mesh):
    in_specs = (
        P(None, ("gx", "gy", "gz")),
        P(("gx", "gy", "gz"), None),
        P(None, ("gx", "gy", "gz"), None),
        P(("gx", "gy", "gz"), None),
        P(None, ("gx", "gy", "gz")),
        P(None, ("gx", "gy", "gz")),
        P(("gx", "gy", "gz")),
        P(("gx", "gy", "gz")),
    )
    out_specs = P(None, ("gx", "gy", "gz"))
    return jax.shard_map(local, mesh=mesh, in_specs=in_specs, out_specs=out_specs, check_vma=False)
```

```python
import functools

import jax
import jax.numpy as jnp
from jax import lax
from jax.experimental import pallas as pl
from jax.experimental.pallas import tpu as pltpu
from jax.sharding import PartitionSpec as P

CX = 2
CY = 8
CZ = 8
LANES = CX * CY * CZ
SLAB = ("gy", "gz")

shear_modulus = 0.05
lame_first = 1.0
data_weight = 0.0625

DISP = 24
OFFS = 27
SLOT = 30
META = 32

VOXELS = 4096


def iota(shape, dim):
    return lax.broadcasted_iota(jnp.int32, shape, dim)


def shifted(planes, bits):
    for bit, count in ((2, 12), (1, 10), (0, 9)):
        step = 1 << bit
        planes = [jnp.where(bits[bit], planes[p + step], planes[p]) for p in range(count)]
    return planes


def offset_bits(offset, rows):
    wide = jnp.broadcast_to(offset, (rows, LANES))
    return [(wide & (1 << bit)) != 0 for bit in range(3)]


def shape_kernel(out_ref):
    voxel, column = iota((512, LANES), 0), iota((512, LANES), 1)

    def weight(index, upper):
        centre = (index.astype(jnp.float32) + 0.5) * 0.125
        return jnp.where(upper == 1, centre, 1.0 - centre)

    values = weight(voxel // 64, column // 2 % 2) * weight(voxel // 8 % 8, column % 2)
    values = values * weight(voxel % 8, column // 4 % 2)
    coarse = values.astype(jnp.bfloat16).astype(jnp.float32)
    values = jnp.where(column < 8, coarse, jnp.where(column < 16, values - coarse, 0.0))
    out_ref[...] = values.astype(jnp.bfloat16)


def pack_kernel(after_ref, fraction_ref, displacement_ref, offset_ref, slot_ref, out_ref):
    out_ref[:DISP, :] = fraction_ref[...].astype(jnp.float32)
    out_ref[DISP:OFFS, :] = displacement_ref[...]
    out_ref[OFFS:SLOT, :] = offset_ref[...].astype(jnp.float32)
    out_ref[SLOT : SLOT + 1, :] = slot_ref[...].astype(jnp.float32)
    out_ref[SLOT + 1 :, :] = jnp.zeros((META - SLOT - 1, LANES), jnp.float32)


def table_kernel(after_ref, later_ref, *refs):
    out_ref = refs[-1]
    for n, ref in enumerate(refs[:-1]):
        for start in range(0, VOXELS, 512):
            out_ref[start : start + 512, LANES * n : LANES * n + LANES] = ref[
                :, start : start + 512
            ].T


def vmem_call(kernel, shapes, name, *operands, cost=1 << 20, flops=1 << 20):
    vmem = pl.BlockSpec(memory_space=pltpu.VMEM)
    return pl.pallas_call(
        kernel,
        out_shape=[jax.ShapeDtypeStruct(shape, dtype) for shape, dtype in shapes],
        in_specs=[vmem] * len(operands),
        out_specs=[vmem] * len(shapes),
        compiler_params=pltpu.CompilerParams(vmem_limit_bytes=24 << 20),
        cost_estimate=pl.CostEstimate(flops=flops, bytes_accessed=cost, transcendentals=0),
        name=name,
    )(*operands)


def interpolated(table_ref, pick, meta, along_a, along_b, along_c):
    upper = meta[:24]
    lower = 1.0 - upper
    offsets = meta[OFFS : OFFS + 3].astype(jnp.int32)
    bits = offset_bits(offsets[0:1], 16)
    for first in range(0, 256, 16):
        starts = [256 * a + first for a in range(16)]
        rows = jnp.concatenate([table_ref[start : start + 16, :] for start in starts], axis=0)
        voxels = jnp.dot(rows, pick, preferred_element_type=jnp.float32)
        window = shifted([voxels[16 * a : 16 * a + 16] for a in range(16)], bits)
        for i in range(8):
            along_a[256 * i + first : 256 * i + first + 16, :] = (
                lower[i : i + 1] * window[i] + upper[i : i + 1] * window[i + 1]
            )
    bits = offset_bits(offsets[1:2], 16)
    for i in range(8):
        window = shifted(
            [along_a[256 * i + 16 * b : 256 * i + 16 * b + 16, :] for b in range(16)], bits
        )
        for j in range(8):
            along_b[128 * i + 16 * j : 128 * i + 16 * j + 16, :] = (
                lower[8 + j : 9 + j] * window[j] + upper[8 + j : 9 + j] * window[j + 1]
            )
    bits = offset_bits(offsets[2:3], 8)
    for i in range(8):
        window = shifted(
            [along_b[pl.ds(128 * i + c, 8, stride=16), :] for c in range(16)], bits
        )
        for k in range(8):
            along_c[pl.ds(64 * i + k, 8, stride=8), :] = (
                lower[16 + k : 17 + k] * window[k] + upper[16 + k : 17 + k] * window[k + 1]
            )
    return along_c[...].T.astype(jnp.bfloat16)


def slot_meta(meta, slots):
    wanted = meta[SLOT : SLOT + 1].astype(jnp.int32)
    return lax.dot_general(
        meta.astype(jnp.bfloat16),
        (wanted == slots).astype(jnp.bfloat16),
        (((1,), (1,)), ((), ())),
        preferred_element_type=jnp.float32,
    )


def pair_kernel(distance, meta_ref, table_ref, own_ref, mate_ref, *rest):
    out_ref, scratch = rest[-4], rest[-3:]
    gy, gz = lax.axis_index("gy"), lax.axis_index("gz")
    half = LANES // 2
    slot = iota((LANES, LANES), 0)
    slots = (((2 * gy + gz) ^ (slot // half)) * half) + slot % half
    meta = slot_meta(meta_ref[...], slots)
    chip = lax.rem(gy + distance, lax.axis_size("gy"))
    chip = pl.ds(chip, 1)
    own, mate = own_ref[chip, :], mate_ref[chip, :]
    first = gz == 0
    own = jnp.where(first, own, pltpu.roll(own, half, 1))
    mate = jnp.where(first, pltpu.roll(mate, half, 1), mate)
    row = jnp.where(iota((1, LANES), 1) < half, own, mate + LANES)
    pick = (iota((2 * LANES, LANES), 0) == row).astype(jnp.bfloat16)
    out_ref[...] = interpolated(table_ref, pick, meta, *scratch)


def group_kernel(group, cap, meta_ref, table_ref, send_ref, out_ref, *scratch):
    holder = lax.axis_index("gy") * lax.axis_size("gz") + lax.axis_index("gz")
    slot = iota((LANES, LANES), 0)
    meta = jnp.zeros((META, LANES), jnp.float32)
    for r in range(LANES // cap):
        slots = jnp.where(slot // cap == r, holder * cap + slot - r * cap, -1)
        meta = meta + slot_meta(meta_ref[r], slots)
    pick = (iota((LANES, LANES), 0) == send_ref[group : group + 1, :]).astype(jnp.bfloat16)
    out_ref[...] = interpolated(table_ref, pick, meta, *scratch)


def sample_call(kernel, *operands):
    vmem = pl.BlockSpec(memory_space=pltpu.VMEM)
    return pl.pallas_call(
        kernel,
        out_shape=jax.ShapeDtypeStruct((LANES, 512), jnp.bfloat16),
        in_specs=[vmem] * len(operands),
        out_specs=vmem,
        scratch_shapes=[
            pltpu.VMEM((2048, LANES), jnp.float32),
            pltpu.VMEM((1024, LANES), jnp.float32),
            pltpu.VMEM((512, LANES), jnp.float32),
        ],
        compiler_params=pltpu.CompilerParams(vmem_limit_bytes=24 << 20),
        cost_estimate=pl.CostEstimate(
            flops=4000000000, bytes_accessed=1, transcendentals=0
        ),
        name="interpolate",
    )(*operands)


def axis_of_lane(rows):
    lane = iota((rows, LANES), 1)
    return lane // (CY * CZ), lane // CZ % CY, lane % CZ


def force_kernel(cap, relative, across_ref, slot_ref, image_ref, slope_ref, shape_ref, *rest):
    arrived, (kept_ref, sent_ref) = rest[:-2], rest[-2:]
    total = sum(piece.shape[0] for piece in arrived)
    number = iota((LANES, total), 1)
    if relative:
        n_y = lax.axis_size("gy")
        chip = lax.rem(lax.axis_index("gy") + n_y - number // (2 * cap), n_y)
        core = (number // cap % 2) ^ lax.axis_index("gz")
        number = (2 * chip + core) * cap + number % cap
    hit = (slot_ref[...] == number).astype(jnp.bfloat16)
    rows = jnp.concatenate([piece[...] for piece in arrived], axis=0)
    samples = jnp.dot(hit, rows, preferred_element_type=jnp.float32)
    difference = image_ref[...].astype(jnp.float32) - samples
    parts = []
    for d in range(3):
        weighted = slope_ref[d].astype(jnp.float32) * difference
        coarse = weighted.astype(jnp.bfloat16)
        parts += [coarse, (weighted - coarse.astype(jnp.float32)).astype(jnp.bfloat16)]
    sums = jnp.dot(
        jnp.concatenate(parts, axis=0), shape_ref[...], preferred_element_type=jnp.float32
    )
    columns = 0.0
    for d in range(3):
        both = sums[2 * LANES * d : 2 * LANES * d + LANES] + sums[2 * LANES * d + LANES : 2 * LANES * (d + 1)]
        columns = columns + (pltpu.roll(both, 16 * d, 1) if d else both)
    columns = columns.T
    _, _, at_k = axis_of_lane(8)
    for d in range(3):
        corners = columns[16 * d : 16 * d + 8] + columns[16 * d + 8 : 16 * d + 16]
        carried = pltpu.roll(corners, 4, 0)
        kept_ref[8 * d : 8 * d + 8, :] = corners + jnp.where(at_k > 0, pltpu.roll(carried, 1, 1), 0.0)
        sent_ref[8 * d : 8 * d + 8, :] = jnp.where(at_k == 0, pltpu.roll(carried, LANES - 7, 1), 0.0)
        sent_ref[8 * d + 4 : 8 * d + 6, :] = across_ref[2 * d : 2 * d + 2, :]


def layer_kernel(kept_ref, arrived_ref, stiff_ref, xy_ref, y_ref, x_ref, own_ref):
    at_i, at_j, _ = axis_of_lane(8)
    behind = lax.axis_index("gz") > 0

    def along_x(lower_half, upper_half):
        moved = pltpu.roll(upper_half, CY * CZ, 1)
        return lower_half + jnp.where(at_i > 0, moved, 0.0), jnp.where(at_i == 0, moved, 0.0)

    for d in range(3):
        part = slice(8 * d, 8 * d + 8)
        z = kept_ref[part, :] + jnp.where(behind, arrived_ref[part, :], 0.0)
        carried = pltpu.roll(z, 7, 0)
        stay = z + jnp.where(at_j > 0, pltpu.roll(carried, CZ, 1), 0.0)
        leave = jnp.where(at_j == 0, pltpu.roll(carried, LANES - CZ * (CY - 1), 1), 0.0)
        own, x = along_x(stay, pltpu.roll(stay, 6, 0))
        y, xy = along_x(leave, pltpu.roll(leave, 6, 0))
        stiff = stiff_ref[2 * d : 2 * d + 2, :] + arrived_ref[8 * d + 4 : 8 * d + 6, :]
        row = slice(d, d + 1)
        xy_ref[row, :] = xy[0:1] * data_weight
        y_ref[row, :] = y[0:1] * data_weight
        x_ref[row, :] = x[0:1] * data_weight + stiff[1:2]
        own_ref[row, :] = own[0:1] * data_weight + stiff[0:1]


def final_kernel(own_ref, xy_ref, y_ref, x_ref, out_ref):
    has_x = lax.axis_index("gx") > 0
    has_y = lax.axis_index("gy") > 0
    total = own_ref[0:3, :] + jnp.where(has_x, x_ref[0:3, :], 0.0)
    total = total + jnp.where(has_y, y_ref[0:3, :], 0.0)
    out_ref[...] = total + jnp.where(has_x & has_y, xy_ref[0:3, :], 0.0)


def navier(fields):
    at = axis_of_lane(8)
    steps = (CY * CZ, CZ, 1)
    extents = (CX, CY, CZ)

    def plus(p, q):
        return q if p is None else p if q is None else p + q

    def times(factor, p):
        return None if p is None else factor * p

    def along(axis, sign, centre, beyond):
        step, extent = steps[axis], extents[axis]
        back = step * (extent - 1)
        if sign > 0:
            inside, near, far = at[axis] < extent - 1, LANES - step, back
        else:
            inside, near, far = at[axis] > 0, step, LANES - back
        if centre is None and beyond is None:
            return None
        return jnp.where(
            inside,
            0.0 if centre is None else pltpu.roll(centre, near, 1),
            0.0 if beyond is None else pltpu.roll(beyond, far, 1),
        )

    def moved(vector, frame=(0, 0, 0), axis=2):
        if axis < 0:
            return fields.get(frame)
        sign = vector[axis]
        centre = moved(vector, frame, axis - 1)
        if sign == 0:
            return centre
        other = tuple(sign if n == axis else frame[n] for n in range(3))
        return along(axis, sign, centre, moved(vector, other, axis - 1))

    units = ((1, 0, 0), (0, 1, 0), (0, 0, 1))
    centre = fields.get((0, 0, 0))
    laplace = times(-6.0, centre)
    second = []
    for unit in units:
        both = plus(moved(unit), moved(tuple(-n for n in unit)))
        laplace = plus(laplace, both)
        second.append(plus(both, times(-2.0, centre)))
    mixed = {}
    for outer in range(3):
        for inner in range(outer + 1, 3):
            ahead = tuple(p + q for p, q in zip(units[outer], units[inner]))
            cross = tuple(p - q for p, q in zip(units[outer], units[inner]))
            aligned = plus(moved(ahead), moved(tuple(-n for n in ahead)))
            crossed = plus(moved(cross), moved(tuple(-n for n in cross)))
            mixed[outer, inner] = times(0.25, plus(aligned, times(-1.0, crossed)))
    rows = []
    for d in range(3):
        parts = [second[d]]
        for b in range(3):
            if b != d:
                part = mixed[min(b, d), max(b, d)]
                parts.append(None if part is None else pltpu.roll(part, (d - b) % 8, 0))
        total = functools.reduce(plus, parts)
        value = plus(times(shear_modulus, laplace), times(lame_first + shear_modulus, total))
        rows.append(jnp.zeros((1, LANES), jnp.float32) if value is None else -value[d : d + 1])
    return rows


def stiffness_kernel(below_ref, own_ref, above_ref, out_ref):
    here = [lax.axis_index(name) for name in ("gx", "gy", "gz")]
    sizes = [lax.axis_size(name) for name in ("gx", "gy", "gz")]
    slabs = {-1: below_ref, 0: own_ref, 1: above_ref}
    fields = {}
    for ox in (-1, 0, 1):
        for oy in (-1, 0, 1):
            for oz in (-1, 0, 1):
                if ox and oy and oz:
                    continue
                place = (here[0] + ox, here[1] + oy, here[2] + oz)
                inside = True
                for where, size in zip(place, sizes):
                    inside = inside & (where >= 0) & (where < size)
                peer = jnp.clip(place[1], 0, sizes[1] - 1) * sizes[2] + jnp.clip(
                    place[2], 0, sizes[2] - 1
                )
                fields[ox, oy, oz] = jnp.where(inside, slabs[ox][peer], 0.0)
    out_ref[...] = jnp.zeros((8, LANES), jnp.float32)
    for d, row in enumerate(navier(fields)):
        out_ref[2 * d : 2 * d + 1, :] = row


def column_kernel(own_ref, above_ref, kept_ref, across_ref):
    gx, gy, gz = [lax.axis_index(name) for name in ("gx", "gy", "gz")]
    n_x, n_y = lax.axis_size("gx"), lax.axis_size("gy")
    here, ahead = {}, {}
    for oy in (-1, 0, 1):
        place = gy + oy
        inside = (place >= 0) & (place < n_y)
        distance = lax.rem(oy + n_y, n_y)
        here[0, oy] = jnp.where(inside, own_ref[distance], 0.0)
        here[1, oy] = jnp.where(inside & (gx + 1 < n_x), above_ref[distance], 0.0)
        ahead[-1, oy] = here[0, oy]
    for n, columns in enumerate((here, ahead)):
        kept = {(ox, oy, 0): value for (ox, oy), value in columns.items()}
        across = {}
        for (ox, oy), value in columns.items():
            if not (ox and oy):
                across[ox, oy, -1] = jnp.where(gz == 0, value, 0.0)
                across[ox, oy, 1] = jnp.where(gz == 1, value, 0.0)
        for ref, fields in ((kept_ref, kept), (across_ref, across)):
            for d, row in enumerate(navier(fields)):
                ref[2 * d + n : 2 * d + n + 1, :] = row


def collect_kernel(after_ref, *refs):
    for n, ref in enumerate(refs[:-1]):
        refs[-1][n] = ref[DISP:META, :]


def small_call(kernel, shapes, name, *operands):
    return vmem_call(kernel, [(shape, jnp.float32) for shape in shapes], name, *operands)


def ring(value, axes, distance=1):
    count = lax.axis_size(axes)
    return lax.ppermute(value, axes, [(i, (i + distance) % count) for i in range(count)])


def ring_2(value):
    nx, ny = lax.axis_size("gx"), lax.axis_size("gy")
    route = [
        (x * ny + y, (x + 1) % nx * ny + (y + 1) % ny) for x in range(nx) for y in range(ny)
    ]
    return lax.ppermute(value, ("gx", "gy"), route)


def swapped(value, axes, mask):
    return lax.ppermute(value, axes, [(i, i ^ mask) for i in range(lax.axis_size(axes))])


def local(
    displacement,
    reference_image,
    image_gradient,
    deformed_blocks,
    fractions,
    offsets,
    send_list,
    recv_slot,
):
    n_y, n_z = lax.axis_size("gy"), lax.axis_size("gz")
    peers = n_y * n_z
    cap = send_list.shape[0] // peers
    (shape_values,) = vmem_call(
        shape_kernel, [((512, LANES), jnp.bfloat16)], "shapes", cost=16 << 20, flops=1 << 33
    )
    (packed,) = small_call(
        pack_kernel,
        [(META, LANES)],
        "pack",
        shape_values,
        fractions,
        displacement,
        offsets,
        recv_slot[None],
    )
    send_rows = send_list.reshape(-1, LANES)
    mate_rows = swapped(send_rows, "gz", 1)

    def table_of(*blocks):
        shape = (VOXELS, len(blocks) * LANES)
        return vmem_call(
            table_kernel, [(shape, jnp.bfloat16)], "table", packed, mate_rows, *blocks, flops=3 << 28
        )[0]

    relative = n_z == 2 and n_y in (2, 4) and 2 * cap == LANES
    if relative:
        metas = [packed] + [ring(packed, "gy", -d) for d in range(1, n_y)]
        table = table_of(deformed_blocks, swapped(deformed_blocks, "gz", 1))
        arrived = [None] * n_y
        previous = []
        for d in ([3, 1, 2] if n_y == 4 else [1]) + [0]:
            samples = sample_call(
                functools.partial(pair_kernel, d),
                metas[d],
                table,
                send_rows,
                mate_rows,
                *previous,
            )
            arrived[d] = ring(samples, "gy", d) if d else samples
            previous = [samples]
        (column,) = small_call(collect_kernel, [(n_y, 8, LANES)], "collect", arrived[n_y - 1], *metas)
        stiff, across = small_call(
            column_kernel, [(8, LANES)] * 2, "stiffness", column, ring(column, "gx", -1)
        )
    else:
        gathered = lax.all_gather(packed, SLAB, axis=0)
        readers = LANES // cap
        table = table_of(deformed_blocks)
        samples = [
            sample_call(
                functools.partial(group_kernel, g, cap),
                gathered[g * readers : (g + 1) * readers],
                table,
                send_rows,
            )
            for g in range(peers // readers)
        ]
        outgoing = jnp.concatenate(samples, axis=0)
        arrived = [lax.all_to_all(outgoing, SLAB, split_axis=0, concat_axis=0, tiled=True)]
        slab = gathered[:, DISP:META]
        (stiff,) = small_call(
            stiffness_kernel, [(8, LANES)], "stiffness", ring(slab, "gx", 1), slab, ring(slab, "gx", -1)
        )
        across = jnp.zeros((8, LANES), jnp.float32)
    kept, sent = small_call(
        functools.partial(force_kernel, cap, relative),
        [(24, LANES)] * 2,
        "forces",
        across,
        recv_slot[:, None],
        reference_image,
        image_gradient,
        shape_values,
        *arrived,
    )
    xy, y, x, own = small_call(
        layer_kernel, [(8, LANES)] * 4, "layers", kept, ring(sent, "gz"), stiff
    )
    return small_call(
        final_kernel, [(3, LANES)], "total", own, ring_2(xy), ring(y, "gy"), ring(x, "gx")
    )[0]


def solution(mesh):
    in_specs = (
        P(None, ("gx", "gy", "gz")),
        P(("gx", "gy", "gz"), None),
        P(None, ("gx", "gy", "gz"), None),
        P(("gx", "gy", "gz"), None),
        P(None, ("gx", "gy", "gz")),
        P(None, ("gx", "gy", "gz")),
        P(("gx", "gy", "gz")),
        P(("gx", "gy", "gz")),
    )
    out_specs = P(None, ("gx", "gy", "gz"))
    return jax.shard_map(local, mesh=mesh, in_specs=in_specs, out_specs=out_specs, check_vma=False)
```

```python
import functools

import jax
import jax.numpy as jnp
from jax import lax
from jax.experimental import pallas as pl
from jax.experimental.pallas import tpu as pltpu
from jax.sharding import PartitionSpec as P

CX = 2
CY = 8
CZ = 8
LANES = CX * CY * CZ
SLAB = ("gy", "gz")

shear_modulus = 0.05
lame_first = 1.0
data_weight = 0.0625

DISP = 24
OFFS = 27
SLOT = 30
META = 32

VOXELS = 4096


def iota(shape, dim):
    return lax.broadcasted_iota(jnp.int32, shape, dim)


def shifted(planes, bits):
    for bit, count in ((2, 12), (1, 10), (0, 9)):
        step = 1 << bit
        planes = [jnp.where(bits[bit], planes[p + step], planes[p]) for p in range(count)]
    return planes


def offset_bits(offset, rows):
    wide = jnp.broadcast_to(offset, (rows, LANES))
    return [(wide & (1 << bit)) != 0 for bit in range(3)]


def shape_kernel(out_ref):
    voxel, column = iota((512, LANES), 0), iota((512, LANES), 1)

    def weight(index, upper):
        centre = (index.astype(jnp.float32) + 0.5) * 0.125
        return jnp.where(upper == 1, centre, 1.0 - centre)

    values = weight(voxel >> 6, (column >> 1) & 1) * weight((voxel >> 3) & 7, column & 1)
    values = values * weight(voxel & 7, (column >> 2) & 1)
    coarse = values.astype(jnp.bfloat16).astype(jnp.float32)
    values = jnp.where(column < 8, coarse, jnp.where(column < 16, values - coarse, 0.0))
    out_ref[...] = values.astype(jnp.bfloat16)


def pack_kernel(after_ref, fraction_ref, displacement_ref, offset_ref, slot_ref, out_ref):
    out_ref[:DISP, :] = fraction_ref[...].astype(jnp.float32)
    out_ref[DISP:OFFS, :] = displacement_ref[...]
    out_ref[OFFS:SLOT, :] = offset_ref[...].astype(jnp.float32)
    out_ref[SLOT : SLOT + 1, :] = slot_ref[...].astype(jnp.float32)
    out_ref[SLOT + 1 :, :] = jnp.zeros((META - SLOT - 1, LANES), jnp.float32)


def table_kernel(after_ref, later_ref, *refs):
    out_ref = refs[-1]
    for n, ref in enumerate(refs[:-1]):
        for start in range(0, VOXELS, 512):
            out_ref[start : start + 512, LANES * n : LANES * n + LANES] = ref[
                :, start : start + 512
            ].T


def vmem_call(kernel, shapes, name, *operands, cost=1 << 20, flops=1 << 20):
    vmem = pl.BlockSpec(memory_space=pltpu.VMEM)
    return pl.pallas_call(
        kernel,
        out_shape=[jax.ShapeDtypeStruct(shape, dtype) for shape, dtype in shapes],
        in_specs=[vmem] * len(operands),
        out_specs=[vmem] * len(shapes),
        compiler_params=pltpu.CompilerParams(vmem_limit_bytes=24 << 20),
        cost_estimate=pl.CostEstimate(flops=flops, bytes_accessed=cost, transcendentals=0),
        name=name,
    )(*operands)


def interpolated(table_ref, pick, meta, along_a, along_b, along_c):
    upper = meta[:24]
    lower = 1.0 - upper
    offsets = meta[OFFS : OFFS + 3].astype(jnp.int32)
    bits = offset_bits(offsets[0:1], 16)
    for first in range(0, 256, 16):
        starts = [256 * a + first for a in range(16)]
        rows = jnp.concatenate([table_ref[start : start + 16, :] for start in starts], axis=0)
        voxels = jnp.dot(rows, pick, preferred_element_type=jnp.float32)
        window = shifted([voxels[16 * a : 16 * a + 16] for a in range(16)], bits)
        for i in range(8):
            along_a[256 * i + first : 256 * i + first + 16, :] = (
                lower[i : i + 1] * window[i] + upper[i : i + 1] * window[i + 1]
            )
    bits = offset_bits(offsets[1:2], 16)
    for i in range(8):
        window = shifted(
            [along_a[256 * i + 16 * b : 256 * i + 16 * b + 16, :] for b in range(16)], bits
        )
        for j in range(8):
            along_b[128 * i + 16 * j : 128 * i + 16 * j + 16, :] = (
                lower[8 + j : 9 + j] * window[j] + upper[8 + j : 9 + j] * window[j + 1]
            )
    bits = offset_bits(offsets[2:3], 8)
    for i in range(8):
        window = shifted(
            [along_b[pl.ds(128 * i + c, 8, stride=16), :] for c in range(16)], bits
        )
        for k in range(8):
            along_c[pl.ds(64 * i + k, 8, stride=8), :] = (
                lower[16 + k : 17 + k] * window[k] + upper[16 + k : 17 + k] * window[k + 1]
            )
    return along_c[...].T.astype(jnp.bfloat16)


def slot_meta(meta, slots):
    wanted = meta[SLOT : SLOT + 1].astype(jnp.int32)
    return lax.dot_general(
        meta.astype(jnp.bfloat16),
        (wanted == slots).astype(jnp.bfloat16),
        (((1,), (1,)), ((), ())),
        preferred_element_type=jnp.float32,
    )


def pair_kernel(distance, meta_ref, table_ref, own_ref, mate_ref, *rest):
    out_ref, scratch = rest[-4], rest[-3:]
    gy, gz = lax.axis_index("gy"), lax.axis_index("gz")
    half = LANES // 2
    slot = iota((LANES, LANES), 0)
    slots = ((2 * gy + gz) * half) ^ slot
    meta = slot_meta(meta_ref[...], slots)
    chip = lax.rem(gy + distance, lax.axis_size("gy"))
    chip = pl.ds(chip, 1)
    own, mate = own_ref[chip, :], mate_ref[chip, :]
    first = gz == 0
    own = jnp.where(first, own, pltpu.roll(own, half, 1))
    mate = jnp.where(first, pltpu.roll(mate, half, 1), mate)
    row = jnp.where(iota((1, LANES), 1) < half, own, mate + LANES)
    pick = (iota((2 * LANES, LANES), 0) == row).astype(jnp.bfloat16)
    out_ref[...] = interpolated(table_ref, pick, meta, *scratch)


def group_kernel(group, cap, meta_ref, table_ref, send_ref, out_ref, *scratch):
    holder = lax.axis_index("gy") * lax.axis_size("gz") + lax.axis_index("gz")
    slot = iota((LANES, LANES), 0)
    meta = jnp.zeros((META, LANES), jnp.float32)
    for r in range(LANES // cap):
        slots = jnp.where(slot // cap == r, holder * cap + slot - r * cap, -1)
        meta = meta + slot_meta(meta_ref[r], slots)
    pick = (iota((LANES, LANES), 0) == send_ref[group : group + 1, :]).astype(jnp.bfloat16)
    out_ref[...] = interpolated(table_ref, pick, meta, *scratch)


def sample_call(kernel, *operands):
    vmem = pl.BlockSpec(memory_space=pltpu.VMEM)
    return pl.pallas_call(
        kernel,
        out_shape=jax.ShapeDtypeStruct((LANES, 512), jnp.bfloat16),
        in_specs=[vmem] * len(operands),
        out_specs=vmem,
        scratch_shapes=[
            pltpu.VMEM((2048, LANES), jnp.float32),
            pltpu.VMEM((1024, LANES), jnp.float32),
            pltpu.VMEM((512, LANES), jnp.float32),
        ],
        compiler_params=pltpu.CompilerParams(vmem_limit_bytes=24 << 20),
        cost_estimate=pl.CostEstimate(
            flops=4000000000, bytes_accessed=1, transcendentals=0
        ),
        name="interpolate",
    )(*operands)


def axis_of_lane(rows):
    lane = iota((rows, LANES), 1)
    return lane >> 6, (lane >> 3) & (CY - 1), lane & (CZ - 1)


def remainder(cap, chips, slot_ref, base_ref, pieces):
    total = sum(piece.shape[0] for piece in pieces)
    number = iota((LANES, total), 1)
    if chips is not None:
        n_y = lax.axis_size("gy")
        gy, gz = lax.axis_index("gy"), lax.axis_index("gz")
        order = [2 * lax.rem(gy + n_y - d, n_y) + gz for d in chips]
        lane = iota((1, LANES), 1)
        number = jnp.concatenate([(holder * cap) ^ lane for holder in order], axis=1)
    hit = (slot_ref[...] == number).astype(jnp.bfloat16)
    rows = jnp.concatenate([piece[...] for piece in pieces], axis=0)
    samples = jnp.dot(hit, rows, preferred_element_type=jnp.float32)
    return base_ref[...].astype(jnp.float32) - samples


def early_kernel(cap, chips, slot_ref, image_ref, *rest):
    rest[-1][...] = remainder(cap, chips, slot_ref, image_ref, rest[:-1])


def force_kernel(cap, chips, across_ref, slot_ref, base_ref, slope_ref, shape_ref, *rest):
    arrived, (kept_ref, sent_ref) = rest[:-2], rest[-2:]
    difference = remainder(cap, chips, slot_ref, base_ref, arrived)
    parts = []
    for d in range(3):
        weighted = slope_ref[d].astype(jnp.float32) * difference
        coarse = weighted.astype(jnp.bfloat16)
        parts += [coarse, (weighted - coarse.astype(jnp.float32)).astype(jnp.bfloat16)]
    sums = jnp.dot(
        jnp.concatenate(parts, axis=0), shape_ref[...], preferred_element_type=jnp.float32
    )
    columns = 0.0
    for d in range(3):
        both = sums[2 * LANES * d : 2 * LANES * d + LANES] + sums[2 * LANES * d + LANES : 2 * LANES * (d + 1)]
        columns = columns + (pltpu.roll(both, 16 * d, 1) if d else both)
    columns = columns.T
    _, _, at_k = axis_of_lane(8)
    for d in range(3):
        corners = columns[16 * d : 16 * d + 8] + columns[16 * d + 8 : 16 * d + 16]
        carried = pltpu.roll(corners, 4, 0)
        kept_ref[8 * d : 8 * d + 8, :] = corners + jnp.where(at_k > 0, pltpu.roll(carried, 1, 1), 0.0)
        sent_ref[8 * d : 8 * d + 8, :] = jnp.where(at_k == 0, pltpu.roll(carried, LANES - 7, 1), 0.0)
        sent_ref[8 * d + 4 : 8 * d + 6, :] = across_ref[2 * d : 2 * d + 2, :]


def layer_kernel(kept_ref, arrived_ref, stiff_ref, xy_ref, y_ref, x_ref, own_ref):
    at_i, at_j, _ = axis_of_lane(8)
    behind = lax.axis_index("gz") > 0

    def along_x(lower_half, upper_half):
        moved = pltpu.roll(upper_half, CY * CZ, 1)
        return lower_half + jnp.where(at_i > 0, moved, 0.0), jnp.where(at_i == 0, moved, 0.0)

    for d in range(3):
        part = slice(8 * d, 8 * d + 8)
        z = kept_ref[part, :] + jnp.where(behind, arrived_ref[part, :], 0.0)
        carried = pltpu.roll(z, 7, 0)
        stay = z + jnp.where(at_j > 0, pltpu.roll(carried, CZ, 1), 0.0)
        leave = jnp.where(at_j == 0, pltpu.roll(carried, LANES - CZ * (CY - 1), 1), 0.0)
        own, x = along_x(stay, pltpu.roll(stay, 6, 0))
        y, xy = along_x(leave, pltpu.roll(leave, 6, 0))
        stiff = stiff_ref[2 * d : 2 * d + 2, :] + arrived_ref[8 * d + 4 : 8 * d + 6, :]
        row = slice(d, d + 1)
        xy_ref[row, :] = xy[0:1] * data_weight
        y_ref[row, :] = y[0:1] * data_weight
        x_ref[row, :] = x[0:1] * data_weight + stiff[1:2]
        own_ref[row, :] = own[0:1] * data_weight + stiff[0:1]


def final_kernel(own_ref, y_ref, xy_ref, x_ref, out_ref):
    has_x = lax.axis_index("gx") > 0
    has_y = lax.axis_index("gy") > 0
    total = own_ref[0:3, :] + jnp.where(has_x, x_ref[0:3, :], 0.0)
    total = total + jnp.where(has_y, y_ref[0:3, :], 0.0)
    out_ref[...] = total + jnp.where(has_x & has_y, xy_ref[0:3, :], 0.0)


def navier(fields):
    at = axis_of_lane(8)
    steps = (CY * CZ, CZ, 1)
    extents = (CX, CY, CZ)

    def plus(p, q):
        return q if p is None else p if q is None else p + q

    def times(factor, p):
        return None if p is None else factor * p

    def along(axis, sign, centre, beyond):
        step, extent = steps[axis], extents[axis]
        back = step * (extent - 1)
        if sign > 0:
            inside, near, far = at[axis] < extent - 1, LANES - step, back
        else:
            inside, near, far = at[axis] > 0, step, LANES - back
        if centre is None and beyond is None:
            return None
        return jnp.where(
            inside,
            0.0 if centre is None else pltpu.roll(centre, near, 1),
            0.0 if beyond is None else pltpu.roll(beyond, far, 1),
        )

    def moved(vector, frame=(0, 0, 0), axis=2):
        if axis < 0:
            return fields.get(frame)
        sign = vector[axis]
        centre = moved(vector, frame, axis - 1)
        if sign == 0:
            return centre
        other = tuple(sign if n == axis else frame[n] for n in range(3))
        return along(axis, sign, centre, moved(vector, other, axis - 1))

    units = ((1, 0, 0), (0, 1, 0), (0, 0, 1))
    centre = fields.get((0, 0, 0))
    laplace = times(-6.0, centre)
    second = []
    for unit in units:
        both = plus(moved(unit), moved(tuple(-n for n in unit)))
        laplace = plus(laplace, both)
        second.append(plus(both, times(-2.0, centre)))
    mixed = {}
    for outer in range(3):
        for inner in range(outer + 1, 3):
            ahead = tuple(p + q for p, q in zip(units[outer], units[inner]))
            cross = tuple(p - q for p, q in zip(units[outer], units[inner]))
            aligned = plus(moved(ahead), moved(tuple(-n for n in ahead)))
            crossed = plus(moved(cross), moved(tuple(-n for n in cross)))
            mixed[outer, inner] = times(0.25, plus(aligned, times(-1.0, crossed)))
    rows = []
    for d in range(3):
        parts = [second[d]]
        for b in range(3):
            if b != d:
                part = mixed[min(b, d), max(b, d)]
                parts.append(None if part is None else pltpu.roll(part, (d - b) % 8, 0))
        total = functools.reduce(plus, parts)
        value = plus(times(shear_modulus, laplace), times(lame_first + shear_modulus, total))
        rows.append(jnp.zeros((1, LANES), jnp.float32) if value is None else -value[d : d + 1])
    return rows


def stiffness_kernel(below_ref, own_ref, above_ref, out_ref):
    here = [lax.axis_index(name) for name in ("gx", "gy", "gz")]
    sizes = [lax.axis_size(name) for name in ("gx", "gy", "gz")]
    slabs = {-1: below_ref, 0: own_ref, 1: above_ref}
    fields = {}
    for ox in (-1, 0, 1):
        for oy in (-1, 0, 1):
            for oz in (-1, 0, 1):
                if ox and oy and oz:
                    continue
                place = (here[0] + ox, here[1] + oy, here[2] + oz)
                inside = True
                for where, size in zip(place, sizes):
                    inside = inside & (where >= 0) & (where < size)
                peer = jnp.clip(place[1], 0, sizes[1] - 1) * sizes[2] + jnp.clip(
                    place[2], 0, sizes[2] - 1
                )
                fields[ox, oy, oz] = jnp.where(inside, slabs[ox][peer], 0.0)
    out_ref[...] = jnp.zeros((8, LANES), jnp.float32)
    for d, row in enumerate(navier(fields)):
        out_ref[2 * d : 2 * d + 1, :] = row


def column_kernel(own_ref, above_ref, kept_ref, across_ref):
    gx, gy, gz = [lax.axis_index(name) for name in ("gx", "gy", "gz")]
    n_x, n_y = lax.axis_size("gx"), lax.axis_size("gy")
    here, ahead = {}, {}
    for oy in (-1, 0, 1):
        place = gy + oy
        inside = (place >= 0) & (place < n_y)
        distance = lax.rem(oy + n_y, n_y)
        here[0, oy] = jnp.where(inside, own_ref[distance], 0.0)
        here[1, oy] = jnp.where(inside & (gx + 1 < n_x), above_ref[distance], 0.0)
        ahead[-1, oy] = here[0, oy]
    for n, columns in enumerate((here, ahead)):
        kept = {(ox, oy, 0): value for (ox, oy), value in columns.items()}
        across = {}
        for (ox, oy), value in columns.items():
            if not (ox and oy):
                across[ox, oy, -1] = jnp.where(gz == 0, value, 0.0)
                across[ox, oy, 1] = jnp.where(gz == 1, value, 0.0)
        for ref, fields in ((kept_ref, kept), (across_ref, across)):
            for d, row in enumerate(navier(fields)):
                ref[2 * d + n : 2 * d + n + 1, :] = row


def collect_kernel(after_ref, *refs):
    for n, ref in enumerate(refs[:-1]):
        refs[-1][n] = ref[DISP:META, :]


def small_call(kernel, shapes, name, *operands):
    return vmem_call(kernel, [(shape, jnp.float32) for shape in shapes], name, *operands)


def ring(value, axes, distance=1):
    count = lax.axis_size(axes)
    return lax.ppermute(value, axes, [(i, (i + distance) % count) for i in range(count)])


def ring_2(value):
    nx, ny = lax.axis_size("gx"), lax.axis_size("gy")
    route = [
        (x * ny + y, (x + 1) % nx * ny + (y + 1) % ny) for x in range(nx) for y in range(ny)
    ]
    return lax.ppermute(value, ("gx", "gy"), route)


def swapped(value, axes, mask):
    return lax.ppermute(value, axes, [(i, i ^ mask) for i in range(lax.axis_size(axes))])


def local(
    displacement,
    reference_image,
    image_gradient,
    deformed_blocks,
    fractions,
    offsets,
    send_list,
    recv_slot,
):
    n_y, n_z = lax.axis_size("gy"), lax.axis_size("gz")
    peers = n_y * n_z
    cap = send_list.shape[0] // peers
    (shape_values,) = vmem_call(
        shape_kernel, [((512, LANES), jnp.bfloat16)], "shapes", cost=16 << 20, flops=1 << 33
    )
    (packed,) = small_call(
        pack_kernel,
        [(META, LANES)],
        "pack",
        shape_values,
        fractions,
        displacement,
        offsets,
        recv_slot[None],
    )
    send_rows = send_list.reshape(-1, LANES)
    mate_rows = swapped(send_rows, "gz", 1)

    def table_of(*blocks):
        shape = (VOXELS, len(blocks) * LANES)
        return vmem_call(
            table_kernel, [(shape, jnp.bfloat16)], "table", packed, mate_rows, *blocks, flops=3 << 28
        )[0]

    relative = n_z == 2 and n_y in (2, 4) and 2 * cap == LANES
    if relative:
        metas = [packed] + [ring(packed, "gy", -d) for d in range(1, n_y)]
        table = table_of(deformed_blocks, swapped(deformed_blocks, "gz", 1))
        arrived = [None] * n_y
        previous = []
        order = [3, 2, 1] if n_y == 4 else [1]
        for d in order + [0]:
            samples = sample_call(
                functools.partial(pair_kernel, d),
                metas[d],
                table,
                send_rows,
                mate_rows,
                *previous,
            )
            arrived[d] = ring(samples, "gy", d) if d else samples
            previous = [samples]
        (column,) = small_call(collect_kernel, [(n_y, 8, LANES)], "collect", arrived[n_y - 1], *metas)
        stiff, across = small_call(
            column_kernel, [(8, LANES)] * 2, "stiffness", column, ring(column, "gx", -1)
        )
    else:
        gathered = lax.all_gather(packed, SLAB, axis=0)
        readers = LANES // cap
        table = table_of(deformed_blocks)
        samples = [
            sample_call(
                functools.partial(group_kernel, g, cap),
                gathered[g * readers : (g + 1) * readers],
                table,
                send_rows,
            )
            for g in range(peers // readers)
        ]
        outgoing = jnp.concatenate(samples, axis=0)
        arrived = [lax.all_to_all(outgoing, SLAB, split_axis=0, concat_axis=0, tiled=True)]
        slab = gathered[:, DISP:META]
        (stiff,) = small_call(
            stiffness_kernel, [(8, LANES)], "stiffness", ring(slab, "gx", 1), slab, ring(slab, "gx", -1)
        )
        across = jnp.zeros((8, LANES), jnp.float32)
    base, chips = reference_image, None
    if relative:
        chips = (0, order[0])[: n_y - 1]
        (base,) = small_call(
            functools.partial(early_kernel, cap, chips),
            [(LANES, 512)],
            "early",
            recv_slot[:, None],
            base,
            *[arrived[d] for d in chips],
        )
        chips = tuple(order[1:]) or (order[0],)
        arrived = [arrived[d] for d in chips]
    kept, sent = small_call(
        functools.partial(force_kernel, cap, chips),
        [(24, LANES)] * 2,
        "forces",
        across,
        recv_slot[:, None],
        base,
        image_gradient,
        shape_values,
        *arrived,
    )
    xy, y, x, own = small_call(
        layer_kernel, [(8, LANES)] * 4, "layers", kept, ring(sent, "gz"), stiff
    )
    return small_call(
        final_kernel, [(3, LANES)], "total", own, ring(y, "gy"), ring_2(xy), ring(x, "gx")
    )[0]


def solution(mesh):
    in_specs = (
        P(None, ("gx", "gy", "gz")),
        P(("gx", "gy", "gz"), None),
        P(None, ("gx", "gy", "gz"), None),
        P(("gx", "gy", "gz"), None),
        P(None, ("gx", "gy", "gz")),
        P(None, ("gx", "gy", "gz")),
        P(("gx", "gy", "gz")),
        P(("gx", "gy", "gz")),
    )
    out_specs = P(None, ("gx", "gy", "gz"))
    return jax.shard_map(local, mesh=mesh, in_specs=in_specs, out_specs=out_specs, check_vma=False)
```

```python
import functools

import jax
import jax.numpy as jnp
from jax import lax
from jax.experimental import pallas as pl
from jax.experimental.pallas import tpu as pltpu
from jax.sharding import PartitionSpec as P

CX = 2
CY = 8
CZ = 8
LANES = CX * CY * CZ
SLAB = ("gy", "gz")

shear_modulus = 0.05
lame_first = 1.0
data_weight = 0.0625

DISP = 24
OFFS = 27
SLOT = 30
META = 32

VOXELS = 4096
SENT = 24


def iota(shape, dim):
    return lax.broadcasted_iota(jnp.int32, shape, dim)


def shifted(planes, bits):
    for bit, count in ((2, 12), (1, 10), (0, 9)):
        step = 1 << bit
        planes = [jnp.where(bits[bit], planes[p + step], planes[p]) for p in range(count)]
    return planes


def offset_bits(offset, rows):
    wide = jnp.broadcast_to(offset, (rows, LANES))
    return [(wide & (1 << bit)) != 0 for bit in range(3)]


def shape_kernel(out_ref):
    voxel, column = iota((512, LANES), 0), iota((512, LANES), 1)

    def weight(index, upper):
        centre = (index.astype(jnp.float32) + 0.5) * 0.125
        return jnp.where(upper == 1, centre, 1.0 - centre)

    values = weight(voxel >> 6, (column >> 1) & 1) * weight((voxel >> 3) & 7, column & 1)
    values = values * weight(voxel & 7, (column >> 2) & 1)
    coarse = values.astype(jnp.bfloat16).astype(jnp.float32)
    values = jnp.where(column < 8, coarse, jnp.where(column < 16, values - coarse, 0.0))
    out_ref[...] = values.astype(jnp.bfloat16)


def pack_kernel(after_ref, fraction_ref, displacement_ref, offset_ref, slot_ref, out_ref):
    out_ref[:DISP, :] = fraction_ref[...].astype(jnp.float32)
    out_ref[DISP:OFFS, :] = displacement_ref[...]
    out_ref[OFFS:SLOT, :] = offset_ref[...].astype(jnp.float32)
    out_ref[SLOT : SLOT + 1, :] = slot_ref[...].astype(jnp.float32)
    out_ref[SLOT + 1 :, :] = jnp.zeros((META - SLOT - 1, LANES), jnp.float32)


def table_kernel(after_ref, later_ref, *refs):
    out_ref = refs[-1]
    for n, ref in enumerate(refs[:-1]):
        for start in range(0, VOXELS, 512):
            out_ref[start : start + 512, LANES * n : LANES * n + LANES] = ref[
                :, start : start + 512
            ].T


def vmem_call(kernel, shapes, name, *operands, cost=1 << 20, flops=1 << 20):
    vmem = pl.BlockSpec(memory_space=pltpu.VMEM)
    return pl.pallas_call(
        kernel,
        out_shape=[jax.ShapeDtypeStruct(shape, dtype) for shape, dtype in shapes],
        in_specs=[vmem] * len(operands),
        out_specs=[vmem] * len(shapes),
        compiler_params=pltpu.CompilerParams(vmem_limit_bytes=24 << 20),
        cost_estimate=pl.CostEstimate(flops=flops, bytes_accessed=cost, transcendentals=0),
        name=name,
    )(*operands)


def interpolated(table_ref, pick, meta, along_a, along_b, along_c):
    upper = meta[:24]
    lower = 1.0 - upper
    offsets = meta[OFFS : OFFS + 3].astype(jnp.int32)
    bits = offset_bits(offsets[0:1], 16)
    for first in range(0, 256, 16):
        starts = [256 * a + first for a in range(16)]
        rows = jnp.concatenate([table_ref[start : start + 16, :] for start in starts], axis=0)
        voxels = jnp.dot(rows, pick, preferred_element_type=jnp.float32)
        window = shifted([voxels[16 * a : 16 * a + 16] for a in range(16)], bits)
        for i in range(8):
            along_a[256 * i + first : 256 * i + first + 16, :] = (
                lower[i : i + 1] * window[i] + upper[i : i + 1] * window[i + 1]
            )
    bits = offset_bits(offsets[1:2], 16)
    for i in range(8):
        window = shifted(
            [along_a[256 * i + 16 * b : 256 * i + 16 * b + 16, :] for b in range(16)], bits
        )
        for j in range(8):
            along_b[128 * i + 16 * j : 128 * i + 16 * j + 16, :] = (
                lower[8 + j : 9 + j] * window[j] + upper[8 + j : 9 + j] * window[j + 1]
            )
    bits = offset_bits(offsets[2:3], 8)
    for i in range(8):
        window = shifted(
            [along_b[pl.ds(128 * i + c, 8, stride=16), :] for c in range(16)], bits
        )
        for k in range(8):
            along_c[pl.ds(64 * i + k, 8, stride=8), :] = (
                lower[16 + k : 17 + k] * window[k] + upper[16 + k : 17 + k] * window[k + 1]
            )
    return along_c[...].T.astype(jnp.bfloat16)


def slot_meta(meta, slots):
    wanted = meta[SLOT : SLOT + 1].astype(jnp.int32)
    return lax.dot_general(
        meta.astype(jnp.bfloat16),
        (wanted == slots).astype(jnp.bfloat16),
        (((1,), (1,)), ((), ())),
        preferred_element_type=jnp.float32,
    )


def pair_kernel(distance, meta_ref, table_ref, own_ref, mate_ref, *rest):
    out_ref, scratch = rest[-4], rest[-3:]
    gy, gz = lax.axis_index("gy"), lax.axis_index("gz")
    half = LANES // 2
    slot = iota((LANES, LANES), 0)
    slots = ((2 * gy + gz) * half) ^ slot
    meta = slot_meta(meta_ref[...], slots)
    chip = lax.rem(gy + distance, lax.axis_size("gy"))
    chip = pl.ds(chip, 1)
    own, mate = own_ref[chip, :], mate_ref[chip, :]
    first = gz == 0
    own = jnp.where(first, own, pltpu.roll(own, half, 1))
    mate = jnp.where(first, pltpu.roll(mate, half, 1), mate)
    row = jnp.where(iota((1, LANES), 1) < half, own, mate + LANES)
    pick = (iota((2 * LANES, LANES), 0) == row).astype(jnp.bfloat16)
    out_ref[...] = interpolated(table_ref, pick, meta, *scratch)


def group_kernel(group, cap, meta_ref, table_ref, send_ref, out_ref, *scratch):
    holder = lax.axis_index("gy") * lax.axis_size("gz") + lax.axis_index("gz")
    slot = iota((LANES, LANES), 0)
    meta = jnp.zeros((META, LANES), jnp.float32)
    for r in range(LANES // cap):
        slots = jnp.where(slot // cap == r, holder * cap + slot - r * cap, -1)
        meta = meta + slot_meta(meta_ref[r], slots)
    pick = (iota((LANES, LANES), 0) == send_ref[group : group + 1, :]).astype(jnp.bfloat16)
    out_ref[...] = interpolated(table_ref, pick, meta, *scratch)


def sample_call(kernel, *operands):
    vmem = pl.BlockSpec(memory_space=pltpu.VMEM)
    return pl.pallas_call(
        kernel,
        out_shape=jax.ShapeDtypeStruct((LANES, 512), jnp.bfloat16),
        in_specs=[vmem] * len(operands),
        out_specs=vmem,
        scratch_shapes=[
            pltpu.VMEM((2048, LANES), jnp.float32),
            pltpu.VMEM((1024, LANES), jnp.float32),
            pltpu.VMEM((512, LANES), jnp.float32),
        ],
        compiler_params=pltpu.CompilerParams(vmem_limit_bytes=24 << 20),
        cost_estimate=pl.CostEstimate(
            flops=4000000000, bytes_accessed=1, transcendentals=0
        ),
        name="interpolate",
    )(*operands)


def axis_of_lane(rows):
    lane = iota((rows, LANES), 1)
    return lane >> 6, (lane >> 3) & (CY - 1), lane & (CZ - 1)


def remainder(cap, chips, slot_ref, base_ref, pieces):
    total = sum(piece.shape[0] for piece in pieces)
    number = iota((LANES, total), 1)
    if chips is not None:
        n_y = lax.axis_size("gy")
        gy, gz = lax.axis_index("gy"), lax.axis_index("gz")
        order = [2 * lax.rem(gy + n_y - d, n_y) + gz for d in chips]
        lane = iota((1, LANES), 1)
        number = jnp.concatenate([(holder * cap) ^ lane for holder in order], axis=1)
    hit = (slot_ref[...] == number).astype(jnp.bfloat16)
    rows = jnp.concatenate([piece[...] for piece in pieces], axis=0)
    samples = jnp.dot(hit, rows, preferred_element_type=jnp.float32)
    return base_ref[...].astype(jnp.float32) - samples


def early_kernel(cap, chips, slot_ref, image_ref, *rest):
    rest[-1][...] = remainder(cap, chips, slot_ref, image_ref, rest[:-1])


def force_kernel(cap, chips, across_ref, slot_ref, base_ref, slope_ref, shape_ref, *rest):
    arrived, out_ref = rest[:-1], rest[-1]
    difference = remainder(cap, chips, slot_ref, base_ref, arrived)
    parts = []
    for d in range(3):
        weighted = slope_ref[d].astype(jnp.float32) * difference
        coarse = weighted.astype(jnp.bfloat16)
        parts += [coarse, (weighted - coarse.astype(jnp.float32)).astype(jnp.bfloat16)]
    sums = jnp.dot(
        jnp.concatenate(parts, axis=0), shape_ref[...], preferred_element_type=jnp.float32
    )
    columns = 0.0
    for d in range(3):
        both = sums[2 * LANES * d : 2 * LANES * d + LANES] + sums[2 * LANES * d + LANES : 2 * LANES * (d + 1)]
        columns = columns + (pltpu.roll(both, 16 * d, 1) if d else both)
    columns = columns.T
    _, _, at_k = axis_of_lane(8)
    for d in range(3):
        corners = columns[16 * d : 16 * d + 8] + columns[16 * d + 8 : 16 * d + 16]
        carried = pltpu.roll(corners, 4, 0)
        kept, sent = 8 * d, SENT + 8 * d
        out_ref[kept : kept + 8, :] = corners + jnp.where(at_k > 0, pltpu.roll(carried, 1, 1), 0.0)
        out_ref[sent : sent + 8, :] = jnp.where(at_k == 0, pltpu.roll(carried, LANES - 7, 1), 0.0)
        out_ref[sent + 4 : sent + 6, :] = across_ref[2 * d : 2 * d + 2, :]


def layers(d, z):
    at_i, at_j, _ = axis_of_lane(8)

    def along_x(lower_half, upper_half):
        moved = pltpu.roll(upper_half, CY * CZ, 1)
        return lower_half + jnp.where(at_i > 0, moved, 0.0), jnp.where(at_i == 0, moved, 0.0)

    carried = pltpu.roll(z, 7, 0)
    stay = z + jnp.where(at_j > 0, pltpu.roll(carried, CZ, 1), 0.0)
    leave = jnp.where(at_j == 0, pltpu.roll(carried, LANES - CZ * (CY - 1), 1), 0.0)
    own, x = along_x(stay, pltpu.roll(stay, 6, 0))
    y, xy = along_x(leave, pltpu.roll(leave, 6, 0))
    return [value[0:1] * data_weight for value in (own, x, y, xy)]


def layer_kernel(kept_ref, arrived_ref, stiff_ref, xy_ref, y_ref, x_ref, own_ref):
    behind = lax.axis_index("gz") > 0
    for d in range(3):
        part, sent = slice(8 * d, 8 * d + 8), slice(SENT + 8 * d, SENT + 8 * d + 8)
        z = kept_ref[part, :] + jnp.where(behind, arrived_ref[sent, :], 0.0)
        own, x, y, xy = layers(d, z)
        stiff = stiff_ref[2 * d : 2 * d + 2, :]
        row = slice(d, d + 1)
        xy_ref[row, :] = xy
        y_ref[row, :] = y
        x_ref[row, :] = x + stiff[1:2]
        own_ref[row, :] = own + stiff[0:1]


def chip_kernel(here_ref, mate_ref, stiff_ref, turn_ref, x_ref, own_ref):
    first = lax.axis_index("gz") == 0
    turn_ref[...] = jnp.zeros((8, LANES), jnp.float32)
    for d in range(3):
        part, sent = slice(8 * d, 8 * d + 8), slice(SENT + 8 * d, SENT + 8 * d + 8)
        z = here_ref[part, :] + jnp.where(first, 0.0, mate_ref[sent, :])
        own, x, y, xy = layers(d, z)
        row = slice(d, d + 1)
        turn_ref[row, :] = jnp.where(first, y, xy)
        stiff = stiff_ref[2 * d : 2 * d + 2, :] + mate_ref[SENT + 8 * d + 4 : SENT + 8 * d + 6, :]
        x_ref[row, :] = x + stiff[1:2]
        own_ref[row, :] = own + stiff[0:1]
        z = mate_ref[part, :] + jnp.where(first, here_ref[sent, :], 0.0)
        _, _, y, xy = layers(d, z)
        turn_ref[d + 3 : d + 4, :] = jnp.where(first, y, xy)


def chip_total_kernel(own_ref, turned_ref, mate_ref, x_ref, out_ref):
    has_x, has_y = lax.axis_index("gx") > 0, lax.axis_index("gy") > 0
    first = lax.axis_index("gz") == 0
    total = own_ref[0:3, :] + jnp.where(has_x, x_ref[0:3, :], 0.0)
    has = has_y & (first | has_x)
    total = total + jnp.where(has, turned_ref[0:3, :], 0.0)
    has = has_y & (jnp.logical_not(first) | has_x)
    out_ref[...] = total + jnp.where(has, mate_ref[3:6, :], 0.0)


def final_kernel(own_ref, y_ref, xy_ref, x_ref, out_ref):
    has_x = lax.axis_index("gx") > 0
    has_y = lax.axis_index("gy") > 0
    total = own_ref[0:3, :] + jnp.where(has_x, x_ref[0:3, :], 0.0)
    total = total + jnp.where(has_y, y_ref[0:3, :], 0.0)
    out_ref[...] = total + jnp.where(has_x & has_y, xy_ref[0:3, :], 0.0)


def navier(fields):
    at = axis_of_lane(8)
    steps = (CY * CZ, CZ, 1)
    extents = (CX, CY, CZ)

    def plus(p, q):
        return q if p is None else p if q is None else p + q

    def times(factor, p):
        return None if p is None else factor * p

    def along(axis, sign, centre, beyond):
        step, extent = steps[axis], extents[axis]
        back = step * (extent - 1)
        if sign > 0:
            inside, near, far = at[axis] < extent - 1, LANES - step, back
        else:
            inside, near, far = at[axis] > 0, step, LANES - back
        if centre is None and beyond is None:
            return None
        return jnp.where(
            inside,
            0.0 if centre is None else pltpu.roll(centre, near, 1),
            0.0 if beyond is None else pltpu.roll(beyond, far, 1),
        )

    def moved(vector, frame=(0, 0, 0), axis=2):
        if axis < 0:
            return fields.get(frame)
        sign = vector[axis]
        centre = moved(vector, frame, axis - 1)
        if sign == 0:
            return centre
        other = tuple(sign if n == axis else frame[n] for n in range(3))
        return along(axis, sign, centre, moved(vector, other, axis - 1))

    units = ((1, 0, 0), (0, 1, 0), (0, 0, 1))
    centre = fields.get((0, 0, 0))
    laplace = times(-6.0, centre)
    second = []
    for unit in units:
        both = plus(moved(unit), moved(tuple(-n for n in unit)))
        laplace = plus(laplace, both)
        second.append(plus(both, times(-2.0, centre)))
    mixed = {}
    for outer in range(3):
        for inner in range(outer + 1, 3):
            ahead = tuple(p + q for p, q in zip(units[outer], units[inner]))
            cross = tuple(p - q for p, q in zip(units[outer], units[inner]))
            aligned = plus(moved(ahead), moved(tuple(-n for n in ahead)))
            crossed = plus(moved(cross), moved(tuple(-n for n in cross)))
            mixed[outer, inner] = times(0.25, plus(aligned, times(-1.0, crossed)))
    rows = []
    for d in range(3):
        parts = [second[d]]
        for b in range(3):
            if b != d:
                part = mixed[min(b, d), max(b, d)]
                parts.append(None if part is None else pltpu.roll(part, (d - b) % 8, 0))
        total = functools.reduce(plus, parts)
        value = plus(times(shear_modulus, laplace), times(lame_first + shear_modulus, total))
        rows.append(jnp.zeros((1, LANES), jnp.float32) if value is None else -value[d : d + 1])
    return rows


def stiffness_kernel(below_ref, own_ref, above_ref, out_ref):
    here = [lax.axis_index(name) for name in ("gx", "gy", "gz")]
    sizes = [lax.axis_size(name) for name in ("gx", "gy", "gz")]
    slabs = {-1: below_ref, 0: own_ref, 1: above_ref}
    fields = {}
    for ox in (-1, 0, 1):
        for oy in (-1, 0, 1):
            for oz in (-1, 0, 1):
                if ox and oy and oz:
                    continue
                place = (here[0] + ox, here[1] + oy, here[2] + oz)
                inside = True
                for where, size in zip(place, sizes):
                    inside = inside & (where >= 0) & (where < size)
                peer = jnp.clip(place[1], 0, sizes[1] - 1) * sizes[2] + jnp.clip(
                    place[2], 0, sizes[2] - 1
                )
                fields[ox, oy, oz] = jnp.where(inside, slabs[ox][peer], 0.0)
    out_ref[...] = jnp.zeros((8, LANES), jnp.float32)
    for d, row in enumerate(navier(fields)):
        out_ref[2 * d : 2 * d + 1, :] = row


def column_kernel(own_ref, above_ref, kept_ref, across_ref):
    gx, gy, gz = [lax.axis_index(name) for name in ("gx", "gy", "gz")]
    n_x, n_y = lax.axis_size("gx"), lax.axis_size("gy")
    here, ahead = {}, {}
    for oy in (-1, 0, 1):
        place = gy + oy
        inside = (place >= 0) & (place < n_y)
        distance = lax.rem(oy + n_y, n_y)
        here[0, oy] = jnp.where(inside, own_ref[distance], 0.0)
        here[1, oy] = jnp.where(inside & (gx + 1 < n_x), above_ref[distance], 0.0)
        ahead[-1, oy] = here[0, oy]
    for n, columns in enumerate((here, ahead)):
        kept = {(ox, oy, 0): value for (ox, oy), value in columns.items()}
        across = {}
        for (ox, oy), value in columns.items():
            if not (ox and oy):
                across[ox, oy, -1] = jnp.where(gz == 0, value, 0.0)
                across[ox, oy, 1] = jnp.where(gz == 1, value, 0.0)
        for ref, fields in ((kept_ref, kept), (across_ref, across)):
            for d, row in enumerate(navier(fields)):
                ref[2 * d + n : 2 * d + n + 1, :] = row


def collect_kernel(after_ref, *refs):
    for n, ref in enumerate(refs[:-1]):
        refs[-1][n] = ref[DISP:META, :]


def small_call(kernel, shapes, name, *operands):
    return vmem_call(kernel, [(shape, jnp.float32) for shape in shapes], name, *operands)


def ring(value, axes, distance=1):
    count = lax.axis_size(axes)
    return lax.ppermute(value, axes, [(i, (i + distance) % count) for i in range(count)])


def ring_2(value):
    nx, ny = lax.axis_size("gx"), lax.axis_size("gy")
    route = [
        (x * ny + y, (x + 1) % nx * ny + (y + 1) % ny) for x in range(nx) for y in range(ny)
    ]
    return lax.ppermute(value, ("gx", "gy"), route)


def turned_ring(value):
    nx, ny = lax.axis_size("gx"), lax.axis_size("gy")
    route = [
        ((x * ny + y) * 2 + core, ((x + core) % nx * ny + (y + 1) % ny) * 2 + core)
        for x in range(nx)
        for y in range(ny)
        for core in range(2)
    ]
    return lax.ppermute(value, ("gx", "gy", "gz"), route)


def swapped(value, axes, mask):
    return lax.ppermute(value, axes, [(i, i ^ mask) for i in range(lax.axis_size(axes))])


def local(
    displacement,
    reference_image,
    image_gradient,
    deformed_blocks,
    fractions,
    offsets,
    send_list,
    recv_slot,
):
    n_y, n_z = lax.axis_size("gy"), lax.axis_size("gz")
    peers = n_y * n_z
    cap = send_list.shape[0] // peers
    (shape_values,) = vmem_call(
        shape_kernel, [((512, LANES), jnp.bfloat16)], "shapes", cost=16 << 20, flops=1 << 33
    )
    (packed,) = small_call(
        pack_kernel,
        [(META, LANES)],
        "pack",
        shape_values,
        fractions,
        displacement,
        offsets,
        recv_slot[None],
    )
    send_rows = send_list.reshape(-1, LANES)
    mate_rows = swapped(send_rows, "gz", 1)

    def table_of(*blocks):
        shape = (VOXELS, len(blocks) * LANES)
        return vmem_call(
            table_kernel, [(shape, jnp.bfloat16)], "table", packed, mate_rows, *blocks, flops=3 << 28
        )[0]

    relative = n_z == 2 and n_y in (2, 4) and 2 * cap == LANES
    if relative:
        metas = [packed] + [ring(packed, "gy", -d) for d in range(1, n_y)]
        table = table_of(deformed_blocks, swapped(deformed_blocks, "gz", 1))
        arrived = [None] * n_y
        previous = []
        order = [3, 2, 1] if n_y == 4 else [1]
        for d in order + [0]:
            samples = sample_call(
                functools.partial(pair_kernel, d),
                metas[d],
                table,
                send_rows,
                mate_rows,
                *previous,
            )
            arrived[d] = ring(samples, "gy", d) if d else samples
            previous = [samples]
        (column,) = small_call(collect_kernel, [(n_y, 8, LANES)], "collect", arrived[n_y - 1], *metas)
        stiff, across = small_call(
            column_kernel, [(8, LANES)] * 2, "stiffness", column, ring(column, "gx", -1)
        )
    else:
        gathered = lax.all_gather(packed, SLAB, axis=0)
        readers = LANES // cap
        table = table_of(deformed_blocks)
        samples = [
            sample_call(
                functools.partial(group_kernel, g, cap),
                gathered[g * readers : (g + 1) * readers],
                table,
                send_rows,
            )
            for g in range(peers // readers)
        ]
        outgoing = jnp.concatenate(samples, axis=0)
        arrived = [lax.all_to_all(outgoing, SLAB, split_axis=0, concat_axis=0, tiled=True)]
        slab = gathered[:, DISP:META]
        (stiff,) = small_call(
            stiffness_kernel, [(8, LANES)], "stiffness", ring(slab, "gx", 1), slab, ring(slab, "gx", -1)
        )
        across = jnp.zeros((8, LANES), jnp.float32)
    base, chips = reference_image, None
    if relative:
        chips = (0, order[0])[: n_y - 1]
        (base,) = small_call(
            functools.partial(early_kernel, cap, chips),
            [(LANES, 512)],
            "early",
            recv_slot[:, None],
            base,
            *[arrived[d] for d in chips],
        )
        chips = tuple(order[1:]) or (order[0],)
        arrived = [arrived[d] for d in chips]
    (force,) = small_call(
        functools.partial(force_kernel, cap, chips),
        [(2 * SENT, LANES)],
        "forces",
        across,
        recv_slot[:, None],
        base,
        image_gradient,
        shape_values,
        *arrived,
    )
    came = ring(force, "gz")
    if relative:
        turn, x, own = small_call(chip_kernel, [(8, LANES)] * 3, "layers", force, came, stiff)
        turned = turned_ring(turn)
        return small_call(
            chip_total_kernel, [(3, LANES)], "total", own, turned, ring(turned, "gz"), ring(x, "gx")
        )[0]
    xy, y, x, own = small_call(layer_kernel, [(8, LANES)] * 4, "layers", force, came, stiff)
    return small_call(
        final_kernel, [(3, LANES)], "total", own, ring(y, "gy"), ring_2(xy), ring(x, "gx")
    )[0]


def solution(mesh):
    in_specs = (
        P(None, ("gx", "gy", "gz")),
        P(("gx", "gy", "gz"), None),
        P(None, ("gx", "gy", "gz"), None),
        P(("gx", "gy", "gz"), None),
        P(None, ("gx", "gy", "gz")),
        P(None, ("gx", "gy", "gz")),
        P(("gx", "gy", "gz")),
        P(("gx", "gy", "gz")),
    )
    out_specs = P(None, ("gx", "gy", "gz"))
    return jax.shard_map(local, mesh=mesh, in_specs=in_specs, out_specs=out_specs, check_vma=False)
```

```python
import functools

import jax
import jax.numpy as jnp
from jax import lax
from jax.experimental import pallas as pl
from jax.experimental.pallas import tpu as pltpu
from jax.sharding import PartitionSpec as P

CX = 2
CY = 8
CZ = 8
LANES = CX * CY * CZ
SLAB = ("gy", "gz")

shear_modulus = 0.05
lame_first = 1.0
data_weight = 0.0625

DISP = 24
OFFS = 27
SLOT = 30
META = 32

VOXELS = 4096
SENT = 24


def iota(shape, dim):
    return lax.broadcasted_iota(jnp.int32, shape, dim)


def shifted(planes, bits):
    for bit, count in ((2, 12), (1, 10), (0, 9)):
        step = 1 << bit
        planes = [jnp.where(bits[bit], planes[p + step], planes[p]) for p in range(count)]
    return planes


def offset_bits(offset, rows):
    wide = jnp.broadcast_to(offset, (rows, LANES))
    return [(wide & (1 << bit)) != 0 for bit in range(3)]


def shape_kernel(out_ref):
    voxel, column = iota((512, LANES), 0), iota((512, LANES), 1)

    def weight(index, upper):
        centre = (index.astype(jnp.float32) + 0.5) * 0.125
        return jnp.where(upper == 1, centre, 1.0 - centre)

    values = weight(voxel >> 6, (column >> 1) & 1) * weight((voxel >> 3) & 7, column & 1)
    values = values * weight(voxel & 7, (column >> 2) & 1)
    coarse = values.astype(jnp.bfloat16).astype(jnp.float32)
    values = jnp.where(column < 8, coarse, jnp.where(column < 16, values - coarse, 0.0))
    out_ref[...] = values.astype(jnp.bfloat16)


def pack_kernel(after_ref, fraction_ref, displacement_ref, offset_ref, slot_ref, out_ref):
    out_ref[:DISP, :] = fraction_ref[...].astype(jnp.float32)
    out_ref[DISP:OFFS, :] = displacement_ref[...]
    out_ref[OFFS:SLOT, :] = offset_ref[...].astype(jnp.float32)
    out_ref[SLOT : SLOT + 1, :] = slot_ref[...].astype(jnp.float32)
    out_ref[SLOT + 1 :, :] = jnp.zeros((META - SLOT - 1, LANES), jnp.float32)


def table_kernel(after_ref, later_ref, *refs):
    out_ref = refs[-1]
    for n, ref in enumerate(refs[:-1]):
        for start in range(0, VOXELS, 512):
            out_ref[start : start + 512, LANES * n : LANES * n + LANES] = ref[
                :, start : start + 512
            ].T


def vmem_call(kernel, shapes, name, *operands, cost=1 << 20, flops=1 << 20):
    vmem = pl.BlockSpec(memory_space=pltpu.VMEM)
    return pl.pallas_call(
        kernel,
        out_shape=[jax.ShapeDtypeStruct(shape, dtype) for shape, dtype in shapes],
        in_specs=[vmem] * len(operands),
        out_specs=[vmem] * len(shapes),
        compiler_params=pltpu.CompilerParams(vmem_limit_bytes=24 << 20),
        cost_estimate=pl.CostEstimate(flops=flops, bytes_accessed=cost, transcendentals=0),
        name=name,
    )(*operands)


def interpolated(table_ref, pick, meta, along_a, along_b, along_c):
    upper = meta[:24]
    lower = 1.0 - upper
    offsets = meta[OFFS : OFFS + 3].astype(jnp.int32)
    bits = offset_bits(offsets[0:1], 16)
    for first in range(0, 256, 16):
        starts = [256 * a + first for a in range(16)]
        rows = jnp.concatenate([table_ref[start : start + 16, :] for start in starts], axis=0)
        voxels = jnp.dot(rows, pick, preferred_element_type=jnp.float32)
        window = shifted([voxels[16 * a : 16 * a + 16] for a in range(16)], bits)
        for i in range(8):
            along_a[256 * i + first : 256 * i + first + 16, :] = (
                lower[i : i + 1] * window[i] + upper[i : i + 1] * window[i + 1]
            )
    bits = offset_bits(offsets[1:2], 16)
    for i in range(8):
        window = shifted(
            [along_a[256 * i + 16 * b : 256 * i + 16 * b + 16, :] for b in range(16)], bits
        )
        for j in range(8):
            along_b[128 * i + 16 * j : 128 * i + 16 * j + 16, :] = (
                lower[8 + j : 9 + j] * window[j] + upper[8 + j : 9 + j] * window[j + 1]
            )
    bits = offset_bits(offsets[2:3], 8)
    for i in range(8):
        window = shifted(
            [along_b[pl.ds(128 * i + c, 8, stride=16), :] for c in range(16)], bits
        )
        for k in range(8):
            along_c[pl.ds(64 * i + k, 8, stride=8), :] = (
                lower[16 + k : 17 + k] * window[k] + upper[16 + k : 17 + k] * window[k + 1]
            )
    return along_c[...].T.astype(jnp.bfloat16)


def slot_meta(meta, slots):
    wanted = meta[SLOT : SLOT + 1].astype(jnp.int32)
    return lax.dot_general(
        meta.astype(jnp.bfloat16),
        (wanted == slots).astype(jnp.bfloat16),
        (((1,), (1,)), ((), ())),
        preferred_element_type=jnp.float32,
    )


def pair_kernel(distance, meta_ref, table_ref, own_ref, mate_ref, *rest):
    out_ref, scratch = rest[-4], rest[-3:]
    gy, gz = lax.axis_index("gy"), lax.axis_index("gz")
    half = LANES // 2
    slot = iota((LANES, LANES), 0)
    slots = ((2 * gy + gz) * half) ^ slot
    meta = slot_meta(meta_ref[...], slots)
    chip = lax.rem(gy + distance, lax.axis_size("gy"))
    chip = pl.ds(chip, 1)
    own, mate = own_ref[chip, :], mate_ref[chip, :]
    first = gz == 0
    own = jnp.where(first, own, pltpu.roll(own, half, 1))
    mate = jnp.where(first, pltpu.roll(mate, half, 1), mate)
    row = jnp.where(iota((1, LANES), 1) < half, own, mate + LANES)
    pick = (iota((2 * LANES, LANES), 0) == row).astype(jnp.bfloat16)
    out_ref[...] = interpolated(table_ref, pick, meta, *scratch)


def group_kernel(group, cap, meta_ref, table_ref, send_ref, out_ref, *scratch):
    holder = lax.axis_index("gy") * lax.axis_size("gz") + lax.axis_index("gz")
    slot = iota((LANES, LANES), 0)
    meta = jnp.zeros((META, LANES), jnp.float32)
    for r in range(LANES // cap):
        slots = jnp.where(slot // cap == r, holder * cap + slot - r * cap, -1)
        meta = meta + slot_meta(meta_ref[r], slots)
    pick = (iota((LANES, LANES), 0) == send_ref[group : group + 1, :]).astype(jnp.bfloat16)
    out_ref[...] = interpolated(table_ref, pick, meta, *scratch)


def sample_call(kernel, *operands):
    vmem = pl.BlockSpec(memory_space=pltpu.VMEM)
    return pl.pallas_call(
        kernel,
        out_shape=jax.ShapeDtypeStruct((LANES, 512), jnp.bfloat16),
        in_specs=[vmem] * len(operands),
        out_specs=vmem,
        scratch_shapes=[
            pltpu.VMEM((2048, LANES), jnp.float32),
            pltpu.VMEM((1024, LANES), jnp.float32),
            pltpu.VMEM((512, LANES), jnp.float32),
        ],
        compiler_params=pltpu.CompilerParams(vmem_limit_bytes=24 << 20),
        cost_estimate=pl.CostEstimate(
            flops=4000000000, bytes_accessed=1, transcendentals=0
        ),
        name="interpolate",
    )(*operands)


def axis_of_lane(rows):
    lane = iota((rows, LANES), 1)
    return lane >> 6, (lane >> 3) & (CY - 1), lane & (CZ - 1)


def remainder(cap, chips, slot_ref, base_ref, pieces):
    total = sum(piece.shape[0] for piece in pieces)
    number = iota((LANES, total), 1)
    if chips is not None:
        n_y = lax.axis_size("gy")
        gy, gz = lax.axis_index("gy"), lax.axis_index("gz")
        order = [2 * lax.rem(gy + n_y - d, n_y) + gz for d in chips]
        lane = iota((1, LANES), 1)
        number = jnp.concatenate([(holder * cap) ^ lane for holder in order], axis=1)
    hit = (slot_ref[...] == number).astype(jnp.bfloat16)
    rows = jnp.concatenate([piece[...] for piece in pieces], axis=0)
    samples = jnp.dot(hit, rows, preferred_element_type=jnp.float32)
    return base_ref[...].astype(jnp.float32) - samples


def early_kernel(cap, chips, slot_ref, image_ref, *rest):
    rest[-1][...] = remainder(cap, chips, slot_ref, image_ref, rest[:-1])


def force_kernel(cap, chips, across_ref, slot_ref, base_ref, slope_ref, shape_ref, *rest):
    arrived, out_ref = rest[:-1], rest[-1]
    difference = remainder(cap, chips, slot_ref, base_ref, arrived)
    parts = []
    for d in range(3):
        weighted = slope_ref[d].astype(jnp.float32) * difference
        coarse = weighted.astype(jnp.bfloat16)
        parts += [coarse, (weighted - coarse.astype(jnp.float32)).astype(jnp.bfloat16)]
    sums = jnp.dot(
        jnp.concatenate(parts, axis=0), shape_ref[...], preferred_element_type=jnp.float32
    )
    columns = 0.0
    for d in range(3):
        both = sums[2 * LANES * d : 2 * LANES * d + LANES] + sums[2 * LANES * d + LANES : 2 * LANES * (d + 1)]
        columns = columns + (pltpu.roll(both, 16 * d, 1) if d else both)
    columns = columns.T
    _, _, at_k = axis_of_lane(8)
    for d in range(3):
        corners = columns[16 * d : 16 * d + 8] + columns[16 * d + 8 : 16 * d + 16]
        carried = pltpu.roll(corners, 4, 0)
        kept, sent = 8 * d, SENT + 8 * d
        out_ref[kept : kept + 8, :] = corners + jnp.where(at_k > 0, pltpu.roll(carried, 1, 1), 0.0)
        out_ref[sent : sent + 8, :] = jnp.where(at_k == 0, pltpu.roll(carried, LANES - 7, 1), 0.0)
        out_ref[sent + 4 : sent + 6, :] = across_ref[2 * d : 2 * d + 2, :]


def layers(d, z):
    at_i, at_j, _ = axis_of_lane(8)

    def along_x(lower_half, upper_half):
        moved = pltpu.roll(upper_half, CY * CZ, 1)
        return lower_half + jnp.where(at_i > 0, moved, 0.0), jnp.where(at_i == 0, moved, 0.0)

    carried = pltpu.roll(z, 7, 0)
    stay = z + jnp.where(at_j > 0, pltpu.roll(carried, CZ, 1), 0.0)
    leave = jnp.where(at_j == 0, pltpu.roll(carried, LANES - CZ * (CY - 1), 1), 0.0)
    own, x = along_x(stay, pltpu.roll(stay, 6, 0))
    y, xy = along_x(leave, pltpu.roll(leave, 6, 0))
    return [value[0:1] * data_weight for value in (own, x, y, xy)]


def layer_kernel(kept_ref, arrived_ref, stiff_ref, xy_ref, y_ref, x_ref, own_ref):
    behind = lax.axis_index("gz") > 0
    for d in range(3):
        part, sent = slice(8 * d, 8 * d + 8), slice(SENT + 8 * d, SENT + 8 * d + 8)
        z = kept_ref[part, :] + jnp.where(behind, arrived_ref[sent, :], 0.0)
        own, x, y, xy = layers(d, z)
        stiff = stiff_ref[2 * d : 2 * d + 2, :]
        row = slice(d, d + 1)
        xy_ref[row, :] = xy
        y_ref[row, :] = y
        x_ref[row, :] = x + stiff[1:2]
        own_ref[row, :] = own + stiff[0:1]


def chip_kernel(here_ref, mate_ref, stiff_ref, turn_ref, x_ref, own_ref):
    first = lax.axis_index("gz") == 0
    turn_ref[...] = jnp.zeros((8, LANES), jnp.float32)
    for d in range(3):
        part, sent = slice(8 * d, 8 * d + 8), slice(SENT + 8 * d, SENT + 8 * d + 8)
        z = here_ref[part, :] + jnp.where(first, 0.0, mate_ref[sent, :])
        own, x, y, xy = layers(d, z)
        row = slice(d, d + 1)
        turn_ref[row, :] = jnp.where(first, y, xy)
        stiff = stiff_ref[2 * d : 2 * d + 2, :] + mate_ref[SENT + 8 * d + 4 : SENT + 8 * d + 6, :]
        x_ref[row, :] = x + stiff[1:2]
        own_ref[row, :] = own + stiff[0:1]
        z = mate_ref[part, :] + jnp.where(first, here_ref[sent, :], 0.0)
        _, _, y, xy = layers(d, z)
        turn_ref[d + 3 : d + 4, :] = jnp.where(first, y, xy)


def chip_total_kernel(own_ref, turned_ref, mate_ref, x_ref, out_ref):
    has_x, has_y = lax.axis_index("gx") > 0, lax.axis_index("gy") > 0
    first = lax.axis_index("gz") == 0
    total = own_ref[0:3, :] + jnp.where(has_x, x_ref[0:3, :], 0.0)
    has = has_y & (first | has_x)
    total = total + jnp.where(has, turned_ref[0:3, :], 0.0)
    has = has_y & (jnp.logical_not(first) | has_x)
    out_ref[...] = total + jnp.where(has, mate_ref[3:6, :], 0.0)


def final_kernel(own_ref, y_ref, xy_ref, x_ref, out_ref):
    has_x = lax.axis_index("gx") > 0
    has_y = lax.axis_index("gy") > 0
    total = own_ref[0:3, :] + jnp.where(has_x, x_ref[0:3, :], 0.0)
    total = total + jnp.where(has_y, y_ref[0:3, :], 0.0)
    out_ref[...] = total + jnp.where(has_x & has_y, xy_ref[0:3, :], 0.0)


def navier(fields):
    at = axis_of_lane(8)
    steps = (CY * CZ, CZ, 1)
    extents = (CX, CY, CZ)

    def plus(p, q):
        return q if p is None else p if q is None else p + q

    def times(factor, p):
        return None if p is None else factor * p

    def along(axis, sign, centre, beyond):
        step, extent = steps[axis], extents[axis]
        back = step * (extent - 1)
        if sign > 0:
            inside, near, far = at[axis] < extent - 1, LANES - step, back
        else:
            inside, near, far = at[axis] > 0, step, LANES - back
        if centre is None and beyond is None:
            return None
        return jnp.where(
            inside,
            0.0 if centre is None else pltpu.roll(centre, near, 1),
            0.0 if beyond is None else pltpu.roll(beyond, far, 1),
        )

    def moved(vector, frame=(0, 0, 0), axis=2):
        if axis < 0:
            return fields.get(frame)
        sign = vector[axis]
        centre = moved(vector, frame, axis - 1)
        if sign == 0:
            return centre
        other = tuple(sign if n == axis else frame[n] for n in range(3))
        return along(axis, sign, centre, moved(vector, other, axis - 1))

    units = ((1, 0, 0), (0, 1, 0), (0, 0, 1))
    centre = fields.get((0, 0, 0))
    laplace = times(-6.0, centre)
    second = []
    for unit in units:
        both = plus(moved(unit), moved(tuple(-n for n in unit)))
        laplace = plus(laplace, both)
        second.append(plus(both, times(-2.0, centre)))
    mixed = {}
    for outer in range(3):
        for inner in range(outer + 1, 3):
            ahead = tuple(p + q for p, q in zip(units[outer], units[inner]))
            cross = tuple(p - q for p, q in zip(units[outer], units[inner]))
            aligned = plus(moved(ahead), moved(tuple(-n for n in ahead)))
            crossed = plus(moved(cross), moved(tuple(-n for n in cross)))
            mixed[outer, inner] = times(0.25, plus(aligned, times(-1.0, crossed)))
    rows = []
    for d in range(3):
        parts = [second[d]]
        for b in range(3):
            if b != d:
                part = mixed[min(b, d), max(b, d)]
                parts.append(None if part is None else pltpu.roll(part, (d - b) % 8, 0))
        total = functools.reduce(plus, parts)
        value = plus(times(shear_modulus, laplace), times(lame_first + shear_modulus, total))
        rows.append(jnp.zeros((1, LANES), jnp.float32) if value is None else -value[d : d + 1])
    return rows


def stiffness_kernel(below_ref, own_ref, above_ref, out_ref):
    here = [lax.axis_index(name) for name in ("gx", "gy", "gz")]
    sizes = [lax.axis_size(name) for name in ("gx", "gy", "gz")]
    slabs = {-1: below_ref, 0: own_ref, 1: above_ref}
    fields = {}
    for ox in (-1, 0, 1):
        for oy in (-1, 0, 1):
            for oz in (-1, 0, 1):
                if ox and oy and oz:
                    continue
                place = (here[0] + ox, here[1] + oy, here[2] + oz)
                inside = True
                for where, size in zip(place, sizes):
                    inside = inside & (where >= 0) & (where < size)
                peer = jnp.clip(place[1], 0, sizes[1] - 1) * sizes[2] + jnp.clip(
                    place[2], 0, sizes[2] - 1
                )
                fields[ox, oy, oz] = jnp.where(inside, slabs[ox][peer], 0.0)
    out_ref[...] = jnp.zeros((8, LANES), jnp.float32)
    for d, row in enumerate(navier(fields)):
        out_ref[2 * d : 2 * d + 1, :] = row


def column_kernel(own_ref, above_ref, kept_ref, across_ref):
    gx, gy, gz = [lax.axis_index(name) for name in ("gx", "gy", "gz")]
    n_x, n_y = lax.axis_size("gx"), lax.axis_size("gy")
    here, ahead = {}, {}
    for oy in (-1, 0, 1):
        place = gy + oy
        inside = (place >= 0) & (place < n_y)
        distance = lax.rem(oy + n_y, n_y)
        here[0, oy] = jnp.where(inside, own_ref[distance], 0.0)
        here[1, oy] = jnp.where(inside & (gx + 1 < n_x), above_ref[distance], 0.0)
        ahead[-1, oy] = here[0, oy]
    for n, columns in enumerate((here, ahead)):
        kept = {(ox, oy, 0): value for (ox, oy), value in columns.items()}
        across = {}
        for (ox, oy), value in columns.items():
            if not (ox and oy):
                across[ox, oy, -1] = jnp.where(gz == 0, value, 0.0)
                across[ox, oy, 1] = jnp.where(gz == 1, value, 0.0)
        for ref, fields in ((kept_ref, kept), (across_ref, across)):
            for d, row in enumerate(navier(fields)):
                ref[2 * d + n : 2 * d + n + 1, :] = row


def collect_kernel(after_ref, *refs):
    for n, ref in enumerate(refs[:-1]):
        refs[-1][n] = ref[DISP:META, :]


def small_call(kernel, shapes, name, *operands):
    return vmem_call(kernel, [(shape, jnp.float32) for shape in shapes], name, *operands)


def ring(value, axes, distance=1):
    count = lax.axis_size(axes)
    return lax.ppermute(value, axes, [(i, (i + distance) % count) for i in range(count)])


def ring_2(value):
    nx, ny = lax.axis_size("gx"), lax.axis_size("gy")
    route = [
        (x * ny + y, (x + 1) % nx * ny + (y + 1) % ny) for x in range(nx) for y in range(ny)
    ]
    return lax.ppermute(value, ("gx", "gy"), route)


def turned_ring(value):
    nx, ny = lax.axis_size("gx"), lax.axis_size("gy")
    place = {
        (x * ny + y) * 2 + core: (x, y, core)
        for x in range(nx)
        for y in range(ny)
        for core in range(2)
    }
    number = {where: i for i, where in place.items()}
    route = [(i, number.get((x + core, y + 1, core))) for i, (x, y, core) in place.items()]
    route = [pair for pair in route if pair[1] is not None]

    def from_order(i):
        x, y, core = place[i]
        return y, -core, x > 0, -x

    def to_order(i):
        x, y, core = place[i]
        return x > 0, y, -core if x else core, -x

    sources = sorted(set(place) - {pair[0] for pair in route}, key=from_order)
    targets = sorted(set(place) - {pair[1] for pair in route}, key=to_order)
    return lax.ppermute(value, ("gx", "gy", "gz"), route + list(zip(sources, targets)))


def swapped(value, axes, mask):
    return lax.ppermute(value, axes, [(i, i ^ mask) for i in range(lax.axis_size(axes))])


def local(
    displacement,
    reference_image,
    image_gradient,
    deformed_blocks,
    fractions,
    offsets,
    send_list,
    recv_slot,
):
    n_y, n_z = lax.axis_size("gy"), lax.axis_size("gz")
    peers = n_y * n_z
    cap = send_list.shape[0] // peers
    (shape_values,) = vmem_call(
        shape_kernel, [((512, LANES), jnp.bfloat16)], "shapes", cost=16 << 20, flops=1 << 33
    )
    (packed,) = small_call(
        pack_kernel,
        [(META, LANES)],
        "pack",
        shape_values,
        fractions,
        displacement,
        offsets,
        recv_slot[None],
    )
    send_rows = send_list.reshape(-1, LANES)
    mate_rows = swapped(send_rows, "gz", 1)

    def table_of(*blocks):
        shape = (VOXELS, len(blocks) * LANES)
        return vmem_call(
            table_kernel, [(shape, jnp.bfloat16)], "table", packed, mate_rows, *blocks, flops=3 << 28
        )[0]

    relative = n_z == 2 and n_y in (2, 4) and 2 * cap == LANES
    if relative:
        metas = [packed] + [ring(packed, "gy", -d) for d in range(1, n_y)]
        table = table_of(deformed_blocks, swapped(deformed_blocks, "gz", 1))
        arrived = [None] * n_y
        previous = []
        order = [3, 2, 1] if n_y == 4 else [1]
        for d in order + [0]:
            samples = sample_call(
                functools.partial(pair_kernel, d),
                metas[d],
                table,
                send_rows,
                mate_rows,
                *previous,
            )
            arrived[d] = ring(samples, "gy", d) if d else samples
            previous = [samples]
        (column,) = small_call(collect_kernel, [(n_y, 8, LANES)], "collect", arrived[n_y - 1], *metas)
        stiff, across = small_call(
            column_kernel, [(8, LANES)] * 2, "stiffness", column, ring(column, "gx", -1)
        )
    else:
        gathered = lax.all_gather(packed, SLAB, axis=0)
        readers = LANES // cap
        table = table_of(deformed_blocks)
        samples = [
            sample_call(
                functools.partial(group_kernel, g, cap),
                gathered[g * readers : (g + 1) * readers],
                table,
                send_rows,
            )
            for g in range(peers // readers)
        ]
        outgoing = jnp.concatenate(samples, axis=0)
        arrived = [lax.all_to_all(outgoing, SLAB, split_axis=0, concat_axis=0, tiled=True)]
        slab = gathered[:, DISP:META]
        (stiff,) = small_call(
            stiffness_kernel, [(8, LANES)], "stiffness", ring(slab, "gx", 1), slab, ring(slab, "gx", -1)
        )
        across = jnp.zeros((8, LANES), jnp.float32)
    base, chips = reference_image, None
    if relative:
        chips = (0, order[0])[: n_y - 1]
        (base,) = small_call(
            functools.partial(early_kernel, cap, chips),
            [(LANES, 512)],
            "early",
            recv_slot[:, None],
            base,
            *[arrived[d] for d in chips],
        )
        chips = tuple(order[1:]) or (order[0],)
        arrived = [arrived[d] for d in chips]
    (force,) = small_call(
        functools.partial(force_kernel, cap, chips),
        [(2 * SENT, LANES)],
        "forces",
        across,
        recv_slot[:, None],
        base,
        image_gradient,
        shape_values,
        *arrived,
    )
    came = ring(force, "gz")
    if relative:
        turn, x, own = small_call(chip_kernel, [(8, LANES)] * 3, "layers", force, came, stiff)
        turned = turned_ring(turn)
        return small_call(
            chip_total_kernel, [(3, LANES)], "total", own, turned, ring(turned, "gz"), ring(x, "gx")
        )[0]
    xy, y, x, own = small_call(layer_kernel, [(8, LANES)] * 4, "layers", force, came, stiff)
    return small_call(
        final_kernel, [(3, LANES)], "total", own, ring(y, "gy"), ring_2(xy), ring(x, "gx")
    )[0]


def solution(mesh):
    in_specs = (
        P(None, ("gx", "gy", "gz")),
        P(("gx", "gy", "gz"), None),
        P(None, ("gx", "gy", "gz"), None),
        P(("gx", "gy", "gz"), None),
        P(None, ("gx", "gy", "gz")),
        P(None, ("gx", "gy", "gz")),
        P(("gx", "gy", "gz")),
        P(("gx", "gy", "gz")),
    )
    out_specs = P(None, ("gx", "gy", "gz"))
    return jax.shard_map(local, mesh=mesh, in_specs=in_specs, out_specs=out_specs, check_vma=False)
```

```python
import functools

import jax
import jax.numpy as jnp
from jax import lax
from jax.experimental import pallas as pl
from jax.experimental.pallas import tpu as pltpu
from jax.sharding import PartitionSpec as P

CX = 2
CY = 8
CZ = 8
LANES = CX * CY * CZ
SLAB = ("gy", "gz")

shear_modulus = 0.05
lame_first = 1.0
data_weight = 0.0625

DISP = 24
OFFS = 27
SLOT = 30
META = 32

VOXELS = 4096
SENT = 24


def iota(shape, dim):
    return lax.broadcasted_iota(jnp.int32, shape, dim)


def shifted(planes, bits):
    for bit, count in ((2, 12), (1, 10), (0, 9)):
        step = 1 << bit
        planes = [jnp.where(bits[bit], planes[p + step], planes[p]) for p in range(count)]
    return planes


def offset_bits(offset, rows):
    wide = jnp.broadcast_to(offset, (rows, LANES))
    return [(wide & (1 << bit)) != 0 for bit in range(3)]


def shape_kernel(out_ref):
    voxel, column = iota((512, LANES), 0), iota((512, LANES), 1)

    def weight(index, upper):
        centre = (index.astype(jnp.float32) + 0.5) * 0.125
        return jnp.where(upper == 1, centre, 1.0 - centre)

    values = weight(voxel >> 6, (column >> 1) & 1) * weight((voxel >> 3) & 7, column & 1)
    values = values * weight(voxel & 7, (column >> 2) & 1)
    coarse = values.astype(jnp.bfloat16).astype(jnp.float32)
    values = jnp.where(column < 8, coarse, jnp.where(column < 16, values - coarse, 0.0))
    out_ref[...] = values.astype(jnp.bfloat16)


def pack_kernel(after_ref, fraction_ref, displacement_ref, offset_ref, slot_ref, out_ref):
    out_ref[:DISP, :] = fraction_ref[...].astype(jnp.float32)
    out_ref[DISP:OFFS, :] = displacement_ref[...]
    out_ref[OFFS:SLOT, :] = offset_ref[...].astype(jnp.float32)
    out_ref[SLOT : SLOT + 1, :] = slot_ref[...].astype(jnp.float32)
    out_ref[SLOT + 1 :, :] = jnp.zeros((META - SLOT - 1, LANES), jnp.float32)


def table_kernel(after_ref, later_ref, *refs):
    out_ref = refs[-1]
    for n, ref in enumerate(refs[:-1]):
        for start in range(0, VOXELS, 512):
            out_ref[start : start + 512, LANES * n : LANES * n + LANES] = ref[
                :, start : start + 512
            ].T


def vmem_call(kernel, shapes, name, *operands, cost=1 << 20, flops=1 << 20):
    vmem = pl.BlockSpec(memory_space=pltpu.VMEM)
    return pl.pallas_call(
        kernel,
        out_shape=[jax.ShapeDtypeStruct(shape, dtype) for shape, dtype in shapes],
        in_specs=[vmem] * len(operands),
        out_specs=[vmem] * len(shapes),
        compiler_params=pltpu.CompilerParams(vmem_limit_bytes=24 << 20),
        cost_estimate=pl.CostEstimate(flops=flops, bytes_accessed=cost, transcendentals=0),
        name=name,
    )(*operands)


def interpolated(table_ref, pick, meta, along_a, along_b, along_c):
    upper = meta[:24]
    lower = 1.0 - upper
    offsets = meta[OFFS : OFFS + 3].astype(jnp.int32)
    bits = offset_bits(offsets[0:1], 16)
    for first in range(0, 256, 16):
        starts = [256 * a + first for a in range(16)]
        rows = jnp.concatenate([table_ref[start : start + 16, :] for start in starts], axis=0)
        voxels = jnp.dot(rows, pick, preferred_element_type=jnp.float32)
        window = shifted([voxels[16 * a : 16 * a + 16] for a in range(16)], bits)
        for i in range(8):
            along_a[256 * i + first : 256 * i + first + 16, :] = (
                lower[i : i + 1] * window[i] + upper[i : i + 1] * window[i + 1]
            )
    bits = offset_bits(offsets[1:2], 16)
    for i in range(8):
        window = shifted(
            [along_a[256 * i + 16 * b : 256 * i + 16 * b + 16, :] for b in range(16)], bits
        )
        for j in range(8):
            along_b[128 * i + 16 * j : 128 * i + 16 * j + 16, :] = (
                lower[8 + j : 9 + j] * window[j] + upper[8 + j : 9 + j] * window[j + 1]
            )
    bits = offset_bits(offsets[2:3], 8)
    for i in range(8):
        window = shifted(
            [along_b[pl.ds(128 * i + c, 8, stride=16), :] for c in range(16)], bits
        )
        for k in range(8):
            along_c[pl.ds(64 * i + k, 8, stride=8), :] = (
                lower[16 + k : 17 + k] * window[k] + upper[16 + k : 17 + k] * window[k + 1]
            )
    return along_c[...].T.astype(jnp.bfloat16)


def slot_meta(meta, slots):
    wanted = meta[SLOT : SLOT + 1].astype(jnp.int32)
    return lax.dot_general(
        meta.astype(jnp.bfloat16),
        (wanted == slots).astype(jnp.bfloat16),
        (((1,), (1,)), ((), ())),
        preferred_element_type=jnp.float32,
    )


def pair_kernel(distance, meta_ref, table_ref, own_ref, mate_ref, *rest):
    out_ref, scratch = rest[-4], rest[-3:]
    gy, gz = lax.axis_index("gy"), lax.axis_index("gz")
    half = LANES // 2
    slot = iota((LANES, LANES), 0)
    slots = ((2 * gy + gz) * half) ^ slot
    meta = slot_meta(meta_ref[...], slots)
    chip = lax.rem(gy + distance, lax.axis_size("gy"))
    chip = pl.ds(chip, 1)
    own, mate = own_ref[chip, :], mate_ref[chip, :]
    first = gz == 0
    own = jnp.where(first, own, pltpu.roll(own, half, 1))
    mate = jnp.where(first, pltpu.roll(mate, half, 1), mate)
    row = jnp.where(iota((1, LANES), 1) < half, own, mate + LANES)
    pick = (iota((2 * LANES, LANES), 0) == row).astype(jnp.bfloat16)
    out_ref[...] = interpolated(table_ref, pick, meta, *scratch)


def group_kernel(group, cap, meta_ref, table_ref, send_ref, out_ref, *scratch):
    holder = lax.axis_index("gy") * lax.axis_size("gz") + lax.axis_index("gz")
    slot = iota((LANES, LANES), 0)
    meta = jnp.zeros((META, LANES), jnp.float32)
    for r in range(LANES // cap):
        slots = jnp.where(slot // cap == r, holder * cap + slot - r * cap, -1)
        meta = meta + slot_meta(meta_ref[r], slots)
    pick = (iota((LANES, LANES), 0) == send_ref[group : group + 1, :]).astype(jnp.bfloat16)
    out_ref[...] = interpolated(table_ref, pick, meta, *scratch)


def sample_call(kernel, *operands):
    vmem = pl.BlockSpec(memory_space=pltpu.VMEM)
    return pl.pallas_call(
        kernel,
        out_shape=jax.ShapeDtypeStruct((LANES, 512), jnp.bfloat16),
        in_specs=[vmem] * len(operands),
        out_specs=vmem,
        scratch_shapes=[
            pltpu.VMEM((2048, LANES), jnp.float32),
            pltpu.VMEM((1024, LANES), jnp.float32),
            pltpu.VMEM((512, LANES), jnp.float32),
        ],
        compiler_params=pltpu.CompilerParams(vmem_limit_bytes=24 << 20),
        cost_estimate=pl.CostEstimate(
            flops=4000000000, bytes_accessed=1, transcendentals=0
        ),
        name="interpolate",
    )(*operands)


def axis_of_lane(rows):
    lane = iota((rows, LANES), 1)
    return lane >> 6, (lane >> 3) & (CY - 1), lane & (CZ - 1)


def remainder(cap, chips, slot_ref, base_ref, pieces):
    total = sum(piece.shape[0] for piece in pieces)
    number = iota((LANES, total), 1)
    if chips is not None:
        n_y = lax.axis_size("gy")
        gy, gz = lax.axis_index("gy"), lax.axis_index("gz")
        order = [2 * lax.rem(gy + n_y - d, n_y) + gz for d in chips]
        lane = iota((1, LANES), 1)
        number = jnp.concatenate([(holder * cap) ^ lane for holder in order], axis=1)
    hit = (slot_ref[...] == number).astype(jnp.bfloat16)
    rows = jnp.concatenate([piece[...] for piece in pieces], axis=0)
    samples = jnp.dot(hit, rows, preferred_element_type=jnp.float32)
    return base_ref[...].astype(jnp.float32) - samples


def early_kernel(cap, chips, slot_ref, image_ref, *rest):
    rest[-1][...] = remainder(cap, chips, slot_ref, image_ref, rest[:-1])


def force_kernel(cap, chips, across_ref, slot_ref, base_ref, slope_ref, shape_ref, *rest):
    arrived, out_ref = rest[:-1], rest[-1]
    difference = remainder(cap, chips, slot_ref, base_ref, arrived)
    parts = []
    for d in range(3):
        weighted = slope_ref[d].astype(jnp.float32) * difference
        coarse = weighted.astype(jnp.bfloat16)
        parts += [coarse, (weighted - coarse.astype(jnp.float32)).astype(jnp.bfloat16)]
    sums = jnp.dot(
        jnp.concatenate(parts, axis=0), shape_ref[...], preferred_element_type=jnp.float32
    )
    columns = 0.0
    for d in range(3):
        both = sums[2 * LANES * d : 2 * LANES * d + LANES] + sums[2 * LANES * d + LANES : 2 * LANES * (d + 1)]
        columns = columns + (pltpu.roll(both, 16 * d, 1) if d else both)
    columns = columns.T
    _, _, at_k = axis_of_lane(8)
    for d in range(3):
        corners = columns[16 * d : 16 * d + 8] + columns[16 * d + 8 : 16 * d + 16]
        carried = pltpu.roll(corners, 4, 0)
        kept, sent = 8 * d, SENT + 8 * d
        out_ref[kept : kept + 8, :] = corners + jnp.where(at_k > 0, pltpu.roll(carried, 1, 1), 0.0)
        out_ref[sent : sent + 8, :] = jnp.where(at_k == 0, pltpu.roll(carried, LANES - 7, 1), 0.0)
        out_ref[sent + 4 : sent + 6, :] = across_ref[2 * d : 2 * d + 2, :]


def layers(d, z):
    at_i, at_j, _ = axis_of_lane(8)

    def along_x(lower_half, upper_half):
        moved = pltpu.roll(upper_half, CY * CZ, 1)
        return lower_half + jnp.where(at_i > 0, moved, 0.0), jnp.where(at_i == 0, moved, 0.0)

    carried = pltpu.roll(z, 7, 0)
    stay = z + jnp.where(at_j > 0, pltpu.roll(carried, CZ, 1), 0.0)
    leave = jnp.where(at_j == 0, pltpu.roll(carried, LANES - CZ * (CY - 1), 1), 0.0)
    own, x = along_x(stay, pltpu.roll(stay, 6, 0))
    y, xy = along_x(leave, pltpu.roll(leave, 6, 0))
    return [value[0:1] * data_weight for value in (own, x, y, xy)]


def layer_kernel(kept_ref, arrived_ref, stiff_ref, xy_ref, y_ref, x_ref, own_ref):
    behind = lax.axis_index("gz") > 0
    for d in range(3):
        part, sent = slice(8 * d, 8 * d + 8), slice(SENT + 8 * d, SENT + 8 * d + 8)
        z = kept_ref[part, :] + jnp.where(behind, arrived_ref[sent, :], 0.0)
        own, x, y, xy = layers(d, z)
        stiff = stiff_ref[2 * d : 2 * d + 2, :]
        row = slice(d, d + 1)
        xy_ref[row, :] = xy
        y_ref[row, :] = y
        x_ref[row, :] = x + stiff[1:2]
        own_ref[row, :] = own + stiff[0:1]


def chip_kernel(here_ref, mate_ref, stiff_ref, turn_ref, x_ref, own_ref):
    first = lax.axis_index("gz") == 0
    turn_ref[...] = jnp.zeros((8, LANES), jnp.float32)
    for d in range(3):
        part, sent = slice(8 * d, 8 * d + 8), slice(SENT + 8 * d, SENT + 8 * d + 8)
        z = here_ref[part, :] + jnp.where(first, 0.0, mate_ref[sent, :])
        own, x, y, xy = layers(d, z)
        row = slice(d, d + 1)
        turn_ref[row, :] = jnp.where(first, y, xy)
        stiff = stiff_ref[2 * d : 2 * d + 2, :] + mate_ref[SENT + 8 * d + 4 : SENT + 8 * d + 6, :]
        x_ref[row, :] = x + stiff[1:2]
        own_ref[row, :] = own + stiff[0:1]
        z = mate_ref[part, :] + jnp.where(first, here_ref[sent, :], 0.0)
        _, _, y, xy = layers(d, z)
        turn_ref[d + 3 : d + 4, :] = jnp.where(first, y, xy)


def chip_total_kernel(own_ref, turned_ref, mate_ref, x_ref, out_ref):
    has_x, has_y = lax.axis_index("gx") > 0, lax.axis_index("gy") > 0
    first = lax.axis_index("gz") == 0
    total = own_ref[0:3, :] + jnp.where(has_x, x_ref[0:3, :], 0.0)
    has = has_y & (first | has_x)
    total = total + jnp.where(has, turned_ref[0:3, :], 0.0)
    has = has_y & (jnp.logical_not(first) | has_x)
    out_ref[...] = total + jnp.where(has, mate_ref[3:6, :], 0.0)


def final_kernel(own_ref, y_ref, xy_ref, x_ref, out_ref):
    has_x = lax.axis_index("gx") > 0
    has_y = lax.axis_index("gy") > 0
    total = own_ref[0:3, :] + jnp.where(has_x, x_ref[0:3, :], 0.0)
    total = total + jnp.where(has_y, y_ref[0:3, :], 0.0)
    out_ref[...] = total + jnp.where(has_x & has_y, xy_ref[0:3, :], 0.0)


def navier(fields):
    at = axis_of_lane(8)
    steps = (CY * CZ, CZ, 1)
    extents = (CX, CY, CZ)

    def plus(p, q):
        return q if p is None else p if q is None else p + q

    def times(factor, p):
        return None if p is None else factor * p

    def along(axis, sign, centre, beyond):
        step, extent = steps[axis], extents[axis]
        back = step * (extent - 1)
        if sign > 0:
            inside, near, far = at[axis] < extent - 1, LANES - step, back
        else:
            inside, near, far = at[axis] > 0, step, LANES - back
        if centre is None and beyond is None:
            return None
        return jnp.where(
            inside,
            0.0 if centre is None else pltpu.roll(centre, near, 1),
            0.0 if beyond is None else pltpu.roll(beyond, far, 1),
        )

    def moved(vector, frame=(0, 0, 0), axis=2):
        if axis < 0:
            return fields.get(frame)
        sign = vector[axis]
        centre = moved(vector, frame, axis - 1)
        if sign == 0:
            return centre
        other = tuple(sign if n == axis else frame[n] for n in range(3))
        return along(axis, sign, centre, moved(vector, other, axis - 1))

    units = ((1, 0, 0), (0, 1, 0), (0, 0, 1))
    centre = fields.get((0, 0, 0))
    laplace = times(-6.0, centre)
    second = []
    for unit in units:
        both = plus(moved(unit), moved(tuple(-n for n in unit)))
        laplace = plus(laplace, both)
        second.append(plus(both, times(-2.0, centre)))
    mixed = {}
    for outer in range(3):
        for inner in range(outer + 1, 3):
            ahead = tuple(p + q for p, q in zip(units[outer], units[inner]))
            cross = tuple(p - q for p, q in zip(units[outer], units[inner]))
            aligned = plus(moved(ahead), moved(tuple(-n for n in ahead)))
            crossed = plus(moved(cross), moved(tuple(-n for n in cross)))
            mixed[outer, inner] = times(0.25, plus(aligned, times(-1.0, crossed)))
    rows = []
    for d in range(3):
        parts = [second[d]]
        for b in range(3):
            if b != d:
                part = mixed[min(b, d), max(b, d)]
                parts.append(None if part is None else pltpu.roll(part, (d - b) % 8, 0))
        total = functools.reduce(plus, parts)
        value = plus(times(shear_modulus, laplace), times(lame_first + shear_modulus, total))
        rows.append(jnp.zeros((1, LANES), jnp.float32) if value is None else -value[d : d + 1])
    return rows


def stiffness_kernel(below_ref, own_ref, above_ref, out_ref):
    here = [lax.axis_index(name) for name in ("gx", "gy", "gz")]
    sizes = [lax.axis_size(name) for name in ("gx", "gy", "gz")]
    slabs = {-1: below_ref, 0: own_ref, 1: above_ref}
    fields = {}
    for ox in (-1, 0, 1):
        for oy in (-1, 0, 1):
            for oz in (-1, 0, 1):
                if ox and oy and oz:
                    continue
                place = (here[0] + ox, here[1] + oy, here[2] + oz)
                inside = True
                for where, size in zip(place, sizes):
                    inside = inside & (where >= 0) & (where < size)
                peer = jnp.clip(place[1], 0, sizes[1] - 1) * sizes[2] + jnp.clip(
                    place[2], 0, sizes[2] - 1
                )
                fields[ox, oy, oz] = jnp.where(inside, slabs[ox][peer], 0.0)
    out_ref[...] = jnp.zeros((8, LANES), jnp.float32)
    for d, row in enumerate(navier(fields)):
        out_ref[2 * d : 2 * d + 1, :] = row


def column_kernel(own_ref, above_ref, kept_ref, across_ref):
    gx, gy, gz = [lax.axis_index(name) for name in ("gx", "gy", "gz")]
    n_x, n_y = lax.axis_size("gx"), lax.axis_size("gy")
    here, ahead = {}, {}
    for oy in (-1, 0, 1):
        place = gy + oy
        inside = (place >= 0) & (place < n_y)
        distance = lax.rem(oy + n_y, n_y)
        here[0, oy] = jnp.where(inside, own_ref[distance], 0.0)
        here[1, oy] = jnp.where(inside & (gx + 1 < n_x), above_ref[distance], 0.0)
        ahead[-1, oy] = here[0, oy]
    for n, columns in enumerate((here, ahead)):
        kept = {(ox, oy, 0): value for (ox, oy), value in columns.items()}
        across = {}
        for (ox, oy), value in columns.items():
            if not (ox and oy):
                across[ox, oy, -1] = jnp.where(gz == 0, value, 0.0)
                across[ox, oy, 1] = jnp.where(gz == 1, value, 0.0)
        for ref, fields in ((kept_ref, kept), (across_ref, across)):
            for d, row in enumerate(navier(fields)):
                ref[2 * d + n : 2 * d + n + 1, :] = row


def collect_kernel(after_ref, *refs):
    for n, ref in enumerate(refs[:-1]):
        refs[-1][n] = ref[DISP:META, :]


def small_call(kernel, shapes, name, *operands):
    return vmem_call(kernel, [(shape, jnp.float32) for shape in shapes], name, *operands)


def ring(value, axes, distance=1):
    count = lax.axis_size(axes)
    return lax.ppermute(value, axes, [(i, (i + distance) % count) for i in range(count)])


def ring_2(value):
    nx, ny = lax.axis_size("gx"), lax.axis_size("gy")
    route = [
        (x * ny + y, (x + 1) % nx * ny + (y + 1) % ny) for x in range(nx) for y in range(ny)
    ]
    return lax.ppermute(value, ("gx", "gy"), route)


def turned_ring(value):
    nx, ny = lax.axis_size("gx"), lax.axis_size("gy")
    place = {
        (x * ny + y) * 2 + core: (x, y, core)
        for x in range(nx)
        for y in range(ny)
        for core in range(2)
    }
    number = {where: i for i, where in place.items()}
    route = [(i, number.get((x + core, y + 1, core))) for i, (x, y, core) in place.items()]
    route = [pair for pair in route if pair[1] is not None]

    def from_order(i):
        x, y, core = place[i]
        return y, -core, x > 0, -x

    def to_order(i):
        x, y, core = place[i]
        return x > 0, y, -core if x else core, -x

    sources = sorted(set(place) - {pair[0] for pair in route}, key=from_order)
    targets = sorted(set(place) - {pair[1] for pair in route}, key=to_order)
    return lax.ppermute(value, ("gx", "gy", "gz"), route + list(zip(sources, targets)))


def swapped(value, axes, mask):
    return lax.ppermute(value, axes, [(i, i ^ mask) for i in range(lax.axis_size(axes))])


def local(
    displacement,
    reference_image,
    image_gradient,
    deformed_blocks,
    fractions,
    offsets,
    send_list,
    recv_slot,
):
    n_y, n_z = lax.axis_size("gy"), lax.axis_size("gz")
    peers = n_y * n_z
    cap = send_list.shape[0] // peers
    (shape_values,) = vmem_call(
        shape_kernel, [((512, LANES), jnp.bfloat16)], "shapes", cost=16 << 20, flops=1 << 33
    )
    (packed,) = small_call(
        pack_kernel,
        [(META, LANES)],
        "pack",
        shape_values,
        fractions,
        displacement,
        offsets,
        recv_slot[None],
    )
    send_rows = send_list.reshape(-1, LANES)
    mate_rows = swapped(send_rows, "gz", 1)

    def table_of(*blocks):
        shape = (VOXELS, len(blocks) * LANES)
        return vmem_call(
            table_kernel, [(shape, jnp.bfloat16)], "table", packed, mate_rows, *blocks, flops=3 << 28
        )[0]

    relative = n_z == 2 and n_y in (2, 4) and 2 * cap == LANES
    if relative:
        metas = [packed] + [ring(packed, "gy", -d) for d in range(1, n_y)]
        table = table_of(deformed_blocks, swapped(deformed_blocks, "gz", 1))
        arrived = [None] * n_y
        previous = []
        order = [3, 2, 1] if n_y == 4 else [1]
        for d in order + [0]:
            samples = sample_call(
                functools.partial(pair_kernel, d),
                metas[d],
                table,
                send_rows,
                mate_rows,
                *previous,
            )
            arrived[d] = ring(samples, "gy", d) if d else samples
            previous = [samples]
        (column,) = small_call(collect_kernel, [(n_y, 8, LANES)], "collect", previous[0], *metas)
        stiff, across = small_call(
            column_kernel, [(8, LANES)] * 2, "stiffness", column, ring(column, "gx", -1)
        )
    else:
        gathered = lax.all_gather(packed, SLAB, axis=0)
        readers = LANES // cap
        table = table_of(deformed_blocks)
        samples = [
            sample_call(
                functools.partial(group_kernel, g, cap),
                gathered[g * readers : (g + 1) * readers],
                table,
                send_rows,
            )
            for g in range(peers // readers)
        ]
        outgoing = jnp.concatenate(samples, axis=0)
        arrived = [lax.all_to_all(outgoing, SLAB, split_axis=0, concat_axis=0, tiled=True)]
        slab = gathered[:, DISP:META]
        (stiff,) = small_call(
            stiffness_kernel, [(8, LANES)], "stiffness", ring(slab, "gx", 1), slab, ring(slab, "gx", -1)
        )
        across = jnp.zeros((8, LANES), jnp.float32)
    base, chips = reference_image, None
    if relative:
        chips = (0, order[0])[: n_y - 1]
        (base,) = small_call(
            functools.partial(early_kernel, cap, chips),
            [(LANES, 512)],
            "early",
            recv_slot[:, None],
            base,
            *[arrived[d] for d in chips],
        )
        chips = tuple(order[1:]) or (order[0],)
        arrived = [arrived[d] for d in chips]
    (force,) = small_call(
        functools.partial(force_kernel, cap, chips),
        [(2 * SENT, LANES)],
        "forces",
        across,
        recv_slot[:, None],
        base,
        image_gradient,
        shape_values,
        *arrived,
    )
    came = ring(force, "gz")
    if relative:
        turn, x, own = small_call(chip_kernel, [(8, LANES)] * 3, "layers", force, came, stiff)
        turned = turned_ring(turn)
        return small_call(
            chip_total_kernel, [(3, LANES)], "total", own, turned, ring(turned, "gz"), ring(x, "gx")
        )[0]
    xy, y, x, own = small_call(layer_kernel, [(8, LANES)] * 4, "layers", force, came, stiff)
    return small_call(
        final_kernel, [(3, LANES)], "total", own, ring(y, "gy"), ring_2(xy), ring(x, "gx")
    )[0]


def solution(mesh):
    in_specs = (
        P(None, ("gx", "gy", "gz")),
        P(("gx", "gy", "gz"), None),
        P(None, ("gx", "gy", "gz"), None),
        P(("gx", "gy", "gz"), None),
        P(None, ("gx", "gy", "gz")),
        P(None, ("gx", "gy", "gz")),
        P(("gx", "gy", "gz")),
        P(("gx", "gy", "gz")),
    )
    out_specs = P(None, ("gx", "gy", "gz"))
    return jax.shard_map(local, mesh=mesh, in_specs=in_specs, out_specs=out_specs, check_vma=False)
```
